32 devices in a mesh: wide: 16 (over z, y, x), freq: 2 (over core).
Axes of the slice: x: 2, y: 2, z: 4, core: 2. Of those that a mesh axis runs over, the one named last changes fastest.
Arguments:
- wave: bfloat16 [2, 2, 1024, 1024], P(None, 'freq', 'wide'), may hold values from -6 to 6
- filters: bfloat16 [2, 2, 2, 3, 81], P(None, None, 'freq'), may hold values from -0.6640625 to 0.6640625
- vel_bins: int32 [2, 2, 3, 1024], replicated, may hold values from 0 to 2
- blend_levels: int32 [2, 2, 3, 1024], replicated, may hold values from 1 to 16
- aperture: int32 [2, 64, 64], replicated, may hold values 0 or 1
Outputs:
- image_shallow: float32 [1024, 1024], P('wide', 'freq')
- image_deep: float32 [1024, 1024], P('wide', 'freq')
The draws below stay inside these ranges and needn't reach their ends.
All inputs are finite; a program needn't handle non-finite values.
Results may differ from the reference program's by a relative error of at most 0.017.
Values may be sent and summed in bfloat16 or wider, within the bound.
No kernel may reach another device: no remote copies, remote signals or barrier semaphores. Data moves between devices by JAX's collectives and lax.ppermute only.
A program may use at most 64 MiB of HBM per device.

```python
import jax
import jax.numpy as jnp
from jax import lax

SIDE = 32
TAPS = 9
VBINS = 3
BLEND = 3
NSTEP = 2
BLK = 16
FREQS = 2
POS = 1024
NBLK = 64


def set_ends(entries, stream_key, smallest, largest):
    index_at = [jax.random.randint(jax.random.fold_in(stream_key, axis), (), 0, length) for axis, length in enumerate(entries.shape)]
    widest = entries.shape.index(max(entries.shape))
    beside = index_at[:widest] + [(index_at[widest] + 1) % entries.shape[widest]] + index_at[widest + 1:]
    return entries.at[tuple(index_at)].set(smallest).at[tuple(beside)].set(largest)


def shard_levels(key, extent, shards, smallest, largest):
    loudness = 1.0
    for dim, blocks in shards:
        steps = jax.random.uniform(jax.random.fold_in(jax.random.fold_in(key, 6), dim), (blocks,), jnp.float32, smallest / len(shards), largest / len(shards))
        loudness = loudness * jnp.repeat(jnp.exp(steps), extent[dim] // blocks).reshape((-1,) + (1,) * (len(extent) - 1 - dim))
    return loudness


def scatter_about(key, dims, spread, most, pieces=(), held_as=jnp.bfloat16):
    drawn = jax.random.normal(key, dims, jnp.float32) * spread
    if len(pieces) > 0:
        drawn = shard_levels(key, dims, pieces, -0.22, 0.18) * drawn
    return jnp.clip(drawn, min=-most, max=most).astype(held_as)


def setup_inputs(seed: int = 0) -> dict:
    seeds = jax.random.split(jax.random.key(seed), 6)
    return {
        "wave": scatter_about(seeds[0], (2, FREQS, POS, POS), 1.0, 6.0, ((1, 2), (2, 16))),
        "filters": scatter_about(seeds[1], (NSTEP, 2, FREQS, VBINS, TAPS * TAPS), (1.2 / TAPS), 0.6640625, ((2, 2),)),
        "vel_bins": set_ends(jax.random.randint(seeds[2], (NSTEP, 2, BLEND, POS), 0, VBINS), jax.random.fold_in(seeds[2], 1), 0, VBINS - 1).astype(jnp.int32),
        "blend_levels": set_ends(jax.random.randint(seeds[3], (NSTEP, 2, BLEND, POS), 1, 17), jax.random.fold_in(seeds[3], 1), 1, 16).astype(jnp.int32),
        "aperture": set_ends((jax.random.randint(seeds[4], (NSTEP, NBLK, NBLK), 0, 3) < 2).astype(jnp.int32), jax.random.fold_in(seeds[4], 1), 0, 1),
    }


def blend_table(bin_ids, levels):
    weights = levels.astype(jnp.float32)
    onehot = (bin_ids[:, None, :] == jnp.arange(VBINS, dtype=jnp.int32)[None, :, None]).astype(jnp.float32)
    return jnp.sum(onehot * weights[:, None, :], axis=0) / jnp.sum(weights, axis=0)[None, :]


def extrapolate(field, filters_now, table):
    length = SIDE + TAPS - 1
    half_taps = TAPS // 2

    def one_freq(operands):
        real_part, imag_part, filt_real, filt_imag = operands
        batch_rows = real_part.shape[0]
        grid_field = (real_part.astype(jnp.float32) + 1j * imag_part.astype(jnp.float32)).reshape(batch_rows, SIDE, SIDE)
        kernel = (filt_real.astype(jnp.float32) + 1j * filt_imag.astype(jnp.float32)).reshape(VBINS, TAPS, TAPS)[:, ::-1, ::-1]
        spectra = jnp.fft.fft2(grid_field, s=(length, length))
        kernel_spec = jnp.fft.fft2(kernel, s=(length, length))

        def bin_term(velocity):
            full_field = jnp.fft.ifft2(spectra * kernel_spec[velocity][None])
            cropped = full_field[:, half_taps:half_taps + SIDE, half_taps:half_taps + SIDE].reshape(batch_rows, SIDE * SIDE)
            return table[velocity][None, :] * cropped

        running = bin_term(0)
        for velocity in range(1, VBINS):
            running = running + bin_term(velocity)
        return jnp.stack([jnp.real(running), jnp.imag(running)]).astype(jnp.bfloat16)

    result = lax.map(one_freq, (field[0], field[1], filters_now[0], filters_now[1]))
    return jnp.swapaxes(result, 0, 1)


def aperture_field(blocks):
    return jnp.repeat(jnp.repeat(blocks, BLK, axis=0), BLK, axis=1)


def reference(wave, filters, vel_bins, blend_levels, aperture):
    first = extrapolate(wave, filters[0], blend_table(vel_bins[0, 0], blend_levels[0, 0]))
    second = extrapolate(jnp.swapaxes(first, 2, 3), filters[0], blend_table(vel_bins[0, 1], blend_levels[0, 1]))
    keep_mask = aperture_field(aperture[0]).T
    shallow_field = jnp.where(keep_mask[None, None] > 0, second, jnp.zeros_like(second))
    image_shallow = jnp.sum(shallow_field[0].astype(jnp.float32), axis=0)
    third = extrapolate(shallow_field, filters[1], blend_table(vel_bins[1, 1], blend_levels[1, 1]))
    fourth = extrapolate(jnp.swapaxes(third, 2, 3), filters[1], blend_table(vel_bins[1, 0], blend_levels[1, 0]))
    keep_mask = aperture_field(aperture[1])
    deep_field = jnp.where(keep_mask[None, None] > 0, fourth, jnp.zeros_like(fourth))
    image_deep = jnp.sum(deep_field[0].astype(jnp.float32), axis=0)
    return image_shallow, image_deep
```

```python
import functools
import math

import jax
import jax.numpy as jnp
from jax import lax
from jax.experimental import pallas as pl
from jax.experimental.pallas import tpu as pltpu
from jax.sharding import PartitionSpec as P

LANES = 128
VMEM_LIMIT = 24 * 1024 * 1024


class Sizes:
    def __init__(self, mesh, wave_shape, filters_shape, aperture_shape):
        self.wide = mesh.shape["wide"]
        self.freq = mesh.shape["freq"]
        self.pos = wave_shape[-1]
        self.rows = wave_shape[-2]
        self.side = math.isqrt(self.pos)
        self.bins = filters_shape[-2]
        self.tap_count = filters_shape[-1]
        self.taps = math.isqrt(self.tap_count)
        self.half = self.taps // 2
        self.tile_rows = LANES // self.side
        self.tiles = self.pos // LANES
        self.halo = -(-self.half // self.tile_rows)
        self.window = (1 + 2 * self.halo) * LANES
        self.blocks = aperture_shape[-1]
        self.blk = self.pos // self.blocks


def fill_taps(z, filt_ref, step, rows_ref):
    rows_ref[...] = jnp.zeros_like(rows_ref)
    for part in range(2):
        rows_ref[part * z.bins : (part + 1) * z.bins, : z.tap_count] = filt_ref[step, part, 0].astype(
            jnp.float32
        )


def fill_table(z, bins_ref, levels_ref, step, side, table_ref):
    ids = bins_ref[step, side]
    weights = levels_ref[step, side].astype(jnp.float32)
    total = jnp.sum(weights, axis=0, keepdims=True)
    table_ref[...] = jnp.zeros_like(table_ref)
    for k in range(z.bins):
        hit = jnp.sum(jnp.where(ids == k, weights, 0.0), axis=0, keepdims=True)
        table_ref[k : k + 1, :] = hit / total


def tap_index(z, in_y, in_x, out_y, out_x):
    a = in_y - out_y + (z.half - z.halo * z.tile_rows)
    b = in_x - out_x + z.half
    valid = (a >= 0) & (a < z.taps) & (b >= 0) & (b < z.taps)
    return jnp.where(valid, a * z.taps + b, LANES - 1)


def spread(rows_ref, row, index):
    source = jnp.broadcast_to(rows_ref[row : row + 1, :], index.shape)
    return jnp.take_along_axis(source, index, axis=1, mode="promise_in_bounds")


def chunk_order(z, column):
    chunk, inside = column // (2 * z.rows), column % (2 * z.rows)
    return inside // z.rows, chunk * z.rows + inside % z.rows


def first_kernel(z, wave_ref, filt_ref, bins_ref, levels_ref, out_ref, taps_ref, table_ref, band_ref, lhs_ref):
    fill_taps(z, filt_ref, 0, taps_ref)
    fill_table(z, bins_ref, levels_ref, 0, 0, table_ref)
    lane = lax.broadcasted_iota(jnp.int32, (z.window, LANES), 1)
    row = lax.broadcasted_iota(jnp.int32, (z.window, LANES), 0)
    for v in range(2):
        part, point = chunk_order(z, lane + v * LANES)
        index = tap_index(z, row // z.side, row % z.side, point // z.side, point % z.side)
        for k in range(z.bins):
            real, imag = spread(taps_ref, k, index), spread(taps_ref, z.bins + k, index)
            columns = slice((2 * k + v) * LANES, (2 * k + v + 1) * LANES)
            band_ref[: z.window, columns] = jnp.where(part == 0, real, imag).astype(jnp.bfloat16)
            band_ref[z.window :, columns] = jnp.where(part == 0, -imag, real).astype(jnp.bfloat16)
    spans = 1 + 2 * z.halo
    for part in range(2):
        for tile in range(z.tiles):
            for span in range(spans):
                source = tile + span - z.halo
                place = (part * spans + span) * LANES
                if 0 <= source < z.tiles:
                    piece = wave_ref[part, :, source * LANES : (source + 1) * LANES]
                else:
                    piece = jnp.zeros((z.rows, LANES), jnp.bfloat16)
                lhs_ref[tile * z.rows : (tile + 1) * z.rows, place : place + LANES] = piece
    lane = lax.broadcasted_iota(jnp.int32, (8, LANES), 1)
    points = [chunk_order(z, lane + v * LANES)[1] for v in range(2)]
    products = [
        jnp.dot(
            lhs_ref[...],
            band_ref[:, 2 * k * LANES : 2 * (k + 1) * LANES],
            preferred_element_type=jnp.float32,
        )
        for k in range(z.bins)
    ]
    for tile in range(z.tiles):
        weights = table_ref[:, tile * LANES : (tile + 1) * LANES]
        weights = jnp.concatenate(
            [jnp.take_along_axis(weights, p, axis=1, mode="promise_in_bounds") for p in points], axis=1
        )
        total = 0.0
        for k in range(z.bins):
            total = total + products[k][tile * z.rows : (tile + 1) * z.rows] * weights[k : k + 1]
        total = total.astype(jnp.bfloat16)
        chunks = LANES // z.rows
        for c in range(chunks):
            out_ref[tile * chunks + c] = total[:, 2 * z.rows * c : 2 * z.rows * (c + 1)]


def fill_columns(z, rows_ref, band_ref):
    lane = lax.broadcasted_iota(jnp.int32, (LANES, LANES), 1)
    row = lax.broadcasted_iota(jnp.int32, (LANES, LANES), 0)
    for span in range(1 + 2 * z.halo):
        inner = lane + span * LANES
        index = tap_index(z, inner // z.side, inner % z.side, row // z.side, row % z.side)
        for k in range(z.bins):
            for part in range(2):
                place = part * z.window + span * LANES
                band_ref[k * LANES : (k + 1) * LANES, place : place + LANES] = spread(
                    rows_ref, part * z.bins + k, index
                ).astype(jnp.bfloat16)


def turned(z, block):
    return jnp.concatenate([-block[:, z.rows :], block[:, : z.rows]], axis=1)


def over_sources(z, band_ref, columns, straight_ref, turned_ref, tile):
    start = tile * LANES
    rhs = jnp.concatenate(
        [straight_ref[start : start + z.window, :], turned_ref[start : start + z.window, :]], axis=0
    )
    product = jnp.dot(band_ref[...], rhs, preferred_element_type=jnp.float32)
    total = 0.0
    for k in range(z.bins):
        total = total + product[k * LANES : (k + 1) * LANES] * columns[start : start + LANES, k : k + 1]
    return total.astype(jnp.bfloat16)


def split_sum(z, real_ref, send_ref, own_ref):
    me = lax.axis_index("freq")
    width = z.pos // z.freq

    def part(shift):
        start = lax.rem(me + shift, z.freq) * width
        return real_ref[:, pl.ds(pl.multiple_of(start, width), width)]

    own_ref[...] = part(0).astype(jnp.float32)
    for shift in range(1, z.freq):
        send_ref[shift - 1] = part(shift)


def middle_kernel(
    z,
    moved_ref,
    filt_ref,
    bins_ref,
    levels_ref,
    aperture_ref,
    out_ref,
    send_ref,
    own_ref,
    taps_ref,
    table_ref,
    band_ref,
    straight_ref,
    turned_ref,
    real_ref,
):
    pad = z.halo * LANES
    width = 2 * z.rows
    for ref in (straight_ref, turned_ref):
        ref[:pad, :] = jnp.zeros((pad, width), jnp.bfloat16)
        ref[pad + z.pos :, :] = jnp.zeros((pad, width), jnp.bfloat16)
    field = moved_ref[...].reshape(z.pos, width)
    straight_ref[pad : pad + z.pos, :] = field
    turned_ref[pad : pad + z.pos, :] = turned(z, field)
    offset = lax.axis_index("wide") * z.rows
    receiver = lax.broadcasted_iota(jnp.int32, (z.blocks, width), 1) % z.rows + offset
    pick = (receiver // z.blk == lax.broadcasted_iota(jnp.int32, (z.blocks, width), 0)).astype(jnp.float32)
    keep = jnp.dot(aperture_ref[0].astype(jnp.float32), pick, preferred_element_type=jnp.float32)

    fill_taps(z, filt_ref, 0, taps_ref)
    fill_columns(z, taps_ref, band_ref)
    fill_table(z, bins_ref, levels_ref, 0, 1, table_ref)
    columns = jnp.transpose(table_ref[...])
    shallow = []
    per_tile = LANES // z.blk
    for tile in range(z.tiles):
        second = over_sources(z, band_ref, columns, straight_ref, turned_ref, tile)
        mask = keep[tile * per_tile : (tile + 1) * per_tile]
        mask = jnp.broadcast_to(mask[:, None, :], (per_tile, z.blk, width)).reshape(LANES, width)
        shallow.append(jnp.where(mask > 0.5, second, jnp.zeros_like(second)))
    for tile in range(z.tiles):
        place = pad + tile * LANES
        straight_ref[place : place + LANES, :] = shallow[tile]
        turned_ref[place : place + LANES, :] = turned(z, shallow[tile])
        flipped = jnp.transpose(shallow[tile].astype(jnp.float32))
        real_ref[:, tile * LANES : (tile + 1) * LANES] = flipped[: z.rows].astype(jnp.bfloat16)
    split_sum(z, real_ref, send_ref, own_ref)

    fill_taps(z, filt_ref, 1, taps_ref)
    fill_columns(z, taps_ref, band_ref)
    fill_table(z, bins_ref, levels_ref, 1, 1, table_ref)
    columns = jnp.transpose(table_ref[...])
    chunks = LANES // z.rows
    for tile in range(z.tiles):
        third = over_sources(z, band_ref, columns, straight_ref, turned_ref, tile)
        out_ref[tile * chunks : (tile + 1) * chunks] = third.reshape(chunks, z.rows, width)


def last_kernel(
    z,
    field_ref,
    filt_ref,
    bins_ref,
    levels_ref,
    aperture_ref,
    send_ref,
    own_ref,
    taps_ref,
    table_ref,
    band_ref,
    lhs_ref,
    real_ref,
):
    fill_taps(z, filt_ref, 1, taps_ref)
    fill_table(z, bins_ref, levels_ref, 1, 0, table_ref)
    lane = lax.broadcasted_iota(jnp.int32, (z.rows, LANES), 1)
    row = lax.broadcasted_iota(jnp.int32, (z.rows, LANES), 0)
    for block in range(2 * z.window // z.rows):
        part, start = block % 2, block // 2 * z.rows
        inner = row + start
        index = tap_index(z, inner // z.side, inner % z.side, lane // z.side, lane % z.side)
        for k in range(z.bins):
            taps = spread(taps_ref, part * z.bins + k, index)
            taps = taps if part == 0 else -taps
            band_ref[block * z.rows : (block + 1) * z.rows, k * LANES : (k + 1) * LANES] = taps.astype(
                jnp.bfloat16
            )
    per_tile = LANES // z.rows
    width = 2 * z.rows
    for tile in range(z.tiles):
        for place in range((1 + 2 * z.halo) * per_tile):
            source = (tile - z.halo) * per_tile + place
            if 0 <= source < z.wide:
                piece = field_ref[source]
            else:
                piece = jnp.zeros((z.rows, width), jnp.bfloat16)
            lhs_ref[tile * z.rows : (tile + 1) * z.rows, place * width : (place + 1) * width] = piece
    offset = lax.axis_index("wide") * z.rows
    source = lax.broadcasted_iota(jnp.int32, (z.rows, z.blocks), 0) + offset
    pick = (source // z.blk == lax.broadcasted_iota(jnp.int32, (z.rows, z.blocks), 1)).astype(jnp.float32)
    mine = jnp.dot(pick, aperture_ref[1].astype(jnp.float32), preferred_element_type=jnp.float32)
    receiver = lax.broadcasted_iota(jnp.int32, (z.blocks, z.pos), 1)
    stretch = (receiver // z.blk == lax.broadcasted_iota(jnp.int32, (z.blocks, z.pos), 0)).astype(jnp.float32)
    keep = jnp.dot(mine, stretch, preferred_element_type=jnp.float32)
    product = jnp.dot(lhs_ref[...], band_ref[...], preferred_element_type=jnp.float32)
    for tile in range(z.tiles):
        columns = slice(tile * LANES, (tile + 1) * LANES)
        total = 0.0
        for k in range(z.bins):
            part = product[tile * z.rows : (tile + 1) * z.rows, k * LANES : (k + 1) * LANES]
            total = total + part * table_ref[k : k + 1, columns]
        real_ref[:, columns] = jnp.where(keep[:, columns] > 0.5, total, 0.0).astype(jnp.bfloat16)
    split_sum(z, real_ref, send_ref, own_ref)


def call(kernel, operands, outs, scratch, flops, name):
    spec = pl.BlockSpec(memory_space=pltpu.VMEM)
    return pl.pallas_call(
        kernel,
        out_shape=outs,
        in_specs=[spec] * len(operands),
        out_specs=jax.tree.map(lambda _: spec, outs),
        scratch_shapes=[pltpu.VMEM(shape, dtype) for shape, dtype in scratch],
        compiler_params=pltpu.CompilerParams(vmem_limit_bytes=VMEM_LIMIT),
        cost_estimate=pl.CostEstimate(flops=flops, bytes_accessed=1 << 20, transcendentals=0),
        name=name,
    )(*operands)


def freq_sum(z, send, own):
    total = own
    for shift in range(1, z.freq):
        pairs = [(source, (source + shift) % z.freq) for source in range(z.freq)]
        total = total + lax.ppermute(send[shift - 1], "freq", pairs).astype(jnp.float32)
    return total


def body(mesh, wave, filters, vel_bins, blend_levels, aperture):
    z = Sizes(mesh, wave.shape, filters.shape, aperture.shape)
    bf16, f32 = jnp.bfloat16, jnp.float32
    chunks = jax.ShapeDtypeStruct((z.wide, z.rows, 2 * z.rows), bf16)
    width = z.pos // z.freq
    parts = [
        jax.ShapeDtypeStruct((z.freq - 1, z.rows, width), bf16),
        jax.ShapeDtypeStruct((z.rows, width), f32),
    ]
    small = [((8, LANES), f32), ((8, z.pos), f32)]
    dense = 2 * 2 * z.window * z.bins * z.pos * z.rows
    first = call(
        functools.partial(first_kernel, z),
        (wave[:, 0], filters, vel_bins, blend_levels),
        chunks,
        small
        + [
            ((2 * z.window, 2 * z.bins * LANES), bf16),
            ((z.tiles * z.rows, 2 * z.window), bf16),
        ],
        2 * dense,
        "first",
    )
    moved = lax.all_to_all(first, "wide", 0, 0, tiled=True)
    padded = z.pos + 2 * z.halo * LANES
    third, send, own = call(
        functools.partial(middle_kernel, z),
        (moved, filters, vel_bins, blend_levels, aperture),
        [chunks] + parts,
        small
        + [
            ((z.bins * LANES, 2 * z.window), bf16),
            ((padded, 2 * z.rows), bf16),
            ((padded, 2 * z.rows), bf16),
            ((z.rows, z.pos), bf16),
        ],
        4 * dense,
        "middle",
    )
    returned = lax.all_to_all(third, "wide", 0, 0, tiled=True)
    image_shallow = freq_sum(z, send, own)
    send, own = call(
        functools.partial(last_kernel, z),
        (returned, filters, vel_bins, blend_levels, aperture),
        parts,
        small
        + [
            ((2 * z.window, z.bins * LANES), bf16),
            ((z.tiles * z.rows, 2 * z.window), bf16),
            ((z.rows, z.pos), bf16),
        ],
        dense,
        "last",
    )
    image_deep = freq_sum(z, send, own)
    return image_shallow, image_deep


def solution(mesh):
    return jax.shard_map(
        functools.partial(body, mesh),
        mesh=mesh,
        in_specs=(P(None, "freq", "wide", None), P(None, None, "freq", None, None), P(), P(), P()),
        out_specs=(P("wide", "freq"), P("wide", "freq")),
        check_vma=False,
    )
```

```python
import functools
import math

import jax
import jax.numpy as jnp
from jax import lax
from jax.experimental import pallas as pl
from jax.experimental.pallas import tpu as pltpu
from jax.sharding import PartitionSpec as P

LANES = 128
VMEM_LIMIT = 24 * 1024 * 1024


class Sizes:
    def __init__(self, mesh, wave_shape, filters_shape, aperture_shape):
        self.wide = mesh.shape["wide"]
        self.freq = mesh.shape["freq"]
        self.pos = wave_shape[-1]
        self.rows = wave_shape[-2]
        self.side = math.isqrt(self.pos)
        self.bins = filters_shape[-2]
        self.tap_count = filters_shape[-1]
        self.taps = math.isqrt(self.tap_count)
        self.half = self.taps // 2
        self.tile_rows = LANES // self.side
        self.tiles = self.pos // LANES
        self.halo = -(-self.half // self.tile_rows)
        self.window = (1 + 2 * self.halo) * LANES
        self.blocks = aperture_shape[-1]
        self.blk = self.pos // self.blocks


def fill_taps(z, filt_ref, step, rows_ref):
    rows_ref[...] = jnp.zeros_like(rows_ref)
    for k in range(z.bins):
        pair = filt_ref[step, 0, k].astype(jnp.float32)
        for part in range(2):
            row = part * z.bins + k
            rows_ref[row : row + 1, : z.tap_count] = pair[part : part + 1]


def fill_table(z, bins_ref, levels_ref, step, side, table_ref):
    blend = bins_ref.shape[1]
    ids = [bins_ref[step, j, side : side + 1] for j in range(blend)]
    weights = [levels_ref[step, j, side : side + 1].astype(jnp.float32) for j in range(blend)]
    total = sum(weights[1:], weights[0])
    table_ref[...] = jnp.zeros_like(table_ref)
    for k in range(z.bins):
        hits = [jnp.where(i == k, w, 0.0) for i, w in zip(ids, weights)]
        table_ref[k : k + 1, :] = sum(hits[1:], hits[0]) / total


def tap_index(z, in_y, in_x, out_y, out_x):
    a = in_y - out_y + (z.half - z.halo * z.tile_rows)
    b = in_x - out_x + z.half
    valid = (a >= 0) & (a < z.taps) & (b >= 0) & (b < z.taps)
    return jnp.where(valid, a * z.taps + b, LANES - 1)


def spread(rows_ref, row, index):
    source = jnp.broadcast_to(rows_ref[row : row + 1, :], index.shape)
    return jnp.take_along_axis(source, index, axis=1, mode="promise_in_bounds")


def chunk_order(z, column):
    chunk, inside = column // (2 * z.rows), column % (2 * z.rows)
    return inside // z.rows, chunk * z.rows + inside % z.rows


def fetch(pairs, sems):
    copies = [pltpu.make_async_copy(source, target, sems.at[i]) for i, (source, target) in enumerate(pairs)]
    for copy in copies:
        copy.start()
    return copies


def sent(z, out_ref, out_hbm, sems, tile):
    chunks = LANES // z.rows
    place = pl.ds(tile * chunks, chunks)
    return pltpu.make_async_copy(out_ref.at[place], out_hbm.at[place], sems.at[tile])


def send_out(z, out_ref, out_hbm, sems, tile):
    sent(z, out_ref, out_hbm, sems, tile).start()


def first_kernel(
    z,
    wave_hbm,
    filt_hbm,
    bins_hbm,
    levels_hbm,
    out_hbm,
    wave_ref,
    filt_ref,
    bins_ref,
    levels_ref,
    taps_ref,
    table_ref,
    band_ref,
    lhs_ref,
    out_ref,
    out_sems,
    sems,
):
    copies = fetch(
        [(filt_hbm, filt_ref), (bins_hbm, bins_ref), (levels_hbm, levels_ref), (wave_hbm, wave_ref)], sems
    )
    copies[0].wait()
    fill_taps(z, filt_ref, 0, taps_ref)
    lane = lax.broadcasted_iota(jnp.int32, (z.window, LANES), 1)
    row = lax.broadcasted_iota(jnp.int32, (z.window, LANES), 0)
    for v in range(2):
        part, point = chunk_order(z, lane + v * LANES)
        index = tap_index(z, row // z.side, row % z.side, point // z.side, point % z.side)
        for k in range(z.bins):
            real, imag = spread(taps_ref, k, index), spread(taps_ref, z.bins + k, index)
            columns = slice((2 * k + v) * LANES, (2 * k + v + 1) * LANES)
            band_ref[: z.window, columns] = jnp.where(part == 0, real, imag).astype(jnp.bfloat16)
            band_ref[z.window :, columns] = jnp.where(part == 0, -imag, real).astype(jnp.bfloat16)
    copies[1].wait()
    copies[2].wait()
    fill_table(z, bins_ref, levels_ref, 0, 0, table_ref)
    copies[3].wait()
    spans = 1 + 2 * z.halo
    for part in range(2):
        for tile in range(z.tiles):
            for span in range(spans):
                source = tile + span - z.halo
                place = (part * spans + span) * LANES
                if 0 <= source < z.tiles:
                    piece = wave_ref[part, :, source * LANES : (source + 1) * LANES]
                else:
                    piece = jnp.zeros((z.rows, LANES), jnp.bfloat16)
                lhs_ref[tile * z.rows : (tile + 1) * z.rows, place : place + LANES] = piece
    lane = lax.broadcasted_iota(jnp.int32, (8, LANES), 1)
    points = [chunk_order(z, lane + v * LANES)[1] for v in range(2)]
    products = [
        jnp.dot(
            lhs_ref[...],
            band_ref[:, 2 * k * LANES : 2 * (k + 1) * LANES],
            preferred_element_type=jnp.float32,
        )
        for k in range(z.bins)
    ]
    for tile in range(z.tiles):
        weights = table_ref[:, tile * LANES : (tile + 1) * LANES]
        weights = jnp.concatenate(
            [jnp.take_along_axis(weights, p, axis=1, mode="promise_in_bounds") for p in points], axis=1
        )
        total = 0.0
        for k in range(z.bins):
            total = total + products[k][tile * z.rows : (tile + 1) * z.rows] * weights[k : k + 1]
        total = total.astype(jnp.bfloat16)
        chunks = LANES // z.rows
        for c in range(chunks):
            out_ref[tile * chunks + c] = total[:, 2 * z.rows * c : 2 * z.rows * (c + 1)]
        send_out(z, out_ref, out_hbm, out_sems, tile)
    for tile in range(z.tiles):
        sent(z, out_ref, out_hbm, out_sems, tile).wait()


def prepare_middle_kernel(
    z,
    filt_hbm,
    bins_hbm,
    levels_hbm,
    aperture_hbm,
    second_ref,
    third_ref,
    keep_ref,
    filt_ref,
    bins_ref,
    levels_ref,
    aperture_ref,
    taps_ref,
    table_ref,
    columns_ref,
    sems,
):
    copies = fetch(
        [(filt_hbm, filt_ref), (bins_hbm, bins_ref), (levels_hbm, levels_ref), (aperture_hbm, aperture_ref)],
        sems,
    )
    for copy in copies:
        copy.wait()
    lane = lax.broadcasted_iota(jnp.int32, (LANES, LANES), 1)
    row = lax.broadcasted_iota(jnp.int32, (LANES, LANES), 0)
    for step, band_ref in ((0, second_ref), (1, third_ref)):
        fill_taps(z, filt_ref, step, taps_ref)
        fill_table(z, bins_ref, levels_ref, step, 1, table_ref)
        columns = jnp.transpose(table_ref[...])
        for k in range(z.bins):
            columns_ref[k] = jnp.broadcast_to(columns[:, k : k + 1], (z.pos, LANES))

        @pl.loop(0, 1 + 2 * z.halo)
        def _(span, band_ref=band_ref):
            inner = lane + span * LANES
            index = tap_index(z, inner // z.side, inner % z.side, row // z.side, row % z.side)
            for part in range(2):
                taps = [spread(taps_ref, part * z.bins + k, index) for k in range(z.bins)]
                place = pl.multiple_of(part * z.window + span * LANES, LANES)
                for tile in range(z.tiles):
                    total = 0.0
                    for k in range(z.bins):
                        total = total + taps[k] * columns_ref[k, tile * LANES : (tile + 1) * LANES, :]
                    band_ref[tile, :, pl.ds(place, LANES)] = total.astype(jnp.bfloat16)

    width = 2 * z.rows
    offset = lax.axis_index("wide") * z.rows
    receiver = lax.broadcasted_iota(jnp.int32, (z.blocks, width), 1) % z.rows + offset
    pick = (receiver // z.blk == lax.broadcasted_iota(jnp.int32, (z.blocks, width), 0)).astype(jnp.float32)
    keep_ref[...] = jnp.dot(aperture_ref[0].astype(jnp.float32), pick, preferred_element_type=jnp.float32)


def prepare_last_kernel(
    z,
    filt_hbm,
    bins_hbm,
    levels_hbm,
    aperture_hbm,
    fourth_ref,
    keep_ref,
    filt_ref,
    bins_ref,
    levels_ref,
    aperture_ref,
    taps_ref,
    table_ref,
    sems,
):
    copies = fetch(
        [(filt_hbm, filt_ref), (bins_hbm, bins_ref), (levels_hbm, levels_ref), (aperture_hbm, aperture_ref)],
        sems,
    )
    for copy in copies:
        copy.wait()
    fill_taps(z, filt_ref, 1, taps_ref)
    fill_table(z, bins_ref, levels_ref, 1, 0, table_ref)
    lane = lax.broadcasted_iota(jnp.int32, (z.rows, LANES), 1)
    row = lax.broadcasted_iota(jnp.int32, (z.rows, LANES), 0)

    @pl.loop(0, z.window // z.rows)
    def _(block):
        inner = row + block * z.rows
        index = tap_index(z, inner // z.side, inner % z.side, lane // z.side, lane % z.side)
        for part in range(2):
            taps = [spread(taps_ref, part * z.bins + k, index) for k in range(z.bins)]
            place = pl.multiple_of((2 * block + part) * z.rows, z.rows)
            for tile in range(z.tiles):
                total = 0.0
                for k in range(z.bins):
                    total = total + taps[k] * table_ref[k : k + 1, tile * LANES : (tile + 1) * LANES]
                total = total if part == 0 else -total
                fourth_ref[tile, pl.ds(place, z.rows), :] = total.astype(jnp.bfloat16)

    offset = lax.axis_index("wide") * z.rows
    source = lax.broadcasted_iota(jnp.int32, (z.rows, z.blocks), 0) + offset
    pick = (source // z.blk == lax.broadcasted_iota(jnp.int32, (z.rows, z.blocks), 1)).astype(jnp.float32)
    mine = jnp.dot(pick, aperture_ref[1].astype(jnp.float32), preferred_element_type=jnp.float32)
    receiver = lax.broadcasted_iota(jnp.int32, (z.blocks, z.pos), 1)
    stretch = (receiver // z.blk == lax.broadcasted_iota(jnp.int32, (z.blocks, z.pos), 0)).astype(jnp.float32)
    keep_ref[...] = jnp.dot(mine, stretch, preferred_element_type=jnp.float32)


def turned(z, block):
    return jnp.concatenate([-block[:, z.rows :], block[:, : z.rows]], axis=1)


def over_sources(z, band_ref, straight_ref, turned_ref, tile):
    start = tile * LANES
    rhs = jnp.concatenate(
        [straight_ref[start : start + z.window, :], turned_ref[start : start + z.window, :]], axis=0
    )
    return jnp.dot(band_ref[tile], rhs, preferred_element_type=jnp.float32)


def middle_kernel(
    z,
    moved_ref,
    second_ref,
    third_ref,
    keep_ref,
    out_hbm,
    shallow_hbm,
    straight_ref,
    turned_ref,
    straight2_ref,
    turned2_ref,
    out_ref,
    out_sems,
    shallow_sem,
):
    pad = z.halo * LANES
    width = 2 * z.rows
    for ref in (straight_ref, turned_ref, straight2_ref, turned2_ref):
        ref[:pad, :] = jnp.zeros((pad, width), jnp.bfloat16)
        ref[pad + z.pos :, :] = jnp.zeros((pad, width), jnp.bfloat16)
    field = moved_ref[...].reshape(z.pos, width)
    straight_ref[pad : pad + z.pos, :] = field
    turned_ref[pad : pad + z.pos, :] = turned(z, field)
    per_tile = LANES // z.blk
    for tile in range(z.tiles):
        place = slice(pad + tile * LANES, pad + (tile + 1) * LANES)
        mask = keep_ref[tile * per_tile : (tile + 1) * per_tile, :]
        mask = jnp.broadcast_to(mask[:, None, :], (per_tile, z.blk, width)).reshape(LANES, width)
        shallow = over_sources(z, second_ref, straight_ref, turned_ref, tile) * mask
        shallow = shallow.astype(jnp.bfloat16)
        straight2_ref[place, :] = shallow
        turned2_ref[place, :] = turned(z, shallow)
    shallow_copy = pltpu.make_async_copy(
        straight2_ref.at[pl.ds(pad, z.pos)], shallow_hbm, shallow_sem.at[0]
    )
    shallow_copy.start()
    chunks = LANES // z.rows
    for tile in range(z.tiles):
        third = over_sources(z, third_ref, straight2_ref, turned2_ref, tile).astype(jnp.bfloat16)
        out_ref[tile * chunks : (tile + 1) * chunks] = third.reshape(chunks, z.rows, width)
        send_out(z, out_ref, out_hbm, out_sems, tile)
    for tile in range(z.tiles):
        sent(z, out_ref, out_hbm, out_sems, tile).wait()
    shallow_copy.wait()


def split_sum(z, real_ref, send_ref, own_ref):
    me = lax.axis_index("freq")
    width = z.pos // z.freq

    def part(shift):
        start = lax.rem(me + shift, z.freq) * width
        return real_ref[:, pl.ds(pl.multiple_of(start, width), width)]

    own_ref[...] = part(0).astype(jnp.float32)
    for shift in range(1, z.freq):
        send_ref[shift - 1] = part(shift)


def turn_kernel(z, shallow_hbm, send_ref, own_ref, shallow_ref, real_ref, sems):
    for copy in fetch([(shallow_hbm, shallow_ref)], sems):
        copy.wait()
    for tile in range(z.tiles):
        columns = slice(tile * LANES, (tile + 1) * LANES)
        flipped = jnp.transpose(shallow_ref[columns, :].astype(jnp.float32))
        real_ref[:, columns] = flipped[: z.rows].astype(jnp.bfloat16)
    split_sum(z, real_ref, send_ref, own_ref)


def last_kernel(z, field_ref, fourth_ref, keep_ref, send_ref, own_ref, lhs_ref, real_ref):
    pad = 2 * z.halo * LANES
    width = 2 * z.rows
    lhs_ref[:, :pad] = jnp.zeros((z.rows, pad), jnp.bfloat16)
    lhs_ref[:, pad + 2 * z.pos :] = jnp.zeros((z.rows, pad), jnp.bfloat16)
    for source in range(z.wide):
        lhs_ref[:, pad + source * width : pad + (source + 1) * width] = field_ref[source]
    for tile in range(z.tiles):
        start = 2 * tile * LANES
        columns = slice(tile * LANES, (tile + 1) * LANES)
        fourth = jnp.dot(
            lhs_ref[:, start : start + 2 * z.window], fourth_ref[tile], preferred_element_type=jnp.float32
        )
        real_ref[:, columns] = (fourth * keep_ref[:, columns]).astype(jnp.bfloat16)
    split_sum(z, real_ref, send_ref, own_ref)


def call(kernel, operands, outs, scratch, flops, name, fetched=False, sent=()):
    source = pltpu.HBM if fetched else pltpu.VMEM
    spaces = [pltpu.HBM if i < len(sent) else pltpu.VMEM for i in range(len(outs))]
    scratch = [pltpu.VMEM(shape, dtype) for shape, dtype in scratch]
    if sent:
        scratch += [pltpu.VMEM(*outs[0])] + [pltpu.SemaphoreType.DMA((parts,)) for parts in sent]
    if fetched:
        scratch = [pltpu.VMEM(x.shape, x.dtype) for x in operands] + scratch
        scratch.append(pltpu.SemaphoreType.DMA((len(operands),)))
        operands = [pltpu.with_memory_space_constraint(x, pltpu.HBM) for x in operands]
    return pl.pallas_call(
        kernel,
        out_shape=[space(shape, dtype) for space, (shape, dtype) in zip(spaces, outs)],
        in_specs=[pl.BlockSpec(memory_space=source)] * len(operands),
        out_specs=[pl.BlockSpec(memory_space=space) for space in spaces],
        scratch_shapes=scratch,
        compiler_params=pltpu.CompilerParams(vmem_limit_bytes=VMEM_LIMIT),
        cost_estimate=pl.CostEstimate(flops=flops, bytes_accessed=1 << 20, transcendentals=0),
        name=name,
    )(*operands)


def freq_sum(z, send, own):
    total = own
    for shift in range(1, z.freq):
        pairs = [(source, (source + shift) % z.freq) for source in range(z.freq)]
        total = total + lax.ppermute(send[shift - 1], "freq", pairs).astype(jnp.float32)
    return total


def body(mesh, wave, filters, vel_bins, blend_levels, aperture):
    z = Sizes(mesh, wave.shape, filters.shape, aperture.shape)
    bf16, f32 = jnp.bfloat16, jnp.float32
    filters = jnp.transpose(filters, (0, 2, 3, 1, 4))
    vel_bins = jnp.transpose(vel_bins, (0, 2, 1, 3))
    blend_levels = jnp.transpose(blend_levels, (0, 2, 1, 3))
    width = 2 * z.rows
    chunks = ((z.wide, z.rows, width), bf16)
    split = z.pos // z.freq
    parts = [((z.freq - 1, z.rows, split), bf16), ((z.rows, split), f32)]
    small = [((8, LANES), f32), ((8, z.pos), f32)]
    dense = 2 * 2 * z.window * z.bins * z.pos * z.rows
    (first,) = call(
        functools.partial(first_kernel, z),
        (wave[:, 0], filters, vel_bins, blend_levels),
        [chunks],
        small
        + [
            ((2 * z.window, 2 * z.bins * LANES), bf16),
            ((z.tiles * z.rows, 2 * z.window), bf16),
        ],
        2 * dense,
        "first",
        fetched=True,
        sent=(z.tiles,),
    )
    moved = lax.all_to_all(first, "wide", 0, 0, tiled=True)
    second_band, third_band, shallow_keep = call(
        functools.partial(prepare_middle_kernel, z),
        (filters, vel_bins, blend_levels, aperture),
        [
            ((z.tiles, LANES, 2 * z.window), bf16),
            ((z.tiles, LANES, 2 * z.window), bf16),
            ((z.blocks, width), f32),
        ],
        small + [((z.bins, z.pos, LANES), f32)],
        dense,
        "prepare_middle",
        fetched=True,
    )
    padded = z.pos + 2 * z.halo * LANES
    third, shallow = call(
        functools.partial(middle_kernel, z),
        (moved, second_band, third_band, shallow_keep),
        [chunks, ((z.pos, width), bf16)],
        [((padded, width), bf16)] * 4,
        dense,
        "middle",
        sent=(z.tiles, 1),
    )
    returned = lax.all_to_all(third, "wide", 0, 0, tiled=True)
    fourth_band, deep_keep = call(
        functools.partial(prepare_last_kernel, z),
        (filters, vel_bins, blend_levels, aperture),
        [((z.tiles, 2 * z.window, LANES), bf16), ((z.rows, z.pos), f32)],
        small,
        dense,
        "prepare_last",
        fetched=True,
    )
    image_shallow = freq_sum(
        z,
        *call(
            functools.partial(turn_kernel, z),
            (shallow,),
            parts,
            [((z.rows, z.pos), bf16)],
            dense // 8,
            "turn",
            fetched=True,
        ),
    )
    returned, image_shallow, fourth_band, deep_keep = lax.optimization_barrier(
        (returned, image_shallow, fourth_band, deep_keep)
    )
    image_deep = freq_sum(
        z,
        *call(
            functools.partial(last_kernel, z),
            (returned, fourth_band, deep_keep),
            parts,
            [((z.rows, 2 * padded), bf16), ((z.rows, z.pos), bf16)],
            dense // 4,
            "last",
        ),
    )
    return image_shallow, image_deep


def solution(mesh):
    return jax.shard_map(
        functools.partial(body, mesh),
        mesh=mesh,
        in_specs=(P(None, "freq", "wide", None), P(None, None, "freq", None, None), P(), P(), P()),
        out_specs=(P("wide", "freq"), P("wide", "freq")),
        check_vma=False,
    )
```

```python
import functools
import math

import jax
import jax.numpy as jnp
from jax import lax
from jax.experimental import pallas as pl
from jax.experimental.pallas import tpu as pltpu
from jax.sharding import PartitionSpec as P

LANES = 128
VMEM_LIMIT = 24 * 1024 * 1024


class Sizes:
    def __init__(self, mesh, wave_shape, filters_shape, aperture_shape):
        self.wide = mesh.shape["wide"]
        self.freq = mesh.shape["freq"]
        self.pos = wave_shape[-1]
        self.rows = wave_shape[-2]
        self.side = math.isqrt(self.pos)
        self.bins = filters_shape[-2]
        self.tap_count = filters_shape[-1]
        self.taps = math.isqrt(self.tap_count)
        self.half = self.taps // 2
        self.tile_rows = LANES // self.side
        self.tiles = self.pos // LANES
        self.halo = -(-self.half // self.tile_rows)
        self.window = (1 + 2 * self.halo) * LANES
        self.blocks = aperture_shape[-1]
        self.blk = self.pos // self.blocks


def fill_taps(z, filt_ref, step, rows_ref):
    rows_ref[...] = jnp.zeros_like(rows_ref)
    for k in range(z.bins):
        pair = filt_ref[step, 0, k].astype(jnp.float32)
        for part in range(2):
            row = part * z.bins + k
            rows_ref[row : row + 1, : z.tap_count] = pair[part : part + 1]


def fill_table(z, bins_ref, levels_ref, step, side, table_ref):
    blend = bins_ref.shape[1]
    ids = [bins_ref[step, j, side : side + 1] for j in range(blend)]
    weights = [levels_ref[step, j, side : side + 1].astype(jnp.float32) for j in range(blend)]
    total = sum(weights[1:], weights[0])
    table_ref[...] = jnp.zeros_like(table_ref)
    for k in range(z.bins):
        hits = [jnp.where(i == k, w, 0.0) for i, w in zip(ids, weights)]
        table_ref[k : k + 1, :] = sum(hits[1:], hits[0]) / total


def tap_index(z, in_y, in_x, out_y, out_x):
    a = in_y - out_y + (z.half - z.halo * z.tile_rows)
    b = in_x - out_x + z.half
    valid = (a >= 0) & (a < z.taps) & (b >= 0) & (b < z.taps)
    return jnp.where(valid, a * z.taps + b, LANES - 1)


def spread(rows_ref, row, index):
    source = jnp.broadcast_to(rows_ref[row : row + 1, :], index.shape)
    return jnp.take_along_axis(source, index, axis=1, mode="promise_in_bounds")


def chunk_order(z, column):
    chunk, inside = column // (2 * z.rows), column % (2 * z.rows)
    return inside // z.rows, chunk * z.rows + inside % z.rows


def fetch(pairs, sems):
    copies = [pltpu.make_async_copy(source, target, sems.at[i]) for i, (source, target) in enumerate(pairs)]
    for copy in copies:
        copy.start()
    return copies


def sent(z, out_ref, out_hbm, sems, tile):
    chunks = LANES // z.rows
    place = pl.ds(tile * chunks, chunks)
    return pltpu.make_async_copy(out_ref.at[place], out_hbm.at[place], sems.at[tile])


def send_out(z, out_ref, out_hbm, sems, tile):
    sent(z, out_ref, out_hbm, sems, tile).start()


def first_kernel(
    z,
    wave_hbm,
    filt_hbm,
    bins_hbm,
    levels_hbm,
    out_hbm,
    wave_ref,
    filt_ref,
    bins_ref,
    levels_ref,
    taps_ref,
    table_ref,
    band_ref,
    lhs_ref,
    out_ref,
    out_sems,
    sems,
):
    copies = fetch(
        [(filt_hbm, filt_ref), (bins_hbm, bins_ref), (levels_hbm, levels_ref), (wave_hbm, wave_ref)], sems
    )
    group_rows = LANES // 2 // z.side
    window_rows = z.window // z.side
    lane = lax.broadcasted_iota(jnp.int32, (z.side, LANES), 1)
    part, point = chunk_order(z, lane)
    out_y = point // z.side - (z.half - z.halo * z.tile_rows)
    b = lax.broadcasted_iota(jnp.int32, (z.side, LANES), 0) - point % z.side + z.half
    b_valid = (b >= 0) & (b < z.taps)
    base = b - out_y * z.taps
    is_real = part == 0
    indices = []
    for y in range(window_rows - group_rows):
        valid = b_valid & (out_y <= y) & (out_y > y - z.taps)
        indices.append(jnp.where(valid, base + y * z.taps, LANES - 1))
    empty = jnp.zeros((group_rows * z.side, LANES), jnp.bfloat16)
    for k in range(z.bins):
        for half in range(2):
            top, columns = half * z.window, 2 * k * LANES
            band_ref[top + z.window - group_rows * z.side : top + z.window, columns : columns + LANES] = empty
            band_ref[top : top + group_rows * z.side, columns + LANES : columns + 2 * LANES] = empty
    copies[0].wait()
    fill_taps(z, filt_ref, 0, taps_ref)
    for k in range(z.bins):
        columns = 2 * k * LANES
        for y, index in enumerate(indices):
            real, imag = spread(taps_ref, k, index), spread(taps_ref, z.bins + k, index)
            blocks = (jnp.where(is_real, real, imag), jnp.where(is_real, -imag, real))
            for half in range(2):
                block = blocks[half].astype(jnp.bfloat16)
                top = half * z.window + y * z.side
                band_ref[top : top + z.side, columns : columns + LANES] = block
                top += group_rows * z.side
                band_ref[top : top + z.side, columns + LANES : columns + 2 * LANES] = block
    copies[1].wait()
    copies[2].wait()
    fill_table(z, bins_ref, levels_ref, 0, 0, table_ref)
    copies[3].wait()
    spans = 1 + 2 * z.halo
    for part in range(2):
        for tile in range(z.tiles):
            for span in range(spans):
                source = tile + span - z.halo
                place = (part * spans + span) * LANES
                if 0 <= source < z.tiles:
                    piece = wave_ref[part, :, source * LANES : (source + 1) * LANES]
                else:
                    piece = jnp.zeros((z.rows, LANES), jnp.bfloat16)
                lhs_ref[tile * z.rows : (tile + 1) * z.rows, place : place + LANES] = piece
    lane = lax.broadcasted_iota(jnp.int32, (8, LANES), 1)
    points = [chunk_order(z, lane + v * LANES)[1] for v in range(2)]
    products = [
        jnp.dot(
            lhs_ref[...],
            band_ref[:, 2 * k * LANES : 2 * (k + 1) * LANES],
            preferred_element_type=jnp.float32,
        )
        for k in range(z.bins)
    ]
    for tile in range(z.tiles):
        weights = table_ref[:, tile * LANES : (tile + 1) * LANES]
        weights = jnp.concatenate(
            [jnp.take_along_axis(weights, p, axis=1, mode="promise_in_bounds") for p in points], axis=1
        )
        total = 0.0
        for k in range(z.bins):
            total = total + products[k][tile * z.rows : (tile + 1) * z.rows] * weights[k : k + 1]
        total = total.astype(jnp.bfloat16)
        chunks = LANES // z.rows
        for c in range(chunks):
            out_ref[tile * chunks + c] = total[:, 2 * z.rows * c : 2 * z.rows * (c + 1)]
        send_out(z, out_ref, out_hbm, out_sems, tile)
    for tile in range(z.tiles):
        sent(z, out_ref, out_hbm, out_sems, tile).wait()


def prepare_middle_kernel(
    z,
    filt_hbm,
    bins_hbm,
    levels_hbm,
    aperture_hbm,
    second_ref,
    third_ref,
    keep_ref,
    filt_ref,
    bins_ref,
    levels_ref,
    aperture_ref,
    taps_ref,
    table_ref,
    columns_ref,
    sems,
):
    copies = fetch(
        [(filt_hbm, filt_ref), (bins_hbm, bins_ref), (levels_hbm, levels_ref), (aperture_hbm, aperture_ref)],
        sems,
    )
    for copy in copies:
        copy.wait()
    lane = lax.broadcasted_iota(jnp.int32, (LANES, LANES), 1)
    row = lax.broadcasted_iota(jnp.int32, (LANES, LANES), 0)
    for step, band_ref in ((0, second_ref), (1, third_ref)):
        fill_taps(z, filt_ref, step, taps_ref)
        fill_table(z, bins_ref, levels_ref, step, 1, table_ref)
        columns = jnp.transpose(table_ref[...])
        for k in range(z.bins):
            columns_ref[k] = jnp.broadcast_to(columns[:, k : k + 1], (z.pos, LANES))

        @pl.loop(0, 1 + 2 * z.halo)
        def _(span, band_ref=band_ref):
            inner = lane + span * LANES
            index = tap_index(z, inner // z.side, inner % z.side, row // z.side, row % z.side)
            for part in range(2):
                taps = [spread(taps_ref, part * z.bins + k, index) for k in range(z.bins)]
                place = pl.multiple_of(part * z.window + span * LANES, LANES)
                for tile in range(z.tiles):
                    total = 0.0
                    for k in range(z.bins):
                        total = total + taps[k] * columns_ref[k, tile * LANES : (tile + 1) * LANES, :]
                    band_ref[tile, :, pl.ds(place, LANES)] = total.astype(jnp.bfloat16)

    width = 2 * z.rows
    offset = lax.axis_index("wide") * z.rows
    receiver = lax.broadcasted_iota(jnp.int32, (z.blocks, width), 1) % z.rows + offset
    pick = (receiver // z.blk == lax.broadcasted_iota(jnp.int32, (z.blocks, width), 0)).astype(jnp.float32)
    keep_ref[...] = jnp.dot(aperture_ref[0].astype(jnp.float32), pick, preferred_element_type=jnp.float32)


def prepare_last_kernel(
    z,
    filt_hbm,
    bins_hbm,
    levels_hbm,
    aperture_hbm,
    fourth_ref,
    keep_ref,
    filt_ref,
    bins_ref,
    levels_ref,
    aperture_ref,
    taps_ref,
    table_ref,
    sems,
):
    copies = fetch(
        [(filt_hbm, filt_ref), (bins_hbm, bins_ref), (levels_hbm, levels_ref), (aperture_hbm, aperture_ref)],
        sems,
    )
    for copy in copies:
        copy.wait()
    fill_taps(z, filt_ref, 1, taps_ref)
    fill_table(z, bins_ref, levels_ref, 1, 0, table_ref)
    lane = lax.broadcasted_iota(jnp.int32, (z.rows, LANES), 1)
    row = lax.broadcasted_iota(jnp.int32, (z.rows, LANES), 0)

    @pl.loop(0, z.window // z.rows)
    def _(block):
        inner = row + block * z.rows
        index = tap_index(z, inner // z.side, inner % z.side, lane // z.side, lane % z.side)
        for part in range(2):
            taps = [spread(taps_ref, part * z.bins + k, index) for k in range(z.bins)]
            place = pl.multiple_of((2 * block + part) * z.rows, z.rows)
            for tile in range(z.tiles):
                total = 0.0
                for k in range(z.bins):
                    total = total + taps[k] * table_ref[k : k + 1, tile * LANES : (tile + 1) * LANES]
                total = total if part == 0 else -total
                fourth_ref[tile, pl.ds(place, z.rows), :] = total.astype(jnp.bfloat16)

    offset = lax.axis_index("wide") * z.rows
    source = lax.broadcasted_iota(jnp.int32, (z.rows, z.blocks), 0) + offset
    pick = (source // z.blk == lax.broadcasted_iota(jnp.int32, (z.rows, z.blocks), 1)).astype(jnp.float32)
    mine = jnp.dot(pick, aperture_ref[1].astype(jnp.float32), preferred_element_type=jnp.float32)
    receiver = lax.broadcasted_iota(jnp.int32, (z.blocks, z.pos), 1)
    stretch = (receiver // z.blk == lax.broadcasted_iota(jnp.int32, (z.blocks, z.pos), 0)).astype(jnp.float32)
    keep_ref[...] = jnp.dot(mine, stretch, preferred_element_type=jnp.float32)


def turned(z, block):
    return jnp.concatenate([-block[:, z.rows :], block[:, : z.rows]], axis=1)


def over_sources(z, band_ref, straight_ref, turned_ref, tile):
    start = tile * LANES
    rhs = jnp.concatenate(
        [straight_ref[start : start + z.window, :], turned_ref[start : start + z.window, :]], axis=0
    )
    return jnp.dot(band_ref[tile], rhs, preferred_element_type=jnp.float32)


def middle_kernel(
    z,
    moved_ref,
    second_ref,
    third_ref,
    keep_ref,
    out_hbm,
    shallow_hbm,
    straight_ref,
    turned_ref,
    straight2_ref,
    turned2_ref,
    out_ref,
    out_sems,
    shallow_sem,
):
    pad = z.halo * LANES
    width = 2 * z.rows
    for ref in (straight_ref, turned_ref, straight2_ref, turned2_ref):
        ref[:pad, :] = jnp.zeros((pad, width), jnp.bfloat16)
        ref[pad + z.pos :, :] = jnp.zeros((pad, width), jnp.bfloat16)
    field = moved_ref[...].reshape(z.pos, width)
    straight_ref[pad : pad + z.pos, :] = field
    turned_ref[pad : pad + z.pos, :] = turned(z, field)
    per_tile = LANES // z.blk
    for tile in range(z.tiles):
        place = slice(pad + tile * LANES, pad + (tile + 1) * LANES)
        mask = keep_ref[tile * per_tile : (tile + 1) * per_tile, :]
        mask = jnp.broadcast_to(mask[:, None, :], (per_tile, z.blk, width)).reshape(LANES, width)
        shallow = over_sources(z, second_ref, straight_ref, turned_ref, tile) * mask
        shallow = shallow.astype(jnp.bfloat16)
        straight2_ref[place, :] = shallow
        turned2_ref[place, :] = turned(z, shallow)
    shallow_copy = pltpu.make_async_copy(
        straight2_ref.at[pl.ds(pad, z.pos)], shallow_hbm, shallow_sem.at[0]
    )
    shallow_copy.start()
    chunks = LANES // z.rows
    for tile in range(z.tiles):
        third = over_sources(z, third_ref, straight2_ref, turned2_ref, tile).astype(jnp.bfloat16)
        out_ref[tile * chunks : (tile + 1) * chunks] = third.reshape(chunks, z.rows, width)
        send_out(z, out_ref, out_hbm, out_sems, tile)
    for tile in range(z.tiles):
        sent(z, out_ref, out_hbm, out_sems, tile).wait()
    shallow_copy.wait()


def split_sum(z, real_ref, send_ref, own_ref):
    me = lax.axis_index("freq")
    width = z.pos // z.freq

    def part(shift):
        start = lax.rem(me + shift, z.freq) * width
        return real_ref[:, pl.ds(pl.multiple_of(start, width), width)]

    own_ref[...] = part(0).astype(jnp.float32)
    for shift in range(1, z.freq):
        send_ref[shift - 1] = part(shift)


def turn_kernel(z, shallow_hbm, send_ref, own_ref, shallow_ref, real_ref, sems):
    for copy in fetch([(shallow_hbm, shallow_ref)], sems):
        copy.wait()
    for tile in range(z.tiles):
        columns = slice(tile * LANES, (tile + 1) * LANES)
        flipped = jnp.transpose(shallow_ref[columns, :].astype(jnp.float32))
        real_ref[:, columns] = flipped[: z.rows].astype(jnp.bfloat16)
    split_sum(z, real_ref, send_ref, own_ref)


def last_kernel(z, shifts, field_ref, fourth_ref, keep_ref, out_ref, lhs_ref):
    pad = 2 * z.halo * LANES
    width = 2 * z.rows
    lhs_ref[:, :pad] = jnp.zeros((z.rows, pad), jnp.bfloat16)
    lhs_ref[:, pad + 2 * z.pos :] = jnp.zeros((z.rows, pad), jnp.bfloat16)
    for source in range(z.wide):
        lhs_ref[:, pad + source * width : pad + (source + 1) * width] = field_ref[source]
    me = lax.axis_index("freq")
    tiles = z.tiles // z.freq
    for i, shift in enumerate(shifts):
        for j in range(tiles):
            tile = lax.rem(me + shift, z.freq) * tiles + j
            window = pl.ds(pl.multiple_of(2 * tile * LANES, 2 * LANES), 2 * z.window)
            columns = pl.ds(pl.multiple_of(tile * LANES, LANES), LANES)
            fourth = jnp.dot(lhs_ref[:, window], fourth_ref[tile], preferred_element_type=jnp.float32)
            out_ref[i, :, j * LANES : (j + 1) * LANES] = (fourth * keep_ref[:, columns]).astype(out_ref.dtype)


def call(kernel, operands, outs, scratch, flops, name, fetched=False, sent=()):
    source = pltpu.HBM if fetched else pltpu.VMEM
    spaces = [pltpu.HBM if i < len(sent) else pltpu.VMEM for i in range(len(outs))]
    scratch = [pltpu.VMEM(shape, dtype) for shape, dtype in scratch]
    if sent:
        scratch += [pltpu.VMEM(*outs[0])] + [pltpu.SemaphoreType.DMA((parts,)) for parts in sent]
    if fetched:
        scratch = [pltpu.VMEM(x.shape, x.dtype) for x in operands] + scratch
        scratch.append(pltpu.SemaphoreType.DMA((len(operands),)))
        operands = [pltpu.with_memory_space_constraint(x, pltpu.HBM) for x in operands]
    return pl.pallas_call(
        kernel,
        out_shape=[space(shape, dtype) for space, (shape, dtype) in zip(spaces, outs)],
        in_specs=[pl.BlockSpec(memory_space=source)] * len(operands),
        out_specs=[pl.BlockSpec(memory_space=space) for space in spaces],
        scratch_shapes=scratch,
        compiler_params=pltpu.CompilerParams(vmem_limit_bytes=VMEM_LIMIT),
        cost_estimate=pl.CostEstimate(flops=flops, bytes_accessed=1 << 20, transcendentals=0),
        name=name,
    )(*operands)


def freq_sum(z, send, own):
    total = own
    for shift in range(1, z.freq):
        pairs = [(source, (source + shift) % z.freq) for source in range(z.freq)]
        total = total + lax.ppermute(send[shift - 1], "freq", pairs).astype(jnp.float32)
    return total


def body(mesh, wave, filters, vel_bins, blend_levels, aperture):
    z = Sizes(mesh, wave.shape, filters.shape, aperture.shape)
    bf16, f32 = jnp.bfloat16, jnp.float32
    filters = jnp.transpose(filters, (0, 2, 3, 1, 4))
    vel_bins = jnp.transpose(vel_bins, (0, 2, 1, 3))
    blend_levels = jnp.transpose(blend_levels, (0, 2, 1, 3))
    width = 2 * z.rows
    chunks = ((z.wide, z.rows, width), bf16)
    split = z.pos // z.freq
    parts = [((z.freq - 1, z.rows, split), bf16), ((z.rows, split), f32)]
    small = [((8, LANES), f32), ((8, z.pos), f32)]
    dense = 2 * 2 * z.window * z.bins * z.pos * z.rows
    (first,) = call(
        functools.partial(first_kernel, z),
        (wave[:, 0], filters, vel_bins, blend_levels),
        [chunks],
        small
        + [
            ((2 * z.window, 2 * z.bins * LANES), bf16),
            ((z.tiles * z.rows, 2 * z.window), bf16),
        ],
        2 * dense,
        "first",
        fetched=True,
        sent=(z.tiles,),
    )
    moved = lax.all_to_all(first, "wide", 0, 0, tiled=True)
    second_band, third_band, shallow_keep = call(
        functools.partial(prepare_middle_kernel, z),
        (filters, vel_bins, blend_levels, aperture),
        [
            ((z.tiles, LANES, 2 * z.window), bf16),
            ((z.tiles, LANES, 2 * z.window), bf16),
            ((z.blocks, width), f32),
        ],
        small + [((z.bins, z.pos, LANES), f32)],
        dense,
        "prepare_middle",
        fetched=True,
    )
    padded = z.pos + 2 * z.halo * LANES
    third, shallow = call(
        functools.partial(middle_kernel, z),
        (moved, second_band, third_band, shallow_keep),
        [chunks, ((z.pos, width), bf16)],
        [((padded, width), bf16)] * 4,
        dense,
        "middle",
        sent=(z.tiles, 1),
    )
    returned = lax.all_to_all(third, "wide", 0, 0, tiled=True)
    fourth_band, deep_keep = call(
        functools.partial(prepare_last_kernel, z),
        (filters, vel_bins, blend_levels, aperture),
        [((z.tiles, 2 * z.window, LANES), bf16), ((z.rows, z.pos), f32)],
        small,
        dense,
        "prepare_last",
        fetched=True,
    )
    image_shallow = freq_sum(
        z,
        *call(
            functools.partial(turn_kernel, z),
            (shallow,),
            parts,
            [((z.rows, z.pos), bf16)],
            dense // 8,
            "turn",
            fetched=True,
        ),
    )
    returned, image_shallow, fourth_band, deep_keep = lax.optimization_barrier(
        (returned, image_shallow, fourth_band, deep_keep)
    )
    deep = []
    for shifts, part in ((range(1, z.freq), parts[0]), (range(1), ((1, z.rows, split), bf16))):
        deep += call(
            functools.partial(last_kernel, z, shifts),
            (returned, fourth_band, deep_keep),
            [part],
            [((z.rows, 2 * padded), bf16)],
            dense // 8,
            "last_own" if len(deep) else "last_send",
        )
    image_deep = freq_sum(z, deep[0], deep[1][0].astype(f32))
    return image_shallow, image_deep


def solution(mesh):
    return jax.shard_map(
        functools.partial(body, mesh),
        mesh=mesh,
        in_specs=(P(None, "freq", "wide", None), P(None, None, "freq", None, None), P(), P(), P()),
        out_specs=(P("wide", "freq"), P("wide", "freq")),
        check_vma=False,
    )
```

```python
import functools
import math

import jax
import jax.numpy as jnp
from jax import lax
from jax.experimental import pallas as pl
from jax.experimental.pallas import tpu as pltpu
from jax.sharding import PartitionSpec as P

LANES = 128
VMEM_LIMIT = 24 * 1024 * 1024


class Sizes:
    def __init__(self, mesh, wave_shape, filters_shape, aperture_shape):
        self.wide = mesh.shape["wide"]
        self.freq = mesh.shape["freq"]
        self.pos = wave_shape[-1]
        self.rows = wave_shape[-2]
        self.side = math.isqrt(self.pos)
        self.bins = filters_shape[-2]
        self.tap_count = filters_shape[-1]
        self.taps = math.isqrt(self.tap_count)
        self.half = self.taps // 2
        self.tile_rows = LANES // self.side
        self.tiles = self.pos // LANES
        self.halo = -(-self.half // self.tile_rows)
        self.window = (1 + 2 * self.halo) * LANES
        self.blocks = aperture_shape[-1]
        self.blk = self.pos // self.blocks
        self.chunks = LANES // self.rows
        start = self.wide // 2 + self.wide // 8
        self.start = start // self.chunks * self.chunks

    def place(self, index):
        return (index - self.start) % self.wide

    def exchange(self, chunks):
        order = [(self.start + i) % self.wide for i in range(self.wide)]
        return lax.all_to_all(chunks, "wide", 0, 0, axis_index_groups=[order], tiled=True)


def fill_taps(z, filt_ref, step, rows_ref):
    rows_ref[...] = jnp.zeros_like(rows_ref)
    for k in range(z.bins):
        pair = filt_ref[step, 0, k].astype(jnp.float32)
        for part in range(2):
            row = part * z.bins + k
            rows_ref[row : row + 1, : z.tap_count] = pair[part : part + 1]


def fill_table(z, bins_ref, levels_ref, step, side, table_ref):
    blend = bins_ref.shape[1]
    ids = [bins_ref[step, j, side : side + 1] for j in range(blend)]
    weights = [levels_ref[step, j, side : side + 1].astype(jnp.float32) for j in range(blend)]
    total = sum(weights[1:], weights[0])
    table_ref[...] = jnp.zeros_like(table_ref)
    for k in range(z.bins):
        hits = [jnp.where(i == k, w, 0.0) for i, w in zip(ids, weights)]
        table_ref[k : k + 1, :] = sum(hits[1:], hits[0]) / total


def tap_index(z, in_y, in_x, out_y, out_x):
    a = in_y - out_y + (z.half - z.halo * z.tile_rows)
    b = in_x - out_x + z.half
    valid = (a >= 0) & (a < z.taps) & (b >= 0) & (b < z.taps)
    return jnp.where(valid, a * z.taps + b, LANES - 1)


def spread(rows_ref, row, index):
    source = jnp.broadcast_to(rows_ref[row : row + 1, :], index.shape)
    return jnp.take_along_axis(source, index, axis=1, mode="promise_in_bounds")


def chunk_order(z, column):
    chunk, inside = column // (2 * z.rows), column % (2 * z.rows)
    return inside // z.rows, chunk * z.rows + inside % z.rows


def fetch(pairs, sems):
    copies = [pltpu.make_async_copy(source, target, sems.at[i]) for i, (source, target) in enumerate(pairs)]
    for copy in copies:
        copy.start()
    return copies


def sent(z, out_ref, out_hbm, sems, tile):
    place = pl.ds(z.place(tile * z.chunks), z.chunks)
    return pltpu.make_async_copy(out_ref.at[place], out_hbm.at[place], sems.at[tile])


def send_out(z, out_ref, out_hbm, sems, tile):
    sent(z, out_ref, out_hbm, sems, tile).start()


def first_kernel(
    z,
    wave_hbm,
    filt_hbm,
    bins_hbm,
    levels_hbm,
    out_hbm,
    wave_ref,
    filt_ref,
    bins_ref,
    levels_ref,
    taps_ref,
    table_ref,
    band_ref,
    lhs_ref,
    out_ref,
    out_sems,
    sems,
):
    copies = fetch(
        [(filt_hbm, filt_ref), (bins_hbm, bins_ref), (levels_hbm, levels_ref), (wave_hbm, wave_ref)], sems
    )
    group_rows = LANES // 2 // z.side
    window_rows = z.window // z.side
    lane = lax.broadcasted_iota(jnp.int32, (z.side, LANES), 1)
    part, point = chunk_order(z, lane)
    out_y = point // z.side - (z.half - z.halo * z.tile_rows)
    b = lax.broadcasted_iota(jnp.int32, (z.side, LANES), 0) - point % z.side + z.half
    b_valid = (b >= 0) & (b < z.taps)
    base = b - out_y * z.taps
    is_real = part == 0
    indices = []
    for y in range(window_rows - group_rows):
        valid = b_valid & (out_y <= y) & (out_y > y - z.taps)
        indices.append(jnp.where(valid, base + y * z.taps, LANES - 1))
    empty = jnp.zeros((group_rows * z.side, LANES), jnp.bfloat16)
    for k in range(z.bins):
        for half in range(2):
            top, columns = half * z.window, 2 * k * LANES
            band_ref[top + z.window - group_rows * z.side : top + z.window, columns : columns + LANES] = empty
            band_ref[top : top + group_rows * z.side, columns + LANES : columns + 2 * LANES] = empty
    copies[0].wait()
    fill_taps(z, filt_ref, 0, taps_ref)
    for k in range(z.bins):
        columns = 2 * k * LANES
        for y, index in enumerate(indices):
            real, imag = spread(taps_ref, k, index), spread(taps_ref, z.bins + k, index)
            blocks = (jnp.where(is_real, real, imag), jnp.where(is_real, -imag, real))
            for half in range(2):
                block = blocks[half].astype(jnp.bfloat16)
                top = half * z.window + y * z.side
                band_ref[top : top + z.side, columns : columns + LANES] = block
                top += group_rows * z.side
                band_ref[top : top + z.side, columns + LANES : columns + 2 * LANES] = block
    copies[1].wait()
    copies[2].wait()
    fill_table(z, bins_ref, levels_ref, 0, 0, table_ref)
    copies[3].wait()
    spans = 1 + 2 * z.halo
    for part in range(2):
        for tile in range(z.tiles):
            for span in range(spans):
                source = tile + span - z.halo
                place = (part * spans + span) * LANES
                if 0 <= source < z.tiles:
                    piece = wave_ref[part, :, source * LANES : (source + 1) * LANES]
                else:
                    piece = jnp.zeros((z.rows, LANES), jnp.bfloat16)
                lhs_ref[tile * z.rows : (tile + 1) * z.rows, place : place + LANES] = piece
    lane = lax.broadcasted_iota(jnp.int32, (8, LANES), 1)
    points = [chunk_order(z, lane + v * LANES)[1] for v in range(2)]
    products = [
        jnp.dot(
            lhs_ref[...],
            band_ref[:, 2 * k * LANES : 2 * (k + 1) * LANES],
            preferred_element_type=jnp.float32,
        )
        for k in range(z.bins)
    ]
    for tile in range(z.tiles):
        weights = table_ref[:, tile * LANES : (tile + 1) * LANES]
        weights = jnp.concatenate(
            [jnp.take_along_axis(weights, p, axis=1, mode="promise_in_bounds") for p in points], axis=1
        )
        total = 0.0
        for k in range(z.bins):
            total = total + products[k][tile * z.rows : (tile + 1) * z.rows] * weights[k : k + 1]
        total = total.astype(jnp.bfloat16)
        for c in range(z.chunks):
            out_ref[z.place(tile * z.chunks + c)] = total[:, 2 * z.rows * c : 2 * z.rows * (c + 1)]
        send_out(z, out_ref, out_hbm, out_sems, tile)
    for tile in range(z.tiles):
        sent(z, out_ref, out_hbm, out_sems, tile).wait()


def prepare_middle_kernel(
    z,
    filt_hbm,
    bins_hbm,
    levels_hbm,
    aperture_hbm,
    second_ref,
    third_ref,
    keep_ref,
    filt_ref,
    bins_ref,
    levels_ref,
    aperture_ref,
    taps_ref,
    table_ref,
    columns_ref,
    sems,
):
    copies = fetch(
        [(filt_hbm, filt_ref), (bins_hbm, bins_ref), (levels_hbm, levels_ref), (aperture_hbm, aperture_ref)],
        sems,
    )
    for copy in copies:
        copy.wait()
    lane = lax.broadcasted_iota(jnp.int32, (LANES, LANES), 1)
    row = lax.broadcasted_iota(jnp.int32, (LANES, LANES), 0)
    for step, band_ref in ((0, second_ref), (1, third_ref)):
        fill_taps(z, filt_ref, step, taps_ref)
        fill_table(z, bins_ref, levels_ref, step, 1, table_ref)
        columns = jnp.transpose(table_ref[...])
        for k in range(z.bins):
            columns_ref[k] = jnp.broadcast_to(columns[:, k : k + 1], (z.pos, LANES))

        @pl.loop(0, 1 + 2 * z.halo)
        def _(span, band_ref=band_ref):
            inner = lane + span * LANES
            index = tap_index(z, inner // z.side, inner % z.side, row // z.side, row % z.side)
            for part in range(2):
                taps = [spread(taps_ref, part * z.bins + k, index) for k in range(z.bins)]
                place = pl.multiple_of(part * z.window + span * LANES, LANES)
                for tile in range(z.tiles):
                    total = 0.0
                    for k in range(z.bins):
                        total = total + taps[k] * columns_ref[k, tile * LANES : (tile + 1) * LANES, :]
                    band_ref[tile, :, pl.ds(place, LANES)] = total.astype(jnp.bfloat16)

    width = 2 * z.rows
    offset = lax.axis_index("wide") * z.rows
    receiver = lax.broadcasted_iota(jnp.int32, (z.blocks, width), 1) % z.rows + offset
    pick = (receiver // z.blk == lax.broadcasted_iota(jnp.int32, (z.blocks, width), 0)).astype(jnp.float32)
    keep_ref[...] = jnp.dot(aperture_ref[0].astype(jnp.float32), pick, preferred_element_type=jnp.float32)


def prepare_last_kernel(
    z,
    filt_hbm,
    bins_hbm,
    levels_hbm,
    aperture_hbm,
    fourth_ref,
    keep_ref,
    filt_ref,
    bins_ref,
    levels_ref,
    aperture_ref,
    taps_ref,
    table_ref,
    sems,
):
    copies = fetch(
        [(filt_hbm, filt_ref), (bins_hbm, bins_ref), (levels_hbm, levels_ref), (aperture_hbm, aperture_ref)],
        sems,
    )
    for copy in copies:
        copy.wait()
    fill_taps(z, filt_ref, 1, taps_ref)
    fill_table(z, bins_ref, levels_ref, 1, 0, table_ref)
    lane = lax.broadcasted_iota(jnp.int32, (z.rows, LANES), 1)
    row = lax.broadcasted_iota(jnp.int32, (z.rows, LANES), 0)

    @pl.loop(0, z.window // z.rows)
    def _(block):
        inner = row + block * z.rows
        index = tap_index(z, inner // z.side, inner % z.side, lane // z.side, lane % z.side)
        for part in range(2):
            taps = [spread(taps_ref, part * z.bins + k, index) for k in range(z.bins)]
            place = pl.multiple_of((2 * block + part) * z.rows, z.rows)
            for tile in range(z.tiles):
                total = 0.0
                for k in range(z.bins):
                    total = total + taps[k] * table_ref[k : k + 1, tile * LANES : (tile + 1) * LANES]
                total = total if part == 0 else -total
                fourth_ref[tile, pl.ds(place, z.rows), :] = total.astype(jnp.bfloat16)

    offset = lax.axis_index("wide") * z.rows
    source = lax.broadcasted_iota(jnp.int32, (z.rows, z.blocks), 0) + offset
    pick = (source // z.blk == lax.broadcasted_iota(jnp.int32, (z.rows, z.blocks), 1)).astype(jnp.float32)
    mine = jnp.dot(pick, aperture_ref[1].astype(jnp.float32), preferred_element_type=jnp.float32)
    receiver = lax.broadcasted_iota(jnp.int32, (z.blocks, z.pos), 1)
    stretch = (receiver // z.blk == lax.broadcasted_iota(jnp.int32, (z.blocks, z.pos), 0)).astype(jnp.float32)
    keep_ref[...] = jnp.dot(mine, stretch, preferred_element_type=jnp.float32)


def turned(z, block):
    return jnp.concatenate([-block[:, z.rows :], block[:, : z.rows]], axis=1)


def over_sources(z, band_ref, straight_ref, turned_ref, tile):
    start = tile * LANES
    rhs = jnp.concatenate(
        [straight_ref[start : start + z.window, :], turned_ref[start : start + z.window, :]], axis=0
    )
    return jnp.dot(band_ref[tile], rhs, preferred_element_type=jnp.float32)


def middle_kernel(
    z,
    moved_ref,
    second_ref,
    third_ref,
    keep_ref,
    out_hbm,
    shallow_hbm,
    straight_ref,
    turned_ref,
    straight2_ref,
    turned2_ref,
    out_ref,
    out_sems,
    shallow_sem,
):
    pad = z.halo * LANES
    width = 2 * z.rows
    for ref in (straight_ref, turned_ref, straight2_ref, turned2_ref):
        ref[:pad, :] = jnp.zeros((pad, width), jnp.bfloat16)
        ref[pad + z.pos :, :] = jnp.zeros((pad, width), jnp.bfloat16)
    for tile in range(z.tiles):
        place = slice(pad + tile * LANES, pad + (tile + 1) * LANES)
        chunk = z.place(tile * z.chunks)
        field = moved_ref[chunk : chunk + z.chunks].reshape(LANES, width)
        straight_ref[place, :] = field
        turned_ref[place, :] = turned(z, field)
    per_tile = LANES // z.blk
    for tile in range(z.tiles):
        place = slice(pad + tile * LANES, pad + (tile + 1) * LANES)
        mask = keep_ref[tile * per_tile : (tile + 1) * per_tile, :]
        mask = jnp.broadcast_to(mask[:, None, :], (per_tile, z.blk, width)).reshape(LANES, width)
        shallow = over_sources(z, second_ref, straight_ref, turned_ref, tile) * mask
        shallow = shallow.astype(jnp.bfloat16)
        straight2_ref[place, :] = shallow
        turned2_ref[place, :] = turned(z, shallow)
    shallow_copy = pltpu.make_async_copy(
        straight2_ref.at[pl.ds(pad, z.pos)], shallow_hbm, shallow_sem.at[0]
    )
    shallow_copy.start()
    for tile in range(z.tiles):
        chunk = z.place(tile * z.chunks)
        third = over_sources(z, third_ref, straight2_ref, turned2_ref, tile).astype(jnp.bfloat16)
        out_ref[chunk : chunk + z.chunks] = third.reshape(z.chunks, z.rows, width)
        send_out(z, out_ref, out_hbm, out_sems, tile)
    for tile in range(z.tiles):
        sent(z, out_ref, out_hbm, out_sems, tile).wait()
    shallow_copy.wait()


def split_sum(z, real_ref, send_ref, own_ref):
    me = lax.axis_index("freq")
    width = z.pos // z.freq

    def part(shift):
        start = lax.rem(me + shift, z.freq) * width
        return real_ref[:, pl.ds(pl.multiple_of(start, width), width)]

    own_ref[...] = part(0).astype(jnp.float32)
    for shift in range(1, z.freq):
        send_ref[shift - 1] = part(shift)


def turn_kernel(z, shallow_hbm, send_ref, own_ref, shallow_ref, real_ref, sems):
    for copy in fetch([(shallow_hbm, shallow_ref)], sems):
        copy.wait()
    for tile in range(z.tiles):
        columns = slice(tile * LANES, (tile + 1) * LANES)
        flipped = jnp.transpose(shallow_ref[columns, :].astype(jnp.float32))
        real_ref[:, columns] = flipped[: z.rows].astype(jnp.bfloat16)
    split_sum(z, real_ref, send_ref, own_ref)


def last_kernel(z, shifts, field_ref, fourth_ref, keep_ref, out_ref, lhs_ref):
    pad = 2 * z.halo * LANES
    width = 2 * z.rows
    lhs_ref[:, :pad] = jnp.zeros((z.rows, pad), jnp.bfloat16)
    lhs_ref[:, pad + 2 * z.pos :] = jnp.zeros((z.rows, pad), jnp.bfloat16)
    for source in range(z.wide):
        lhs_ref[:, pad + source * width : pad + (source + 1) * width] = field_ref[z.place(source)]
    me = lax.axis_index("freq")
    tiles = z.tiles // z.freq
    for i, shift in enumerate(shifts):
        for j in range(tiles):
            tile = lax.rem(me + shift, z.freq) * tiles + j
            window = pl.ds(pl.multiple_of(2 * tile * LANES, 2 * LANES), 2 * z.window)
            columns = pl.ds(pl.multiple_of(tile * LANES, LANES), LANES)
            fourth = jnp.dot(lhs_ref[:, window], fourth_ref[tile], preferred_element_type=jnp.float32)
            out_ref[i, :, j * LANES : (j + 1) * LANES] = (fourth * keep_ref[:, columns]).astype(out_ref.dtype)


def call(kernel, operands, outs, scratch, flops, name, fetched=False, sent=()):
    source = pltpu.HBM if fetched else pltpu.VMEM
    spaces = [pltpu.HBM if i < len(sent) else pltpu.VMEM for i in range(len(outs))]
    scratch = [pltpu.VMEM(shape, dtype) for shape, dtype in scratch]
    if sent:
        scratch += [pltpu.VMEM(*outs[0])] + [pltpu.SemaphoreType.DMA((parts,)) for parts in sent]
    if fetched:
        scratch = [pltpu.VMEM(x.shape, x.dtype) for x in operands] + scratch
        scratch.append(pltpu.SemaphoreType.DMA((len(operands),)))
        operands = [pltpu.with_memory_space_constraint(x, pltpu.HBM) for x in operands]
    return pl.pallas_call(
        kernel,
        out_shape=[space(shape, dtype) for space, (shape, dtype) in zip(spaces, outs)],
        in_specs=[pl.BlockSpec(memory_space=source)] * len(operands),
        out_specs=[pl.BlockSpec(memory_space=space) for space in spaces],
        scratch_shapes=scratch,
        compiler_params=pltpu.CompilerParams(vmem_limit_bytes=VMEM_LIMIT),
        cost_estimate=pl.CostEstimate(flops=flops, bytes_accessed=1 << 20, transcendentals=0),
        name=name,
    )(*operands)


def freq_sum(z, send, own):
    total = own
    for shift in range(1, z.freq):
        pairs = [(source, (source + shift) % z.freq) for source in range(z.freq)]
        total = total + lax.ppermute(send[shift - 1], "freq", pairs).astype(jnp.float32)
    return total


def body(mesh, wave, filters, vel_bins, blend_levels, aperture):
    z = Sizes(mesh, wave.shape, filters.shape, aperture.shape)
    bf16, f32 = jnp.bfloat16, jnp.float32
    filters = jnp.transpose(filters, (0, 2, 3, 1, 4))
    vel_bins = jnp.transpose(vel_bins, (0, 2, 1, 3))
    blend_levels = jnp.transpose(blend_levels, (0, 2, 1, 3))
    width = 2 * z.rows
    chunks = ((z.wide, z.rows, width), bf16)
    split = z.pos // z.freq
    parts = [((z.freq - 1, z.rows, split), bf16), ((z.rows, split), f32)]
    small = [((8, LANES), f32), ((8, z.pos), f32)]
    dense = 2 * 2 * z.window * z.bins * z.pos * z.rows
    (first,) = call(
        functools.partial(first_kernel, z),
        (wave[:, 0], filters, vel_bins, blend_levels),
        [chunks],
        small
        + [
            ((2 * z.window, 2 * z.bins * LANES), bf16),
            ((z.tiles * z.rows, 2 * z.window), bf16),
        ],
        2 * dense,
        "first",
        fetched=True,
        sent=(z.tiles,),
    )
    moved = z.exchange(first)
    second_band, third_band, shallow_keep = call(
        functools.partial(prepare_middle_kernel, z),
        (filters, vel_bins, blend_levels, aperture),
        [
            ((z.tiles, LANES, 2 * z.window), bf16),
            ((z.tiles, LANES, 2 * z.window), bf16),
            ((z.blocks, width), f32),
        ],
        small + [((z.bins, z.pos, LANES), f32)],
        dense,
        "prepare_middle",
        fetched=True,
    )
    padded = z.pos + 2 * z.halo * LANES
    third, shallow = call(
        functools.partial(middle_kernel, z),
        (moved, second_band, third_band, shallow_keep),
        [chunks, ((z.pos, width), bf16)],
        [((padded, width), bf16)] * 4,
        dense,
        "middle",
        sent=(z.tiles, 1),
    )
    returned = z.exchange(third)
    fourth_band, deep_keep = call(
        functools.partial(prepare_last_kernel, z),
        (filters, vel_bins, blend_levels, aperture),
        [((z.tiles, 2 * z.window, LANES), bf16), ((z.rows, z.pos), f32)],
        small,
        dense,
        "prepare_last",
        fetched=True,
    )
    image_shallow = freq_sum(
        z,
        *call(
            functools.partial(turn_kernel, z),
            (shallow,),
            parts,
            [((z.rows, z.pos), bf16)],
            dense // 8,
            "turn",
            fetched=True,
        ),
    )
    returned, image_shallow, fourth_band, deep_keep = lax.optimization_barrier(
        (returned, image_shallow, fourth_band, deep_keep)
    )
    deep = []
    for shifts, part in ((range(1, z.freq), parts[0]), (range(1), ((1, z.rows, split), bf16))):
        deep += call(
            functools.partial(last_kernel, z, shifts),
            (returned, fourth_band, deep_keep),
            [part],
            [((z.rows, 2 * padded), bf16)],
            dense // 8,
            "last_own" if len(deep) else "last_send",
        )
    image_deep = freq_sum(z, deep[0], deep[1][0].astype(f32))
    return image_shallow, image_deep


def solution(mesh):
    return jax.shard_map(
        functools.partial(body, mesh),
        mesh=mesh,
        in_specs=(P(None, "freq", "wide", None), P(None, None, "freq", None, None), P(), P(), P()),
        out_specs=(P("wide", "freq"), P("wide", "freq")),
        check_vma=False,
    )
```

```python
import functools
import math

import jax
import jax.numpy as jnp
from jax import lax
from jax.experimental import pallas as pl
from jax.experimental.pallas import tpu as pltpu
from jax.sharding import PartitionSpec as P

LANES = 128
VMEM_LIMIT = 24 * 1024 * 1024


class Sizes:
    def __init__(self, mesh, wave_shape, filters_shape, aperture_shape):
        self.wide = mesh.shape["wide"]
        self.freq = mesh.shape["freq"]
        self.pos = wave_shape[-1]
        self.rows = wave_shape[-2]
        self.side = math.isqrt(self.pos)
        self.bins = filters_shape[-2]
        self.tap_count = filters_shape[-1]
        self.taps = math.isqrt(self.tap_count)
        self.half = self.taps // 2
        self.tile_rows = LANES // self.side
        self.tiles = self.pos // LANES
        self.halo = -(-self.half // self.tile_rows)
        self.window = (1 + 2 * self.halo) * LANES
        self.blocks = aperture_shape[-1]
        self.blk = self.pos // self.blocks
        self.chunks = LANES // self.rows
        start = self.wide // 2 + self.wide // 8
        self.start = start // self.chunks * self.chunks

    def place(self, index):
        return (index - self.start) % self.wide

    def exchange(self, chunks):
        order = [(self.start + i) % self.wide for i in range(self.wide)]
        return lax.all_to_all(chunks, "wide", 0, 0, axis_index_groups=[order], tiled=True)


def fill_taps(z, filt_ref, step, rows_ref):
    rows_ref[...] = jnp.zeros_like(rows_ref)
    for k in range(z.bins):
        pair = filt_ref[step, 0, k].astype(jnp.float32)
        for part in range(2):
            row = part * z.bins + k
            rows_ref[row : row + 1, : z.tap_count] = pair[part : part + 1]


def fill_table(z, bins_ref, levels_ref, step, side, table_ref):
    blend = bins_ref.shape[1]
    ids = [bins_ref[step, j, side : side + 1] for j in range(blend)]
    weights = [levels_ref[step, j, side : side + 1].astype(jnp.float32) for j in range(blend)]
    total = sum(weights[1:], weights[0])
    table_ref[...] = jnp.zeros_like(table_ref)
    for k in range(z.bins):
        hits = [jnp.where(i == k, w, 0.0) for i, w in zip(ids, weights)]
        table_ref[k : k + 1, :] = sum(hits[1:], hits[0]) / total


def tap_index(z, in_y, in_x, out_y, out_x):
    a = in_y - out_y + (z.half - z.halo * z.tile_rows)
    b = in_x - out_x + z.half
    valid = (a >= 0) & (a < z.taps) & (b >= 0) & (b < z.taps)
    return jnp.where(valid, a * z.taps + b, LANES - 1)


def spread(rows_ref, row, index):
    source = jnp.broadcast_to(rows_ref[row : row + 1, :], index.shape)
    return jnp.take_along_axis(source, index, axis=1, mode="promise_in_bounds")


def chunk_order(z, column):
    chunk, inside = column // (2 * z.rows), column % (2 * z.rows)
    return inside // z.rows, chunk * z.rows + inside % z.rows


def fetch(pairs, sems):
    copies = [pltpu.make_async_copy(source, target, sems.at[i]) for i, (source, target) in enumerate(pairs)]
    for copy in copies:
        copy.start()
    return copies


def sent(z, out_ref, out_hbm, sems, tile):
    place = pl.ds(z.place(tile * z.chunks), z.chunks)
    return pltpu.make_async_copy(out_ref.at[place], out_hbm.at[place], sems.at[tile])


def send_out(z, out_ref, out_hbm, sems, tile):
    sent(z, out_ref, out_hbm, sems, tile).start()


def first_kernel(
    z,
    wave_hbm,
    filt_hbm,
    bins_hbm,
    levels_hbm,
    out_hbm,
    wave_ref,
    filt_ref,
    bins_ref,
    levels_ref,
    taps_ref,
    table_ref,
    band_ref,
    lhs_ref,
    acc_ref,
    out_ref,
    out_sems,
    sems,
):
    copies = fetch(
        [(filt_hbm, filt_ref), (bins_hbm, bins_ref), (levels_hbm, levels_ref), (wave_hbm, wave_ref)], sems
    )
    group_rows = LANES // 2 // z.side
    window_rows = z.window // z.side
    lane = lax.broadcasted_iota(jnp.int32, (z.side, LANES), 1)
    part, point = chunk_order(z, lane)
    out_y = point // z.side - (z.half - z.halo * z.tile_rows)
    b = lax.broadcasted_iota(jnp.int32, (z.side, LANES), 0) - point % z.side + z.half
    b_valid = (b >= 0) & (b < z.taps)
    base = b - out_y * z.taps
    is_real = part == 0
    indices = []
    for y in range(window_rows - group_rows):
        valid = b_valid & (out_y <= y) & (out_y > y - z.taps)
        indices.append(jnp.where(valid, base + y * z.taps, LANES - 1))
    empty = jnp.zeros((group_rows * z.side, LANES), jnp.bfloat16)
    for k in range(z.bins):
        for half in range(2):
            top, columns = half * z.window, 2 * k * LANES
            band_ref[top + z.window - group_rows * z.side : top + z.window, columns : columns + LANES] = empty
            band_ref[top : top + group_rows * z.side, columns + LANES : columns + 2 * LANES] = empty
    copies[0].wait()
    fill_taps(z, filt_ref, 0, taps_ref)
    for k in range(z.bins):
        columns = 2 * k * LANES
        for y, index in enumerate(indices):
            real, imag = spread(taps_ref, k, index), spread(taps_ref, z.bins + k, index)
            blocks = (jnp.where(is_real, real, imag), jnp.where(is_real, -imag, real))
            for half in range(2):
                block = blocks[half].astype(jnp.bfloat16)
                top = half * z.window + y * z.side
                band_ref[top : top + z.side, columns : columns + LANES] = block
                top += group_rows * z.side
                band_ref[top : top + z.side, columns + LANES : columns + 2 * LANES] = block
    copies[1].wait()
    copies[2].wait()
    fill_table(z, bins_ref, levels_ref, 0, 0, table_ref)
    copies[3].wait()
    spans = 1 + 2 * z.halo
    for part in range(2):
        for tile in range(z.tiles):
            for span in range(spans):
                source = tile + span - z.halo
                place = (part * spans + span) * LANES
                if 0 <= source < z.tiles:
                    piece = wave_ref[part, :, source * LANES : (source + 1) * LANES]
                else:
                    piece = jnp.zeros((z.rows, LANES), jnp.bfloat16)
                lhs_ref[tile * z.rows : (tile + 1) * z.rows, place : place + LANES] = piece
    lane = lax.broadcasted_iota(jnp.int32, (8, LANES), 1)
    points = [chunk_order(z, lane + v * LANES)[1] for v in range(2)]
    columns = []
    for tile in range(z.tiles):
        weights = table_ref[:, tile * LANES : (tile + 1) * LANES]
        picked = [jnp.take_along_axis(weights, p, axis=1, mode="promise_in_bounds") for p in points]
        columns.append(jnp.concatenate(picked, axis=1))
    for k in range(z.bins):
        product = jnp.dot(
            lhs_ref[...],
            band_ref[:, 2 * k * LANES : 2 * (k + 1) * LANES],
            preferred_element_type=jnp.float32,
        )
        for tile in range(z.tiles):
            rows = slice(tile * z.rows, (tile + 1) * z.rows)
            part = product[rows] * columns[tile][k : k + 1]
            if k:
                part = part + acc_ref[rows, :]
            if k < z.bins - 1:
                acc_ref[rows, :] = part
            else:
                total = part.astype(jnp.bfloat16)
                for c in range(z.chunks):
                    out_ref[z.place(tile * z.chunks + c)] = total[:, 2 * z.rows * c : 2 * z.rows * (c + 1)]
                send_out(z, out_ref, out_hbm, out_sems, tile)
    for tile in range(z.tiles):
        sent(z, out_ref, out_hbm, out_sems, tile).wait()


def prepare_middle_kernel(
    z,
    filt_hbm,
    bins_hbm,
    levels_hbm,
    aperture_hbm,
    second_ref,
    third_ref,
    keep_ref,
    filt_ref,
    bins_ref,
    levels_ref,
    aperture_ref,
    taps_ref,
    table_ref,
    columns_ref,
    sems,
):
    copies = fetch(
        [(filt_hbm, filt_ref), (bins_hbm, bins_ref), (levels_hbm, levels_ref), (aperture_hbm, aperture_ref)],
        sems,
    )
    for copy in copies:
        copy.wait()
    lane = lax.broadcasted_iota(jnp.int32, (LANES, LANES), 1)
    row = lax.broadcasted_iota(jnp.int32, (LANES, LANES), 0)
    for step, band_ref in ((0, second_ref), (1, third_ref)):
        fill_taps(z, filt_ref, step, taps_ref)
        fill_table(z, bins_ref, levels_ref, step, 1, table_ref)
        columns = jnp.transpose(table_ref[...])
        for k in range(z.bins):
            columns_ref[k] = jnp.broadcast_to(columns[:, k : k + 1], (z.pos, LANES))

        @pl.loop(0, 1 + 2 * z.halo)
        def _(span, band_ref=band_ref):
            inner = lane + span * LANES
            index = tap_index(z, inner // z.side, inner % z.side, row // z.side, row % z.side)
            for part in range(2):
                taps = [spread(taps_ref, part * z.bins + k, index) for k in range(z.bins)]
                place = pl.multiple_of(part * z.window + span * LANES, LANES)
                for tile in range(z.tiles):
                    total = 0.0
                    for k in range(z.bins):
                        total = total + taps[k] * columns_ref[k, tile * LANES : (tile + 1) * LANES, :]
                    band_ref[tile, :, pl.ds(place, LANES)] = total.astype(jnp.bfloat16)

    width = 2 * z.rows
    offset = lax.axis_index("wide") * z.rows
    receiver = lax.broadcasted_iota(jnp.int32, (z.blocks, width), 1) % z.rows + offset
    pick = (receiver // z.blk == lax.broadcasted_iota(jnp.int32, (z.blocks, width), 0)).astype(jnp.float32)
    keep_ref[...] = jnp.dot(aperture_ref[0].astype(jnp.float32), pick, preferred_element_type=jnp.float32)


def prepare_last_kernel(
    z,
    filt_hbm,
    bins_hbm,
    levels_hbm,
    aperture_hbm,
    fourth_ref,
    keep_ref,
    filt_ref,
    bins_ref,
    levels_ref,
    aperture_ref,
    taps_ref,
    table_ref,
    sems,
):
    copies = fetch(
        [(filt_hbm, filt_ref), (bins_hbm, bins_ref), (levels_hbm, levels_ref), (aperture_hbm, aperture_ref)],
        sems,
    )
    for copy in copies:
        copy.wait()
    fill_taps(z, filt_ref, 1, taps_ref)
    fill_table(z, bins_ref, levels_ref, 1, 0, table_ref)
    lane = lax.broadcasted_iota(jnp.int32, (z.rows, LANES), 1)
    row = lax.broadcasted_iota(jnp.int32, (z.rows, LANES), 0)

    @pl.loop(0, z.window // z.rows)
    def _(block):
        inner = row + block * z.rows
        index = tap_index(z, inner // z.side, inner % z.side, lane // z.side, lane % z.side)
        for part in range(2):
            taps = [spread(taps_ref, part * z.bins + k, index) for k in range(z.bins)]
            place = pl.multiple_of((2 * block + part) * z.rows, z.rows)
            for tile in range(z.tiles):
                total = 0.0
                for k in range(z.bins):
                    total = total + taps[k] * table_ref[k : k + 1, tile * LANES : (tile + 1) * LANES]
                total = total if part == 0 else -total
                if tile < z.halo:
                    total = jnp.where(block * z.rows >= (z.halo - tile) * LANES, total, 0.0)
                if tile >= z.tiles - z.halo:
                    total = jnp.where(block * z.rows < (z.tiles + z.halo - tile) * LANES, total, 0.0)
                fourth_ref[tile, pl.ds(place, z.rows), :] = total.astype(jnp.bfloat16)

    offset = lax.axis_index("wide") * z.rows
    source = lax.broadcasted_iota(jnp.int32, (z.rows, z.blocks), 0) + offset
    pick = (source // z.blk == lax.broadcasted_iota(jnp.int32, (z.rows, z.blocks), 1)).astype(jnp.float32)
    mine = jnp.dot(pick, aperture_ref[1].astype(jnp.float32), preferred_element_type=jnp.float32)
    receiver = lax.broadcasted_iota(jnp.int32, (z.blocks, z.pos), 1)
    stretch = (receiver // z.blk == lax.broadcasted_iota(jnp.int32, (z.blocks, z.pos), 0)).astype(jnp.float32)
    keep_ref[...] = jnp.dot(mine, stretch, preferred_element_type=jnp.float32)


def turned(z, block):
    return jnp.concatenate([-block[:, z.rows :], block[:, : z.rows]], axis=1)


def over_sources(z, band_ref, straight, turn, tile):
    low, high = max(tile - z.halo, 0), min(tile + z.halo, z.tiles - 1)
    reach = range(low, high + 1)
    rhs = jnp.concatenate([straight(j) for j in reach] + [turn(j) for j in reach], axis=0)
    width = len(reach) * LANES
    starts = [part * z.window + (low - tile + z.halo) * LANES for part in range(2)]
    band = jnp.concatenate([band_ref[tile, :, start : start + width] for start in starts], axis=1)
    return jnp.dot(band, rhs, preferred_element_type=jnp.float32)


def middle_kernel(
    z,
    moved_ref,
    second_ref,
    third_ref,
    keep_ref,
    out_hbm,
    shallow_hbm,
    turned_ref,
    straight2_ref,
    turned2_ref,
    out_ref,
    out_sems,
    shallow_sem,
):
    width = 2 * z.rows

    def field(tile):
        chunk = z.place(tile * z.chunks)
        return moved_ref[chunk : chunk + z.chunks].reshape(LANES, width)

    for tile in range(z.tiles):
        turned_ref[tile] = turned(z, field(tile))
    per_tile = LANES // z.blk
    for tile in range(z.tiles):
        mask = keep_ref[tile * per_tile : (tile + 1) * per_tile, :]
        mask = jnp.broadcast_to(mask[:, None, :], (per_tile, z.blk, width)).reshape(LANES, width)
        shallow = over_sources(z, second_ref, field, lambda j: turned_ref[j], tile) * mask
        shallow = shallow.astype(jnp.bfloat16)
        straight2_ref[tile * LANES : (tile + 1) * LANES, :] = shallow
        turned2_ref[tile] = turned(z, shallow)
    shallow_copy = pltpu.make_async_copy(straight2_ref, shallow_hbm, shallow_sem.at[0])
    shallow_copy.start()
    for tile in range(z.tiles):
        chunk = z.place(tile * z.chunks)
        third = over_sources(
            z, third_ref, lambda j: straight2_ref[j * LANES : (j + 1) * LANES, :], lambda j: turned2_ref[j], tile
        ).astype(jnp.bfloat16)
        out_ref[chunk : chunk + z.chunks] = third.reshape(z.chunks, z.rows, width)
        send_out(z, out_ref, out_hbm, out_sems, tile)
    for tile in range(z.tiles):
        sent(z, out_ref, out_hbm, out_sems, tile).wait()
    shallow_copy.wait()


def split_sum(z, real_ref, send_ref, own_ref):
    me = lax.axis_index("freq")
    width = z.pos // z.freq

    def part(shift):
        start = lax.rem(me + shift, z.freq) * width
        return real_ref[:, pl.ds(pl.multiple_of(start, width), width)]

    own_ref[...] = part(0).astype(jnp.float32)
    for shift in range(1, z.freq):
        send_ref[shift - 1] = part(shift)


def turn_kernel(z, shallow_hbm, send_ref, own_ref, shallow_ref, real_ref, sems):
    for copy in fetch([(shallow_hbm, shallow_ref)], sems):
        copy.wait()
    for tile in range(z.tiles):
        columns = slice(tile * LANES, (tile + 1) * LANES)
        flipped = jnp.transpose(shallow_ref[columns, :].astype(jnp.float32))
        real_ref[:, columns] = flipped[: z.rows].astype(jnp.bfloat16)
    split_sum(z, real_ref, send_ref, own_ref)


def last_kernel(z, shifts, field_ref, fourth_ref, keep_ref, out_ref):
    me = lax.axis_index("freq")
    tiles = z.tiles // z.freq
    for i, shift in enumerate(shifts):
        for j in range(tiles):
            tile = lax.rem(me + shift, z.freq) * tiles + j
            first = (tile - z.halo) * z.chunks - z.start + 2 * z.wide
            pieces = [field_ref[lax.rem(first + c, z.wide)] for c in range((1 + 2 * z.halo) * z.chunks)]
            columns = pl.ds(pl.multiple_of(tile * LANES, LANES), LANES)
            fourth = jnp.dot(
                jnp.concatenate(pieces, axis=1), fourth_ref[tile], preferred_element_type=jnp.float32
            )
            out_ref[i, :, j * LANES : (j + 1) * LANES] = (fourth * keep_ref[:, columns]).astype(out_ref.dtype)


def call(kernel, operands, outs, scratch, flops, name, fetched=False, sent=()):
    source = pltpu.HBM if fetched else pltpu.VMEM
    spaces = [pltpu.HBM if i < len(sent) else pltpu.VMEM for i in range(len(outs))]
    scratch = [pltpu.VMEM(shape, dtype) for shape, dtype in scratch]
    if sent:
        scratch += [pltpu.VMEM(*outs[0])] + [pltpu.SemaphoreType.DMA((parts,)) for parts in sent]
    if fetched:
        scratch = [pltpu.VMEM(x.shape, x.dtype) for x in operands] + scratch
        scratch.append(pltpu.SemaphoreType.DMA((len(operands),)))
        operands = [pltpu.with_memory_space_constraint(x, pltpu.HBM) for x in operands]
    return pl.pallas_call(
        kernel,
        out_shape=[space(shape, dtype) for space, (shape, dtype) in zip(spaces, outs)],
        in_specs=[pl.BlockSpec(memory_space=source)] * len(operands),
        out_specs=[pl.BlockSpec(memory_space=space) for space in spaces],
        scratch_shapes=scratch,
        compiler_params=pltpu.CompilerParams(vmem_limit_bytes=VMEM_LIMIT),
        cost_estimate=pl.CostEstimate(flops=flops, bytes_accessed=1 << 20, transcendentals=0),
        name=name,
    )(*operands)


def freq_sum(z, send, own):
    total = own
    for shift in range(1, z.freq):
        pairs = [(source, (source + shift) % z.freq) for source in range(z.freq)]
        total = total + lax.ppermute(send[shift - 1], "freq", pairs).astype(jnp.float32)
    return total


def body(mesh, wave, filters, vel_bins, blend_levels, aperture):
    z = Sizes(mesh, wave.shape, filters.shape, aperture.shape)
    bf16, f32 = jnp.bfloat16, jnp.float32
    filters = jnp.transpose(filters, (0, 2, 3, 1, 4))
    vel_bins = jnp.transpose(vel_bins, (0, 2, 1, 3))
    blend_levels = jnp.transpose(blend_levels, (0, 2, 1, 3))
    width = 2 * z.rows
    chunks = ((z.wide, z.rows, width), bf16)
    split = z.pos // z.freq
    parts = [((z.freq - 1, z.rows, split), bf16), ((z.rows, split), f32)]
    small = [((8, LANES), f32), ((8, z.pos), f32)]
    dense = 2 * 2 * z.window * z.bins * z.pos * z.rows
    (first,) = call(
        functools.partial(first_kernel, z),
        (wave[:, 0], filters, vel_bins, blend_levels),
        [chunks],
        small
        + [
            ((2 * z.window, 2 * z.bins * LANES), bf16),
            ((z.tiles * z.rows, 2 * z.window), bf16),
            ((z.tiles * z.rows, 2 * LANES), f32),
        ],
        2 * dense,
        "first",
        fetched=True,
        sent=(z.tiles,),
    )
    moved = z.exchange(first)
    second_band, third_band, shallow_keep = call(
        functools.partial(prepare_middle_kernel, z),
        (filters, vel_bins, blend_levels, aperture),
        [
            ((z.tiles, LANES, 2 * z.window), bf16),
            ((z.tiles, LANES, 2 * z.window), bf16),
            ((z.blocks, width), f32),
        ],
        small + [((z.bins, z.pos, LANES), f32)],
        dense,
        "prepare_middle",
        fetched=True,
    )
    third, shallow = call(
        functools.partial(middle_kernel, z),
        (moved, second_band, third_band, shallow_keep),
        [chunks, ((z.pos, width), bf16)],
        [((z.tiles, LANES, width), bf16), ((z.pos, width), bf16), ((z.tiles, LANES, width), bf16)],
        dense,
        "middle",
        sent=(z.tiles, 1),
    )
    returned = z.exchange(third)
    fourth_band, deep_keep = call(
        functools.partial(prepare_last_kernel, z),
        (filters, vel_bins, blend_levels, aperture),
        [((z.tiles, 2 * z.window, LANES), bf16), ((z.rows, z.pos), f32)],
        small,
        dense,
        "prepare_last",
        fetched=True,
    )
    image_shallow = freq_sum(
        z,
        *call(
            functools.partial(turn_kernel, z),
            (shallow,),
            parts,
            [((z.rows, z.pos), bf16)],
            dense // 8,
            "turn",
            fetched=True,
        ),
    )
    returned, image_shallow, fourth_band, deep_keep = lax.optimization_barrier(
        (returned, image_shallow, fourth_band, deep_keep)
    )
    deep = []
    for shifts, part in ((range(1, z.freq), parts[0]), (range(1), ((1, z.rows, split), bf16))):
        deep += call(
            functools.partial(last_kernel, z, shifts),
            (returned, fourth_band, deep_keep),
            [part],
            [],
            dense // 8,
            "last_own" if len(deep) else "last_send",
        )
    image_deep = freq_sum(z, deep[0], deep[1][0].astype(f32))
    return image_shallow, image_deep


def solution(mesh):
    return jax.shard_map(
        functools.partial(body, mesh),
        mesh=mesh,
        in_specs=(P(None, "freq", "wide", None), P(None, None, "freq", None, None), P(), P(), P()),
        out_specs=(P("wide", "freq"), P("wide", "freq")),
        check_vma=False,
    )
```

```python
import functools
import math

import jax
import jax.numpy as jnp
from jax import lax
from jax.experimental import pallas as pl
from jax.experimental.pallas import tpu as pltpu
from jax.sharding import PartitionSpec as P

LANES = 128
VMEM_LIMIT = 24 * 1024 * 1024


class Sizes:
    def __init__(self, mesh, wave_shape, filters_shape, aperture_shape):
        self.wide = mesh.shape["wide"]
        self.freq = mesh.shape["freq"]
        self.pos = wave_shape[-1]
        self.rows = wave_shape[-2]
        self.side = math.isqrt(self.pos)
        self.bins = filters_shape[-2]
        self.tap_count = filters_shape[-1]
        self.taps = math.isqrt(self.tap_count)
        self.half = self.taps // 2
        self.tile_rows = LANES // self.side
        self.tiles = self.pos // LANES
        self.halo = -(-self.half // self.tile_rows)
        self.window = (1 + 2 * self.halo) * LANES
        self.blocks = aperture_shape[-1]
        self.blk = self.pos // self.blocks
        self.chunks = LANES // self.rows
        start = self.wide // 2 + self.wide // 8
        self.start = start // self.chunks * self.chunks

    def place(self, index):
        return (index - self.start) % self.wide

    def exchange(self, chunks):
        order = [(self.start + i) % self.wide for i in range(self.wide)]
        return lax.all_to_all(chunks, "wide", 0, 0, axis_index_groups=[order], tiled=True)


def fill_taps(z, filt_ref, step, rows_ref):
    rows_ref[...] = jnp.zeros_like(rows_ref)
    for k in range(z.bins):
        pair = filt_ref[step, 0, k].astype(jnp.float32)
        for part in range(2):
            row = part * z.bins + k
            rows_ref[row : row + 1, : z.tap_count] = pair[part : part + 1]


def fill_table(z, bins_ref, levels_ref, step, side, table_ref):
    blend = bins_ref.shape[1]
    ids = [bins_ref[step, j, side : side + 1] for j in range(blend)]
    weights = [levels_ref[step, j, side : side + 1].astype(jnp.float32) for j in range(blend)]
    total = sum(weights[1:], weights[0])
    table_ref[...] = jnp.zeros_like(table_ref)
    for k in range(z.bins):
        hits = [jnp.where(i == k, w, 0.0) for i, w in zip(ids, weights)]
        table_ref[k : k + 1, :] = sum(hits[1:], hits[0]) / total


def tap_index(z, in_y, in_x, out_y, out_x):
    a = in_y - out_y + (z.half - z.halo * z.tile_rows)
    b = in_x - out_x + z.half
    valid = (a >= 0) & (a < z.taps) & (b >= 0) & (b < z.taps)
    return jnp.where(valid, a * z.taps + b, LANES - 1)


def spread(rows_ref, row, index):
    source = jnp.broadcast_to(rows_ref[row : row + 1, :], index.shape)
    return jnp.take_along_axis(source, index, axis=1, mode="promise_in_bounds")


def chunk_order(z, column):
    chunk, inside = column // (2 * z.rows), column % (2 * z.rows)
    return inside // z.rows, chunk * z.rows + inside % z.rows


def fetch(pairs, sems):
    copies = [pltpu.make_async_copy(source, target, sems.at[i]) for i, (source, target) in enumerate(pairs)]
    for copy in copies:
        copy.start()
    return copies


def sent(z, out_ref, out_hbm, sems, tile):
    place = pl.ds(z.place(tile * z.chunks), z.chunks)
    return pltpu.make_async_copy(out_ref.at[place], out_hbm.at[place], sems.at[tile])


def send_out(z, out_ref, out_hbm, sems, tile):
    sent(z, out_ref, out_hbm, sems, tile).start()


def first_kernel(
    z,
    wave_hbm,
    filt_hbm,
    bins_hbm,
    levels_hbm,
    out_hbm,
    wave_ref,
    filt_ref,
    bins_ref,
    levels_ref,
    taps_ref,
    table_ref,
    band_ref,
    lhs_ref,
    acc_ref,
    source_ref,
    out_ref,
    out_sems,
    sems,
):
    copies = fetch(
        [(filt_hbm, filt_ref), (bins_hbm, bins_ref), (levels_hbm, levels_ref), (wave_hbm, wave_ref)], sems
    )
    group_rows = LANES // 2 // z.side
    window_rows = z.window // z.side
    lift = z.half - z.halo * z.tile_rows
    steps = window_rows - group_rows
    half_lanes = LANES // 2
    lane = lax.broadcasted_iota(jnp.int32, (z.side, LANES), 1)
    part, point = chunk_order(z, lane)
    b = lax.broadcasted_iota(jnp.int32, (z.side, LANES), 0) - point % z.side + z.half
    index = (group_rows - 1 - point // z.side) * z.taps + b + part * half_lanes
    index = jnp.where((b >= 0) & (b < z.taps), index, LANES - 1)
    lane = lax.broadcasted_iota(jnp.int32, (16, LANES), 1)
    row = lax.broadcasted_iota(jnp.int32, (16, LANES), 0)
    is_low = lane < half_lanes
    inside = jnp.where(is_low, lane, lane - half_lanes)
    tap = (row - (group_rows - 1) + lift) * z.taps + inside
    picked = jnp.where((inside < group_rows * z.taps) & (tap >= 0) & (tap < z.tap_count), tap, LANES - 1)
    empty = jnp.zeros((group_rows * z.side, LANES), jnp.bfloat16)
    for k in range(z.bins):
        for half in range(2):
            top, columns = half * z.window, 2 * k * LANES
            band_ref[top + z.window - group_rows * z.side : top + z.window, columns : columns + LANES] = empty
            band_ref[top : top + group_rows * z.side, columns + LANES : columns + 2 * LANES] = empty
    copies[0].wait()
    fill_taps(z, filt_ref, 0, taps_ref)
    for k in range(z.bins):
        columns = 2 * k * LANES
        real, imag = spread(taps_ref, k, picked), spread(taps_ref, z.bins + k, picked)
        source_ref[2 * k] = jnp.where(is_low, real, imag)
        source_ref[2 * k + 1] = jnp.where(is_low, -imag, real)
        for y in range(steps):
            for half in range(2):
                block = spread(source_ref.at[2 * k + half], y, index).astype(jnp.bfloat16)
                top = half * z.window + y * z.side
                band_ref[top : top + z.side, columns : columns + LANES] = block
                top += group_rows * z.side
                band_ref[top : top + z.side, columns + LANES : columns + 2 * LANES] = block
    copies[1].wait()
    copies[2].wait()
    fill_table(z, bins_ref, levels_ref, 0, 0, table_ref)
    copies[3].wait()
    spans = 1 + 2 * z.halo
    for part in range(2):
        for tile in range(z.tiles):
            for span in range(spans):
                source = tile + span - z.halo
                place = (part * spans + span) * LANES
                if 0 <= source < z.tiles:
                    piece = wave_ref[part, :, source * LANES : (source + 1) * LANES]
                else:
                    piece = jnp.zeros((z.rows, LANES), jnp.bfloat16)
                lhs_ref[tile * z.rows : (tile + 1) * z.rows, place : place + LANES] = piece
    lane = lax.broadcasted_iota(jnp.int32, (8, LANES), 1)
    points = [chunk_order(z, lane + v * LANES)[1] for v in range(2)]
    columns = []
    for tile in range(z.tiles):
        weights = table_ref[:, tile * LANES : (tile + 1) * LANES]
        picked = [jnp.take_along_axis(weights, p, axis=1, mode="promise_in_bounds") for p in points]
        columns.append(jnp.concatenate(picked, axis=1))
    for k in range(z.bins):
        product = jnp.dot(
            lhs_ref[...],
            band_ref[:, 2 * k * LANES : 2 * (k + 1) * LANES],
            preferred_element_type=jnp.float32,
        )
        for tile in range(z.tiles):
            rows = slice(tile * z.rows, (tile + 1) * z.rows)
            part = product[rows] * columns[tile][k : k + 1]
            if k:
                part = part + acc_ref[rows, :]
            if k < z.bins - 1:
                acc_ref[rows, :] = part
            else:
                total = part.astype(jnp.bfloat16)
                for c in range(z.chunks):
                    out_ref[z.place(tile * z.chunks + c)] = total[:, 2 * z.rows * c : 2 * z.rows * (c + 1)]
                send_out(z, out_ref, out_hbm, out_sems, tile)
    for tile in range(z.tiles):
        sent(z, out_ref, out_hbm, out_sems, tile).wait()


def prepare_middle_kernel(
    z,
    filt_hbm,
    bins_hbm,
    levels_hbm,
    aperture_hbm,
    second_ref,
    third_ref,
    keep_ref,
    filt_ref,
    bins_ref,
    levels_ref,
    aperture_ref,
    taps_ref,
    table_ref,
    columns_ref,
    sems,
):
    copies = fetch(
        [(filt_hbm, filt_ref), (bins_hbm, bins_ref), (levels_hbm, levels_ref), (aperture_hbm, aperture_ref)],
        sems,
    )
    for copy in copies:
        copy.wait()
    lane = lax.broadcasted_iota(jnp.int32, (LANES, LANES), 1)
    row = lax.broadcasted_iota(jnp.int32, (LANES, LANES), 0)
    for step, band_ref in ((0, second_ref), (1, third_ref)):
        fill_taps(z, filt_ref, step, taps_ref)
        fill_table(z, bins_ref, levels_ref, step, 1, table_ref)
        columns = jnp.transpose(table_ref[...])
        for k in range(z.bins):
            columns_ref[k] = jnp.broadcast_to(columns[:, k : k + 1], (z.pos, LANES))

        @pl.loop(0, 1 + 2 * z.halo)
        def _(span, band_ref=band_ref):
            inner = lane + span * LANES
            index = tap_index(z, inner // z.side, inner % z.side, row // z.side, row % z.side)
            for part in range(2):
                taps = [spread(taps_ref, part * z.bins + k, index) for k in range(z.bins)]
                place = pl.multiple_of(part * z.window + span * LANES, LANES)
                for tile in range(z.tiles):
                    total = 0.0
                    for k in range(z.bins):
                        total = total + taps[k] * columns_ref[k, tile * LANES : (tile + 1) * LANES, :]
                    band_ref[tile, :, pl.ds(place, LANES)] = total.astype(jnp.bfloat16)

    width = 2 * z.rows
    offset = lax.axis_index("wide") * z.rows
    receiver = lax.broadcasted_iota(jnp.int32, (z.blocks, width), 1) % z.rows + offset
    pick = (receiver // z.blk == lax.broadcasted_iota(jnp.int32, (z.blocks, width), 0)).astype(jnp.float32)
    keep_ref[...] = jnp.dot(aperture_ref[0].astype(jnp.float32), pick, preferred_element_type=jnp.float32)


def prepare_last_kernel(
    z,
    filt_hbm,
    bins_hbm,
    levels_hbm,
    aperture_hbm,
    fourth_ref,
    keep_ref,
    filt_ref,
    bins_ref,
    levels_ref,
    aperture_ref,
    taps_ref,
    table_ref,
    sems,
):
    copies = fetch(
        [(filt_hbm, filt_ref), (bins_hbm, bins_ref), (levels_hbm, levels_ref), (aperture_hbm, aperture_ref)],
        sems,
    )
    for copy in copies:
        copy.wait()
    fill_taps(z, filt_ref, 1, taps_ref)
    fill_table(z, bins_ref, levels_ref, 1, 0, table_ref)
    lane = lax.broadcasted_iota(jnp.int32, (z.rows, LANES), 1)
    row = lax.broadcasted_iota(jnp.int32, (z.rows, LANES), 0)

    @pl.loop(0, z.window // z.rows)
    def _(block):
        inner = row + block * z.rows
        index = tap_index(z, inner // z.side, inner % z.side, lane // z.side, lane % z.side)
        for part in range(2):
            taps = [spread(taps_ref, part * z.bins + k, index) for k in range(z.bins)]
            place = pl.multiple_of((2 * block + part) * z.rows, z.rows)
            for tile in range(z.tiles):
                total = 0.0
                for k in range(z.bins):
                    total = total + taps[k] * table_ref[k : k + 1, tile * LANES : (tile + 1) * LANES]
                total = total if part == 0 else -total
                if tile < z.halo:
                    total = jnp.where(block * z.rows >= (z.halo - tile) * LANES, total, 0.0)
                if tile >= z.tiles - z.halo:
                    total = jnp.where(block * z.rows < (z.tiles + z.halo - tile) * LANES, total, 0.0)
                fourth_ref[tile, pl.ds(place, z.rows), :] = total.astype(jnp.bfloat16)

    offset = lax.axis_index("wide") * z.rows
    source = lax.broadcasted_iota(jnp.int32, (z.rows, z.blocks), 0) + offset
    pick = (source // z.blk == lax.broadcasted_iota(jnp.int32, (z.rows, z.blocks), 1)).astype(jnp.float32)
    mine = jnp.dot(pick, aperture_ref[1].astype(jnp.float32), preferred_element_type=jnp.float32)
    receiver = lax.broadcasted_iota(jnp.int32, (z.blocks, z.pos), 1)
    stretch = (receiver // z.blk == lax.broadcasted_iota(jnp.int32, (z.blocks, z.pos), 0)).astype(jnp.float32)
    keep_ref[...] = jnp.dot(mine, stretch, preferred_element_type=jnp.float32)


def turned(z, block):
    return jnp.concatenate([-block[:, z.rows :], block[:, : z.rows]], axis=1)


def over_sources(z, band_ref, straight, turn, tile):
    low, high = max(tile - z.halo, 0), min(tile + z.halo, z.tiles - 1)
    reach = range(low, high + 1)
    rhs = jnp.concatenate([straight(j) for j in reach] + [turn(j) for j in reach], axis=0)
    width = len(reach) * LANES
    starts = [part * z.window + (low - tile + z.halo) * LANES for part in range(2)]
    band = jnp.concatenate([band_ref[tile, :, start : start + width] for start in starts], axis=1)
    return jnp.dot(band, rhs, preferred_element_type=jnp.float32)


def middle_kernel(
    z,
    moved_ref,
    second_ref,
    third_ref,
    keep_ref,
    out_hbm,
    shallow_hbm,
    turned_ref,
    straight2_ref,
    turned2_ref,
    out_ref,
    out_sems,
    shallow_sem,
):
    width = 2 * z.rows

    def field(tile):
        chunk = z.place(tile * z.chunks)
        return moved_ref[chunk : chunk + z.chunks].reshape(LANES, width)

    for tile in range(z.tiles):
        turned_ref[tile] = turned(z, field(tile))
    per_tile = LANES // z.blk
    for tile in range(z.tiles):
        mask = keep_ref[tile * per_tile : (tile + 1) * per_tile, :]
        mask = jnp.broadcast_to(mask[:, None, :], (per_tile, z.blk, width)).reshape(LANES, width)
        shallow = over_sources(z, second_ref, field, lambda j: turned_ref[j], tile) * mask
        shallow = shallow.astype(jnp.bfloat16)
        straight2_ref[tile * LANES : (tile + 1) * LANES, :] = shallow
        turned2_ref[tile] = turned(z, shallow)
    shallow_copy = pltpu.make_async_copy(straight2_ref, shallow_hbm, shallow_sem.at[0])
    shallow_copy.start()
    for tile in range(z.tiles):
        chunk = z.place(tile * z.chunks)
        third = over_sources(
            z, third_ref, lambda j: straight2_ref[j * LANES : (j + 1) * LANES, :], lambda j: turned2_ref[j], tile
        ).astype(jnp.bfloat16)
        out_ref[chunk : chunk + z.chunks] = third.reshape(z.chunks, z.rows, width)
        send_out(z, out_ref, out_hbm, out_sems, tile)
    for tile in range(z.tiles):
        sent(z, out_ref, out_hbm, out_sems, tile).wait()
    shallow_copy.wait()


def split_sum(z, real_ref, send_ref, own_ref):
    me = lax.axis_index("freq")
    width = z.pos // z.freq

    def part(shift):
        start = lax.rem(me + shift, z.freq) * width
        return real_ref[:, pl.ds(pl.multiple_of(start, width), width)]

    own_ref[...] = part(0).astype(jnp.float32)
    for shift in range(1, z.freq):
        send_ref[shift - 1] = part(shift)


def turn_kernel(z, shallow_hbm, send_ref, own_ref, shallow_ref, real_ref, sems):
    for copy in fetch([(shallow_hbm, shallow_ref)], sems):
        copy.wait()
    for tile in range(z.tiles):
        columns = slice(tile * LANES, (tile + 1) * LANES)
        flipped = jnp.transpose(shallow_ref[columns, :].astype(jnp.float32))
        real_ref[:, columns] = flipped[: z.rows].astype(jnp.bfloat16)
    split_sum(z, real_ref, send_ref, own_ref)


def last_kernel(z, shifts, field_ref, fourth_ref, keep_ref, out_ref):
    me = lax.axis_index("freq")
    tiles = z.tiles // z.freq
    for i, shift in enumerate(shifts):
        for j in range(tiles):
            tile = lax.rem(me + shift, z.freq) * tiles + j
            first = (tile - z.halo) * z.chunks - z.start + 2 * z.wide
            pieces = [field_ref[lax.rem(first + c, z.wide)] for c in range((1 + 2 * z.halo) * z.chunks)]
            columns = pl.ds(pl.multiple_of(tile * LANES, LANES), LANES)
            fourth = jnp.dot(
                jnp.concatenate(pieces, axis=1), fourth_ref[tile], preferred_element_type=jnp.float32
            )
            out_ref[i, :, j * LANES : (j + 1) * LANES] = (fourth * keep_ref[:, columns]).astype(out_ref.dtype)


def call(kernel, operands, outs, scratch, flops, name, fetched=False, sent=()):
    source = pltpu.HBM if fetched else pltpu.VMEM
    spaces = [pltpu.HBM if i < len(sent) else pltpu.VMEM for i in range(len(outs))]
    scratch = [pltpu.VMEM(shape, dtype) for shape, dtype in scratch]
    if sent:
        scratch += [pltpu.VMEM(*outs[0])] + [pltpu.SemaphoreType.DMA((parts,)) for parts in sent]
    if fetched:
        scratch = [pltpu.VMEM(x.shape, x.dtype) for x in operands] + scratch
        scratch.append(pltpu.SemaphoreType.DMA((len(operands),)))
        operands = [pltpu.with_memory_space_constraint(x, pltpu.HBM) for x in operands]
    return pl.pallas_call(
        kernel,
        out_shape=[space(shape, dtype) for space, (shape, dtype) in zip(spaces, outs)],
        in_specs=[pl.BlockSpec(memory_space=source)] * len(operands),
        out_specs=[pl.BlockSpec(memory_space=space) for space in spaces],
        scratch_shapes=scratch,
        compiler_params=pltpu.CompilerParams(vmem_limit_bytes=VMEM_LIMIT),
        cost_estimate=pl.CostEstimate(flops=flops, bytes_accessed=1 << 20, transcendentals=0),
        name=name,
    )(*operands)


def freq_sum(z, send, own):
    total = own
    for shift in range(1, z.freq):
        pairs = [(source, (source + shift) % z.freq) for source in range(z.freq)]
        total = total + lax.ppermute(send[shift - 1], "freq", pairs).astype(jnp.float32)
    return total


def body(mesh, wave, filters, vel_bins, blend_levels, aperture):
    z = Sizes(mesh, wave.shape, filters.shape, aperture.shape)
    bf16, f32 = jnp.bfloat16, jnp.float32
    filters = jnp.transpose(filters, (0, 2, 3, 1, 4))
    vel_bins = jnp.transpose(vel_bins, (0, 2, 1, 3))
    blend_levels = jnp.transpose(blend_levels, (0, 2, 1, 3))
    width = 2 * z.rows
    chunks = ((z.wide, z.rows, width), bf16)
    split = z.pos // z.freq
    parts = [((z.freq - 1, z.rows, split), bf16), ((z.rows, split), f32)]
    small = [((8, LANES), f32), ((8, z.pos), f32)]
    dense = 2 * 2 * z.window * z.bins * z.pos * z.rows
    (first,) = call(
        functools.partial(first_kernel, z),
        (wave[:, 0], filters, vel_bins, blend_levels),
        [chunks],
        small
        + [
            ((2 * z.window, 2 * z.bins * LANES), bf16),
            ((z.tiles * z.rows, 2 * z.window), bf16),
            ((z.tiles * z.rows, 2 * LANES), f32),
            ((2 * z.bins, 16, LANES), f32),
        ],
        2 * dense,
        "first",
        fetched=True,
        sent=(z.tiles,),
    )
    moved = z.exchange(first)
    second_band, third_band, shallow_keep = call(
        functools.partial(prepare_middle_kernel, z),
        (filters, vel_bins, blend_levels, aperture),
        [
            ((z.tiles, LANES, 2 * z.window), bf16),
            ((z.tiles, LANES, 2 * z.window), bf16),
            ((z.blocks, width), f32),
        ],
        small + [((z.bins, z.pos, LANES), f32)],
        dense,
        "prepare_middle",
        fetched=True,
    )
    third, shallow = call(
        functools.partial(middle_kernel, z),
        (moved, second_band, third_band, shallow_keep),
        [chunks, ((z.pos, width), bf16)],
        [((z.tiles, LANES, width), bf16), ((z.pos, width), bf16), ((z.tiles, LANES, width), bf16)],
        dense,
        "middle",
        sent=(z.tiles, 1),
    )
    returned = z.exchange(third)
    fourth_band, deep_keep = call(
        functools.partial(prepare_last_kernel, z),
        (filters, vel_bins, blend_levels, aperture),
        [((z.tiles, 2 * z.window, LANES), bf16), ((z.rows, z.pos), f32)],
        small,
        dense,
        "prepare_last",
        fetched=True,
    )
    image_shallow = freq_sum(
        z,
        *call(
            functools.partial(turn_kernel, z),
            (shallow,),
            parts,
            [((z.rows, z.pos), bf16)],
            dense // 8,
            "turn",
            fetched=True,
        ),
    )
    returned, image_shallow, fourth_band, deep_keep = lax.optimization_barrier(
        (returned, image_shallow, fourth_band, deep_keep)
    )
    deep = []
    for shifts, part in ((range(1, z.freq), parts[0]), (range(1), ((1, z.rows, split), bf16))):
        deep += call(
            functools.partial(last_kernel, z, shifts),
            (returned, fourth_band, deep_keep),
            [part],
            [],
            dense // 8,
            "last_own" if len(deep) else "last_send",
        )
    image_deep = freq_sum(z, deep[0], deep[1][0].astype(f32))
    return image_shallow, image_deep


def solution(mesh):
    return jax.shard_map(
        functools.partial(body, mesh),
        mesh=mesh,
        in_specs=(P(None, "freq", "wide", None), P(None, None, "freq", None, None), P(), P(), P()),
        out_specs=(P("wide", "freq"), P("wide", "freq")),
        check_vma=False,
    )
```

```python
import functools
import math

import jax
import jax.numpy as jnp
from jax import lax
from jax.experimental import pallas as pl
from jax.experimental.pallas import tpu as pltpu
from jax.sharding import PartitionSpec as P

LANES = 128
VMEM_LIMIT = 24 * 1024 * 1024


class Sizes:
    def __init__(self, mesh, wave_shape, filters_shape, aperture_shape):
        self.wide = mesh.shape["wide"]
        self.freq = mesh.shape["freq"]
        self.pos = wave_shape[-1]
        self.rows = wave_shape[-2]
        self.side = math.isqrt(self.pos)
        self.bins = filters_shape[-2]
        self.tap_count = filters_shape[-1]
        self.taps = math.isqrt(self.tap_count)
        self.half = self.taps // 2
        self.tile_rows = LANES // self.side
        self.tiles = self.pos // LANES
        self.halo = -(-self.half // self.tile_rows)
        self.window = (1 + 2 * self.halo) * LANES
        self.blocks = aperture_shape[-1]
        self.blk = self.pos // self.blocks
        self.chunks = LANES // self.rows
        quarter = self.wide // 4
        blocks = [list(range(i * quarter, (i + 1) * quarter)) for i in range(4)]
        middle = quarter // 2
        self.start = blocks[2][middle]
        self.orders = (
            blocks[2][middle:] + blocks[2][:middle] + blocks[1][::-1] + blocks[0] + blocks[3],
            [(self.start + i) % self.wide for i in range(self.wide)],
        )

    def place(self, turn, index):
        return self.orders[turn].index(index)

    def exchange(self, turn, chunks):
        return lax.all_to_all(chunks, "wide", 0, 0, axis_index_groups=[self.orders[turn]], tiled=True)


def fill_taps(z, filt_ref, step, rows_ref):
    rows_ref[...] = jnp.zeros_like(rows_ref)
    for k in range(z.bins):
        pair = filt_ref[step, 0, k].astype(jnp.float32)
        for part in range(2):
            row = part * z.bins + k
            rows_ref[row : row + 1, : z.tap_count] = pair[part : part + 1]


def fill_table(z, bins_ref, levels_ref, step, side, table_ref):
    blend = bins_ref.shape[1]
    ids = [bins_ref[step, j, side : side + 1] for j in range(blend)]
    weights = [levels_ref[step, j, side : side + 1].astype(jnp.float32) for j in range(blend)]
    total = sum(weights[1:], weights[0])
    table_ref[...] = jnp.zeros_like(table_ref)
    for k in range(z.bins):
        hits = [jnp.where(i == k, w, 0.0) for i, w in zip(ids, weights)]
        table_ref[k : k + 1, :] = sum(hits[1:], hits[0]) / total


def tap_index(z, in_y, in_x, out_y, out_x):
    a = in_y - out_y + (z.half - z.halo * z.tile_rows)
    b = in_x - out_x + z.half
    valid = (a >= 0) & (a < z.taps) & (b >= 0) & (b < z.taps)
    return jnp.where(valid, a * z.taps + b, LANES - 1)


def spread(rows_ref, row, index):
    source = jnp.broadcast_to(rows_ref[row : row + 1, :], index.shape)
    return jnp.take_along_axis(source, index, axis=1, mode="promise_in_bounds")


def chunk_order(z, column):
    chunk, inside = column // (2 * z.rows), column % (2 * z.rows)
    return inside // z.rows, chunk * z.rows + inside % z.rows


def fetch(pairs, sems):
    copies = [pltpu.make_async_copy(source, target, sems.at[i]) for i, (source, target) in enumerate(pairs)]
    for copy in copies:
        copy.start()
    return copies


def sent(z, turn, out_ref, out_hbm, sems, tile):
    place = pl.ds(min(z.place(turn, tile * z.chunks + c) for c in range(z.chunks)), z.chunks)
    return pltpu.make_async_copy(out_ref.at[place], out_hbm.at[place], sems.at[tile])


def first_kernel(
    z,
    wave_hbm,
    filt_hbm,
    bins_hbm,
    levels_hbm,
    out_hbm,
    wave_ref,
    filt_ref,
    bins_ref,
    levels_ref,
    taps_ref,
    table_ref,
    band_ref,
    lhs_ref,
    acc_ref,
    source_ref,
    out_ref,
    out_sems,
    sems,
):
    copies = fetch(
        [(filt_hbm, filt_ref), (bins_hbm, bins_ref), (levels_hbm, levels_ref), (wave_hbm, wave_ref)], sems
    )
    group_rows = LANES // 2 // z.side
    window_rows = z.window // z.side
    lift = z.half - z.halo * z.tile_rows
    steps = window_rows - group_rows
    half_lanes = LANES // 2
    lane = lax.broadcasted_iota(jnp.int32, (z.side, LANES), 1)
    part, point = chunk_order(z, lane)
    b = lax.broadcasted_iota(jnp.int32, (z.side, LANES), 0) - point % z.side + z.half
    index = (group_rows - 1 - point // z.side) * z.taps + b + part * half_lanes
    index = jnp.where((b >= 0) & (b < z.taps), index, LANES - 1)
    lane = lax.broadcasted_iota(jnp.int32, (16, LANES), 1)
    row = lax.broadcasted_iota(jnp.int32, (16, LANES), 0)
    is_low = lane < half_lanes
    inside = jnp.where(is_low, lane, lane - half_lanes)
    tap = (row - (group_rows - 1) + lift) * z.taps + inside
    picked = jnp.where((inside < group_rows * z.taps) & (tap >= 0) & (tap < z.tap_count), tap, LANES - 1)
    empty = jnp.zeros((group_rows * z.side, LANES), jnp.bfloat16)
    for k in range(z.bins):
        for half in range(2):
            top, columns = half * z.window, 2 * k * LANES
            band_ref[top + z.window - group_rows * z.side : top + z.window, columns : columns + LANES] = empty
            band_ref[top : top + group_rows * z.side, columns + LANES : columns + 2 * LANES] = empty
    copies[0].wait()
    fill_taps(z, filt_ref, 0, taps_ref)
    for k in range(z.bins):
        columns = 2 * k * LANES
        real, imag = spread(taps_ref, k, picked), spread(taps_ref, z.bins + k, picked)
        source_ref[2 * k] = jnp.where(is_low, real, imag)
        source_ref[2 * k + 1] = jnp.where(is_low, -imag, real)
        for y in range(steps):
            for half in range(2):
                block = spread(source_ref.at[2 * k + half], y, index).astype(jnp.bfloat16)
                top = half * z.window + y * z.side
                band_ref[top : top + z.side, columns : columns + LANES] = block
                top += group_rows * z.side
                band_ref[top : top + z.side, columns + LANES : columns + 2 * LANES] = block
    copies[1].wait()
    copies[2].wait()
    fill_table(z, bins_ref, levels_ref, 0, 0, table_ref)
    copies[3].wait()
    spans = 1 + 2 * z.halo
    for part in range(2):
        for tile in range(z.tiles):
            for span in range(spans):
                source = tile + span - z.halo
                place = (part * spans + span) * LANES
                if 0 <= source < z.tiles:
                    piece = wave_ref[part, :, source * LANES : (source + 1) * LANES]
                else:
                    piece = jnp.zeros((z.rows, LANES), jnp.bfloat16)
                lhs_ref[tile * z.rows : (tile + 1) * z.rows, place : place + LANES] = piece
    lane = lax.broadcasted_iota(jnp.int32, (8, LANES), 1)
    points = [chunk_order(z, lane + v * LANES)[1] for v in range(2)]
    columns = []
    for tile in range(z.tiles):
        weights = table_ref[:, tile * LANES : (tile + 1) * LANES]
        picked = [jnp.take_along_axis(weights, p, axis=1, mode="promise_in_bounds") for p in points]
        columns.append(jnp.concatenate(picked, axis=1))
    for k in range(z.bins):
        product = jnp.dot(
            lhs_ref[...],
            band_ref[:, 2 * k * LANES : 2 * (k + 1) * LANES],
            preferred_element_type=jnp.float32,
        )
        for tile in range(z.tiles):
            rows = slice(tile * z.rows, (tile + 1) * z.rows)
            part = product[rows] * columns[tile][k : k + 1]
            if k:
                part = part + acc_ref[rows, :]
            if k < z.bins - 1:
                acc_ref[rows, :] = part
            else:
                total = part.astype(jnp.bfloat16)
                for c in range(z.chunks):
                    out_ref[z.place(0, tile * z.chunks + c)] = total[:, 2 * z.rows * c : 2 * z.rows * (c + 1)]
                sent(z, 0, out_ref, out_hbm, out_sems, tile).start()
    for tile in range(z.tiles):
        sent(z, 0, out_ref, out_hbm, out_sems, tile).wait()


def prepare_middle_kernel(
    z,
    filt_hbm,
    bins_hbm,
    levels_hbm,
    aperture_hbm,
    second_ref,
    third_ref,
    keep_ref,
    filt_ref,
    bins_ref,
    levels_ref,
    aperture_ref,
    taps_ref,
    table_ref,
    columns_ref,
    sems,
):
    copies = fetch(
        [(filt_hbm, filt_ref), (bins_hbm, bins_ref), (levels_hbm, levels_ref), (aperture_hbm, aperture_ref)],
        sems,
    )
    for copy in copies:
        copy.wait()
    lane = lax.broadcasted_iota(jnp.int32, (LANES, LANES), 1)
    row = lax.broadcasted_iota(jnp.int32, (LANES, LANES), 0)
    for step, band_ref in ((0, second_ref), (1, third_ref)):
        fill_taps(z, filt_ref, step, taps_ref)
        fill_table(z, bins_ref, levels_ref, step, 1, table_ref)
        columns = jnp.transpose(table_ref[...])
        for k in range(z.bins):
            columns_ref[k] = jnp.broadcast_to(columns[:, k : k + 1], (z.pos, LANES))

        @pl.loop(0, 1 + 2 * z.halo)
        def _(span, band_ref=band_ref):
            inner = lane + span * LANES
            index = tap_index(z, inner // z.side, inner % z.side, row // z.side, row % z.side)
            for part in range(2):
                taps = [spread(taps_ref, part * z.bins + k, index) for k in range(z.bins)]
                place = pl.multiple_of(part * z.window + span * LANES, LANES)
                for tile in range(z.tiles):
                    total = 0.0
                    for k in range(z.bins):
                        total = total + taps[k] * columns_ref[k, tile * LANES : (tile + 1) * LANES, :]
                    band_ref[tile, :, pl.ds(place, LANES)] = total.astype(jnp.bfloat16)

    width = 2 * z.rows
    offset = lax.axis_index("wide") * z.rows
    receiver = lax.broadcasted_iota(jnp.int32, (z.blocks, width), 1) % z.rows + offset
    pick = (receiver // z.blk == lax.broadcasted_iota(jnp.int32, (z.blocks, width), 0)).astype(jnp.float32)
    keep_ref[...] = jnp.dot(aperture_ref[0].astype(jnp.float32), pick, preferred_element_type=jnp.float32)


def prepare_last_kernel(
    z,
    filt_hbm,
    bins_hbm,
    levels_hbm,
    aperture_hbm,
    fourth_ref,
    keep_ref,
    filt_ref,
    bins_ref,
    levels_ref,
    aperture_ref,
    taps_ref,
    table_ref,
    sems,
):
    copies = fetch(
        [(filt_hbm, filt_ref), (bins_hbm, bins_ref), (levels_hbm, levels_ref), (aperture_hbm, aperture_ref)],
        sems,
    )
    for copy in copies:
        copy.wait()
    fill_taps(z, filt_ref, 1, taps_ref)
    fill_table(z, bins_ref, levels_ref, 1, 0, table_ref)
    lane = lax.broadcasted_iota(jnp.int32, (z.rows, LANES), 1)
    row = lax.broadcasted_iota(jnp.int32, (z.rows, LANES), 0)

    @pl.loop(0, z.window // z.rows)
    def _(block):
        inner = row + block * z.rows
        index = tap_index(z, inner // z.side, inner % z.side, lane // z.side, lane % z.side)
        for part in range(2):
            taps = [spread(taps_ref, part * z.bins + k, index) for k in range(z.bins)]
            place = pl.multiple_of((2 * block + part) * z.rows, z.rows)
            for tile in range(z.tiles):
                total = 0.0
                for k in range(z.bins):
                    total = total + taps[k] * table_ref[k : k + 1, tile * LANES : (tile + 1) * LANES]
                total = total if part == 0 else -total
                if tile < z.halo:
                    total = jnp.where(block * z.rows >= (z.halo - tile) * LANES, total, 0.0)
                if tile >= z.tiles - z.halo:
                    total = jnp.where(block * z.rows < (z.tiles + z.halo - tile) * LANES, total, 0.0)
                fourth_ref[tile, pl.ds(place, z.rows), :] = total.astype(jnp.bfloat16)

    offset = lax.axis_index("wide") * z.rows
    source = lax.broadcasted_iota(jnp.int32, (z.rows, z.blocks), 0) + offset
    pick = (source // z.blk == lax.broadcasted_iota(jnp.int32, (z.rows, z.blocks), 1)).astype(jnp.float32)
    mine = jnp.dot(pick, aperture_ref[1].astype(jnp.float32), preferred_element_type=jnp.float32)
    receiver = lax.broadcasted_iota(jnp.int32, (z.blocks, z.pos), 1)
    stretch = (receiver // z.blk == lax.broadcasted_iota(jnp.int32, (z.blocks, z.pos), 0)).astype(jnp.float32)
    keep_ref[...] = jnp.dot(mine, stretch, preferred_element_type=jnp.float32)


def turned(z, block):
    return jnp.concatenate([-block[:, z.rows :], block[:, : z.rows]], axis=1)


def over_sources(z, band_ref, straight, turn, tile):
    low, high = max(tile - z.halo, 0), min(tile + z.halo, z.tiles - 1)
    reach = range(low, high + 1)
    rhs = jnp.concatenate([straight(j) for j in reach] + [turn(j) for j in reach], axis=0)
    width = len(reach) * LANES
    starts = [part * z.window + (low - tile + z.halo) * LANES for part in range(2)]
    band = jnp.concatenate([band_ref[tile, :, start : start + width] for start in starts], axis=1)
    return jnp.dot(band, rhs, preferred_element_type=jnp.float32)


def middle_kernel(
    z,
    moved_ref,
    second_ref,
    third_ref,
    keep_ref,
    out_hbm,
    shallow_hbm,
    turned_ref,
    straight2_ref,
    turned2_ref,
    out_ref,
    out_sems,
    shallow_sem,
):
    width = 2 * z.rows

    def field(tile):
        return jnp.concatenate([moved_ref[z.place(0, tile * z.chunks + c)] for c in range(z.chunks)], axis=0)

    for tile in range(z.tiles):
        turned_ref[tile] = turned(z, field(tile))
    per_tile = LANES // z.blk
    for tile in range(z.tiles):
        mask = keep_ref[tile * per_tile : (tile + 1) * per_tile, :]
        mask = jnp.broadcast_to(mask[:, None, :], (per_tile, z.blk, width)).reshape(LANES, width)
        shallow = over_sources(z, second_ref, field, lambda j: turned_ref[j], tile) * mask
        shallow = shallow.astype(jnp.bfloat16)
        straight2_ref[tile * LANES : (tile + 1) * LANES, :] = shallow
        turned2_ref[tile] = turned(z, shallow)
    shallow_copy = pltpu.make_async_copy(straight2_ref, shallow_hbm, shallow_sem.at[0])
    shallow_copy.start()
    for tile in range(z.tiles):
        chunk = z.place(1, tile * z.chunks)
        third = over_sources(
            z, third_ref, lambda j: straight2_ref[j * LANES : (j + 1) * LANES, :], lambda j: turned2_ref[j], tile
        ).astype(jnp.bfloat16)
        out_ref[chunk : chunk + z.chunks] = third.reshape(z.chunks, z.rows, width)
        sent(z, 1, out_ref, out_hbm, out_sems, tile).start()
    for tile in range(z.tiles):
        sent(z, 1, out_ref, out_hbm, out_sems, tile).wait()
    shallow_copy.wait()


def split_sum(z, real_ref, send_ref, own_ref):
    me = lax.axis_index("freq")
    width = z.pos // z.freq

    def part(shift):
        start = lax.rem(me + shift, z.freq) * width
        return real_ref[:, pl.ds(pl.multiple_of(start, width), width)]

    own_ref[...] = part(0).astype(jnp.float32)
    for shift in range(1, z.freq):
        send_ref[shift - 1] = part(shift)


def turn_kernel(z, shallow_hbm, send_ref, own_ref, shallow_ref, real_ref, sems):
    for copy in fetch([(shallow_hbm, shallow_ref)], sems):
        copy.wait()
    for tile in range(z.tiles):
        columns = slice(tile * LANES, (tile + 1) * LANES)
        flipped = jnp.transpose(shallow_ref[columns, :].astype(jnp.float32))
        real_ref[:, columns] = flipped[: z.rows].astype(jnp.bfloat16)
    split_sum(z, real_ref, send_ref, own_ref)


def last_kernel(z, shifts, field_ref, fourth_ref, keep_ref, out_ref):
    me = lax.axis_index("freq")
    tiles = z.tiles // z.freq
    for i, shift in enumerate(shifts):
        for j in range(tiles):
            tile = lax.rem(me + shift, z.freq) * tiles + j
            first = (tile - z.halo) * z.chunks - z.start + 2 * z.wide
            pieces = [field_ref[lax.rem(first + c, z.wide)] for c in range((1 + 2 * z.halo) * z.chunks)]
            columns = pl.ds(pl.multiple_of(tile * LANES, LANES), LANES)
            fourth = jnp.dot(
                jnp.concatenate(pieces, axis=1), fourth_ref[tile], preferred_element_type=jnp.float32
            )
            out_ref[i, :, j * LANES : (j + 1) * LANES] = (fourth * keep_ref[:, columns]).astype(out_ref.dtype)


def call(kernel, operands, outs, scratch, flops, name, fetched=False, sent=()):
    source = pltpu.HBM if fetched else pltpu.VMEM
    spaces = [pltpu.HBM if i < len(sent) else pltpu.VMEM for i in range(len(outs))]
    scratch = [pltpu.VMEM(shape, dtype) for shape, dtype in scratch]
    if sent:
        scratch += [pltpu.VMEM(*outs[0])] + [pltpu.SemaphoreType.DMA((parts,)) for parts in sent]
    if fetched:
        scratch = [pltpu.VMEM(x.shape, x.dtype) for x in operands] + scratch
        scratch.append(pltpu.SemaphoreType.DMA((len(operands),)))
        operands = [pltpu.with_memory_space_constraint(x, pltpu.HBM) for x in operands]
    return pl.pallas_call(
        kernel,
        out_shape=[space(shape, dtype) for space, (shape, dtype) in zip(spaces, outs)],
        in_specs=[pl.BlockSpec(memory_space=source)] * len(operands),
        out_specs=[pl.BlockSpec(memory_space=space) for space in spaces],
        scratch_shapes=scratch,
        compiler_params=pltpu.CompilerParams(vmem_limit_bytes=VMEM_LIMIT),
        cost_estimate=pl.CostEstimate(flops=flops, bytes_accessed=1 << 20, transcendentals=0),
        name=name,
    )(*operands)


def freq_sum(z, send, own):
    total = own
    for shift in range(1, z.freq):
        pairs = [(source, (source + shift) % z.freq) for source in range(z.freq)]
        total = total + lax.ppermute(send[shift - 1], "freq", pairs).astype(jnp.float32)
    return total


def body(mesh, wave, filters, vel_bins, blend_levels, aperture):
    z = Sizes(mesh, wave.shape, filters.shape, aperture.shape)
    bf16, f32 = jnp.bfloat16, jnp.float32
    filters = jnp.transpose(filters, (0, 2, 3, 1, 4))
    vel_bins = jnp.transpose(vel_bins, (0, 2, 1, 3))
    blend_levels = jnp.transpose(blend_levels, (0, 2, 1, 3))
    width = 2 * z.rows
    chunks = ((z.wide, z.rows, width), bf16)
    split = z.pos // z.freq
    parts = [((z.freq - 1, z.rows, split), bf16), ((z.rows, split), f32)]
    small = [((8, LANES), f32), ((8, z.pos), f32)]
    dense = 2 * 2 * z.window * z.bins * z.pos * z.rows
    (first,) = call(
        functools.partial(first_kernel, z),
        (wave[:, 0], filters, vel_bins, blend_levels),
        [chunks],
        small
        + [
            ((2 * z.window, 2 * z.bins * LANES), bf16),
            ((z.tiles * z.rows, 2 * z.window), bf16),
            ((z.tiles * z.rows, 2 * LANES), f32),
            ((2 * z.bins, 16, LANES), f32),
        ],
        2 * dense,
        "first",
        fetched=True,
        sent=(z.tiles,),
    )
    moved = z.exchange(0, first)
    second_band, third_band, shallow_keep = call(
        functools.partial(prepare_middle_kernel, z),
        (filters, vel_bins, blend_levels, aperture),
        [
            ((z.tiles, LANES, 2 * z.window), bf16),
            ((z.tiles, LANES, 2 * z.window), bf16),
            ((z.blocks, width), f32),
        ],
        small + [((z.bins, z.pos, LANES), f32)],
        dense,
        "prepare_middle",
        fetched=True,
    )
    third, shallow = call(
        functools.partial(middle_kernel, z),
        (moved, second_band, third_band, shallow_keep),
        [chunks, ((z.pos, width), bf16)],
        [((z.tiles, LANES, width), bf16), ((z.pos, width), bf16), ((z.tiles, LANES, width), bf16)],
        dense,
        "middle",
        sent=(z.tiles, 1),
    )
    returned = z.exchange(1, third)
    fourth_band, deep_keep = call(
        functools.partial(prepare_last_kernel, z),
        (filters, vel_bins, blend_levels, aperture),
        [((z.tiles, 2 * z.window, LANES), bf16), ((z.rows, z.pos), f32)],
        small,
        dense,
        "prepare_last",
        fetched=True,
    )
    image_shallow = freq_sum(
        z,
        *call(
            functools.partial(turn_kernel, z),
            (shallow,),
            parts,
            [((z.rows, z.pos), bf16)],
            dense // 8,
            "turn",
            fetched=True,
        ),
    )
    returned, image_shallow, fourth_band, deep_keep = lax.optimization_barrier(
        (returned, image_shallow, fourth_band, deep_keep)
    )
    deep = []
    for shifts, part in ((range(1, z.freq), parts[0]), (range(1), ((1, z.rows, split), bf16))):
        deep += call(
            functools.partial(last_kernel, z, shifts),
            (returned, fourth_band, deep_keep),
            [part],
            [],
            dense // 8,
            "last_own" if len(deep) else "last_send",
        )
    image_deep = freq_sum(z, deep[0], deep[1][0].astype(f32))
    return image_shallow, image_deep


def solution(mesh):
    return jax.shard_map(
        functools.partial(body, mesh),
        mesh=mesh,
        in_specs=(P(None, "freq", "wide", None), P(None, None, "freq", None, None), P(), P(), P()),
        out_specs=(P("wide", "freq"), P("wide", "freq")),
        check_vma=False,
    )
```

```python
import functools
import math

import jax
import jax.numpy as jnp
from jax import lax
from jax.experimental import pallas as pl
from jax.experimental.pallas import tpu as pltpu
from jax.sharding import PartitionSpec as P

LANES = 128
VMEM_LIMIT = 24 * 1024 * 1024


class Sizes:
    def __init__(self, mesh, wave_shape, filters_shape, aperture_shape):
        self.wide = mesh.shape["wide"]
        self.freq = mesh.shape["freq"]
        self.pos = wave_shape[-1]
        self.rows = wave_shape[-2]
        self.side = math.isqrt(self.pos)
        self.bins = filters_shape[-2]
        self.tap_count = filters_shape[-1]
        self.taps = math.isqrt(self.tap_count)
        self.half = self.taps // 2
        self.tile_rows = LANES // self.side
        self.tiles = self.pos // LANES
        self.halo = -(-self.half // self.tile_rows)
        self.window = (1 + 2 * self.halo) * LANES
        self.blocks = aperture_shape[-1]
        self.blk = self.pos // self.blocks
        self.chunks = LANES // self.rows
        quarter = self.wide // 4
        blocks = [list(range(i * quarter, (i + 1) * quarter)) for i in range(4)]
        middle = quarter // 2
        self.start = blocks[2][middle]
        self.orders = (
            blocks[2][middle:] + blocks[2][:middle] + blocks[1][::-1] + blocks[0] + blocks[3],
            [(self.start + i) % self.wide for i in range(self.wide)],
        )

    def place(self, turn, index):
        return self.orders[turn].index(index)

    def exchange(self, turn, chunks):
        return lax.all_to_all(chunks, "wide", 0, 0, axis_index_groups=[self.orders[turn]], tiled=True)


def fill_taps(z, filt_ref, step, rows_ref):
    rows_ref[...] = jnp.zeros_like(rows_ref)
    for k in range(z.bins):
        pair = filt_ref[step, 0, k].astype(jnp.float32)
        for part in range(2):
            row = part * z.bins + k
            rows_ref[row : row + 1, : z.tap_count] = pair[part : part + 1]


def fill_table(z, bins_ref, levels_ref, step, side, table_ref):
    blend = bins_ref.shape[1]
    ids = [bins_ref[step, j, side : side + 1] for j in range(blend)]
    weights = [levels_ref[step, j, side : side + 1].astype(jnp.float32) for j in range(blend)]
    total = sum(weights[1:], weights[0])
    table_ref[...] = jnp.zeros_like(table_ref)
    for k in range(z.bins):
        hits = [jnp.where(i == k, w, 0.0) for i, w in zip(ids, weights)]
        table_ref[k : k + 1, :] = sum(hits[1:], hits[0]) / total


def tap_index(z, in_y, in_x, out_y, out_x):
    a = in_y - out_y + (z.half - z.halo * z.tile_rows)
    b = in_x - out_x + z.half
    valid = (a >= 0) & (a < z.taps) & (b >= 0) & (b < z.taps)
    return jnp.where(valid, a * z.taps + b, LANES - 1)


def spread(rows_ref, row, index):
    source = jnp.broadcast_to(rows_ref[row : row + 1, :], index.shape)
    return jnp.take_along_axis(source, index, axis=1, mode="promise_in_bounds")


def chunk_order(z, column):
    chunk, inside = column // (2 * z.rows), column % (2 * z.rows)
    return inside // z.rows, chunk * z.rows + inside % z.rows


def fetch(pairs, sems):
    copies = [pltpu.make_async_copy(source, target, sems.at[i]) for i, (source, target) in enumerate(pairs)]
    for copy in copies:
        copy.start()
    return copies


def sent(z, turn, out_ref, out_hbm, sems, tile):
    place = pl.ds(min(z.place(turn, tile * z.chunks + c) for c in range(z.chunks)), z.chunks)
    return pltpu.make_async_copy(out_ref.at[place], out_hbm.at[place], sems.at[tile])


def first_kernel(
    z,
    wave_hbm,
    filt_hbm,
    bins_hbm,
    levels_hbm,
    out_hbm,
    wave_ref,
    filt_ref,
    bins_ref,
    levels_ref,
    taps_ref,
    table_ref,
    band_ref,
    lhs_ref,
    acc_ref,
    source_ref,
    out_ref,
    out_sems,
    sems,
):
    copies = fetch(
        [(filt_hbm, filt_ref), (bins_hbm, bins_ref), (levels_hbm, levels_ref), (wave_hbm, wave_ref)], sems
    )
    group_rows = LANES // 2 // z.side
    window_rows = z.window // z.side
    lift = z.half - z.halo * z.tile_rows
    steps = window_rows - group_rows
    half_lanes = LANES // 2
    lane = lax.broadcasted_iota(jnp.int32, (z.side, LANES), 1)
    part, point = chunk_order(z, lane)
    b = lax.broadcasted_iota(jnp.int32, (z.side, LANES), 0) - point % z.side + z.half
    index = (group_rows - 1 - point // z.side) * z.taps + b + part * half_lanes
    index = jnp.where((b >= 0) & (b < z.taps), index, LANES - 1)
    lane = lax.broadcasted_iota(jnp.int32, (16, LANES), 1)
    row = lax.broadcasted_iota(jnp.int32, (16, LANES), 0)
    is_low = lane < half_lanes
    inside = jnp.where(is_low, lane, lane - half_lanes)
    tap = (row - (group_rows - 1) + lift) * z.taps + inside
    picked = jnp.where((inside < group_rows * z.taps) & (tap >= 0) & (tap < z.tap_count), tap, LANES - 1)
    empty = jnp.zeros((group_rows * z.side, LANES), jnp.bfloat16)
    for k in range(z.bins):
        for half in range(2):
            top, columns = half * z.window, 2 * k * LANES
            band_ref[top + z.window - group_rows * z.side : top + z.window, columns : columns + LANES] = empty
            band_ref[top : top + group_rows * z.side, columns + LANES : columns + 2 * LANES] = empty
    copies[0].wait()
    fill_taps(z, filt_ref, 0, taps_ref)
    for k in range(z.bins):
        columns = 2 * k * LANES
        real, imag = spread(taps_ref, k, picked), spread(taps_ref, z.bins + k, picked)
        source_ref[2 * k] = jnp.where(is_low, real, imag)
        source_ref[2 * k + 1] = jnp.where(is_low, -imag, real)
        for y in range(steps):
            for half in range(2):
                block = spread(source_ref.at[2 * k + half], y, index).astype(jnp.bfloat16)
                top = half * z.window + y * z.side
                band_ref[top : top + z.side, columns : columns + LANES] = block
                top += group_rows * z.side
                band_ref[top : top + z.side, columns + LANES : columns + 2 * LANES] = block
    copies[1].wait()
    copies[2].wait()
    copies[3].wait()
    spans = 1 + 2 * z.halo
    for part in range(2):
        for tile in range(z.tiles):
            for span in range(spans):
                source = tile + span - z.halo
                place = (part * spans + span) * LANES
                if 0 <= source < z.tiles:
                    piece = wave_ref[part, :, source * LANES : (source + 1) * LANES]
                else:
                    piece = jnp.zeros((z.rows, LANES), jnp.bfloat16)
                lhs_ref[tile * z.rows : (tile + 1) * z.rows, place : place + LANES] = piece
    lane = lax.broadcasted_iota(jnp.int32, (8, LANES), 1)
    points = [chunk_order(z, lane + v * LANES)[1] for v in range(2)]
    for k in range(z.bins):
        product = jnp.dot(
            lhs_ref[...],
            band_ref[:, 2 * k * LANES : 2 * (k + 1) * LANES],
            preferred_element_type=jnp.float32,
        )
        if k == 0:
            fill_table(z, bins_ref, levels_ref, 0, 0, table_ref)
            columns = []
            for tile in range(z.tiles):
                weights = table_ref[:, tile * LANES : (tile + 1) * LANES]
                picked = [jnp.take_along_axis(weights, p, axis=1, mode="promise_in_bounds") for p in points]
                columns.append(jnp.concatenate(picked, axis=1))
        for tile in range(z.tiles):
            rows = slice(tile * z.rows, (tile + 1) * z.rows)
            part = product[rows] * columns[tile][k : k + 1]
            if k:
                part = part + acc_ref[rows, :]
            if k < z.bins - 1:
                acc_ref[rows, :] = part
            else:
                total = part.astype(jnp.bfloat16)
                for c in range(z.chunks):
                    out_ref[z.place(0, tile * z.chunks + c)] = total[:, 2 * z.rows * c : 2 * z.rows * (c + 1)]
                sent(z, 0, out_ref, out_hbm, out_sems, tile).start()
    for tile in range(z.tiles):
        sent(z, 0, out_ref, out_hbm, out_sems, tile).wait()


def prepare_middle_kernel(
    z,
    filt_hbm,
    bins_hbm,
    levels_hbm,
    aperture_hbm,
    second_ref,
    third_ref,
    keep_ref,
    filt_ref,
    bins_ref,
    levels_ref,
    aperture_ref,
    taps_ref,
    table_ref,
    columns_ref,
    sems,
):
    copies = fetch(
        [(filt_hbm, filt_ref), (bins_hbm, bins_ref), (levels_hbm, levels_ref), (aperture_hbm, aperture_ref)],
        sems,
    )
    for copy in copies:
        copy.wait()
    lane = lax.broadcasted_iota(jnp.int32, (LANES, LANES), 1)
    row = lax.broadcasted_iota(jnp.int32, (LANES, LANES), 0)
    for step, band_ref in ((0, second_ref), (1, third_ref)):
        fill_taps(z, filt_ref, step, taps_ref)
        fill_table(z, bins_ref, levels_ref, step, 1, table_ref)
        columns = jnp.transpose(table_ref[...])
        for k in range(z.bins):
            columns_ref[k] = jnp.broadcast_to(columns[:, k : k + 1], (z.pos, LANES))

        @pl.loop(0, 1 + 2 * z.halo)
        def _(span, band_ref=band_ref):
            inner = lane + span * LANES
            index = tap_index(z, inner // z.side, inner % z.side, row // z.side, row % z.side)
            for part in range(2):
                taps = [spread(taps_ref, part * z.bins + k, index) for k in range(z.bins)]
                place = pl.multiple_of(part * z.window + span * LANES, LANES)
                for tile in range(z.tiles):
                    total = 0.0
                    for k in range(z.bins):
                        total = total + taps[k] * columns_ref[k, tile * LANES : (tile + 1) * LANES, :]
                    band_ref[tile, :, pl.ds(place, LANES)] = total.astype(jnp.bfloat16)

    width = 2 * z.rows
    offset = lax.axis_index("wide") * z.rows
    receiver = lax.broadcasted_iota(jnp.int32, (z.blocks, width), 1) % z.rows + offset
    pick = (receiver // z.blk == lax.broadcasted_iota(jnp.int32, (z.blocks, width), 0)).astype(jnp.float32)
    keep_ref[...] = jnp.dot(aperture_ref[0].astype(jnp.float32), pick, preferred_element_type=jnp.float32)


def prepare_last_kernel(
    z,
    filt_hbm,
    bins_hbm,
    levels_hbm,
    aperture_hbm,
    fourth_ref,
    keep_ref,
    filt_ref,
    bins_ref,
    levels_ref,
    aperture_ref,
    taps_ref,
    table_ref,
    sems,
):
    copies = fetch(
        [(filt_hbm, filt_ref), (bins_hbm, bins_ref), (levels_hbm, levels_ref), (aperture_hbm, aperture_ref)],
        sems,
    )
    for copy in copies:
        copy.wait()
    fill_taps(z, filt_ref, 1, taps_ref)
    fill_table(z, bins_ref, levels_ref, 1, 0, table_ref)
    lane = lax.broadcasted_iota(jnp.int32, (z.rows, LANES), 1)
    row = lax.broadcasted_iota(jnp.int32, (z.rows, LANES), 0)

    @pl.loop(0, z.window // z.rows)
    def _(block):
        inner = row + block * z.rows
        index = tap_index(z, inner // z.side, inner % z.side, lane // z.side, lane % z.side)
        for part in range(2):
            taps = [spread(taps_ref, part * z.bins + k, index) for k in range(z.bins)]
            place = pl.multiple_of((2 * block + part) * z.rows, z.rows)
            for tile in range(z.tiles):
                total = 0.0
                for k in range(z.bins):
                    total = total + taps[k] * table_ref[k : k + 1, tile * LANES : (tile + 1) * LANES]
                total = total if part == 0 else -total
                if tile < z.halo:
                    total = jnp.where(block * z.rows >= (z.halo - tile) * LANES, total, 0.0)
                if tile >= z.tiles - z.halo:
                    total = jnp.where(block * z.rows < (z.tiles + z.halo - tile) * LANES, total, 0.0)
                fourth_ref[tile, pl.ds(place, z.rows), :] = total.astype(jnp.bfloat16)

    offset = lax.axis_index("wide") * z.rows
    source = lax.broadcasted_iota(jnp.int32, (z.rows, z.blocks), 0) + offset
    pick = (source // z.blk == lax.broadcasted_iota(jnp.int32, (z.rows, z.blocks), 1)).astype(jnp.float32)
    mine = jnp.dot(pick, aperture_ref[1].astype(jnp.float32), preferred_element_type=jnp.float32)
    receiver = lax.broadcasted_iota(jnp.int32, (z.blocks, z.pos), 1)
    stretch = (receiver // z.blk == lax.broadcasted_iota(jnp.int32, (z.blocks, z.pos), 0)).astype(jnp.float32)
    keep_ref[...] = jnp.dot(mine, stretch, preferred_element_type=jnp.float32)


def turned(z, block):
    return jnp.concatenate([-block[:, z.rows :], block[:, : z.rows]], axis=1)


def over_sources(z, band_ref, straight, turn, tile):
    low, high = max(tile - z.halo, 0), min(tile + z.halo, z.tiles - 1)
    reach = range(low, high + 1)
    rhs = jnp.concatenate([straight(j) for j in reach] + [turn(j) for j in reach], axis=0)
    width = len(reach) * LANES
    starts = [part * z.window + (low - tile + z.halo) * LANES for part in range(2)]
    band = jnp.concatenate([band_ref[tile, :, start : start + width] for start in starts], axis=1)
    return jnp.dot(band, rhs, preferred_element_type=jnp.float32)


def middle_kernel(
    z,
    moved_ref,
    second_ref,
    third_ref,
    keep_ref,
    out_hbm,
    shallow_hbm,
    turned_ref,
    straight2_ref,
    turned2_ref,
    out_ref,
    out_sems,
    shallow_sem,
):
    width = 2 * z.rows

    def field(tile):
        return jnp.concatenate([moved_ref[z.place(0, tile * z.chunks + c)] for c in range(z.chunks)], axis=0)

    for tile in range(z.tiles):
        turned_ref[tile] = turned(z, field(tile))
    per_tile = LANES // z.blk
    for tile in range(z.tiles):
        mask = keep_ref[tile * per_tile : (tile + 1) * per_tile, :]
        mask = jnp.broadcast_to(mask[:, None, :], (per_tile, z.blk, width)).reshape(LANES, width)
        shallow = over_sources(z, second_ref, field, lambda j: turned_ref[j], tile) * mask
        shallow = shallow.astype(jnp.bfloat16)
        straight2_ref[tile * LANES : (tile + 1) * LANES, :] = shallow
        turned2_ref[tile] = turned(z, shallow)
    shallow_copy = pltpu.make_async_copy(straight2_ref, shallow_hbm, shallow_sem.at[0])
    shallow_copy.start()
    for tile in range(z.tiles):
        chunk = z.place(1, tile * z.chunks)
        third = over_sources(
            z, third_ref, lambda j: straight2_ref[j * LANES : (j + 1) * LANES, :], lambda j: turned2_ref[j], tile
        ).astype(jnp.bfloat16)
        out_ref[chunk : chunk + z.chunks] = third.reshape(z.chunks, z.rows, width)
        sent(z, 1, out_ref, out_hbm, out_sems, tile).start()
    for tile in range(z.tiles):
        sent(z, 1, out_ref, out_hbm, out_sems, tile).wait()
    shallow_copy.wait()


def split_sum(z, real_ref, send_ref, own_ref):
    me = lax.axis_index("freq")
    width = z.pos // z.freq

    def part(shift):
        start = lax.rem(me + shift, z.freq) * width
        return real_ref[:, pl.ds(pl.multiple_of(start, width), width)]

    own_ref[...] = part(0).astype(jnp.float32)
    for shift in range(1, z.freq):
        send_ref[shift - 1] = part(shift)


def turn_kernel(z, shallow_hbm, send_ref, own_ref, shallow_ref, real_ref, sems):
    for copy in fetch([(shallow_hbm, shallow_ref)], sems):
        copy.wait()
    for tile in range(z.tiles):
        columns = slice(tile * LANES, (tile + 1) * LANES)
        flipped = jnp.transpose(shallow_ref[columns, :].astype(jnp.float32))
        real_ref[:, columns] = flipped[: z.rows].astype(jnp.bfloat16)
    split_sum(z, real_ref, send_ref, own_ref)


def last_kernel(z, shifts, field_ref, fourth_ref, keep_ref, out_ref):
    me = lax.axis_index("freq")
    tiles = z.tiles // z.freq
    for i, shift in enumerate(shifts):
        for j in range(tiles):
            tile = lax.rem(me + shift, z.freq) * tiles + j
            first = (tile - z.halo) * z.chunks - z.start + 2 * z.wide
            pieces = [field_ref[lax.rem(first + c, z.wide)] for c in range((1 + 2 * z.halo) * z.chunks)]
            columns = pl.ds(pl.multiple_of(tile * LANES, LANES), LANES)
            fourth = jnp.dot(
                jnp.concatenate(pieces, axis=1), fourth_ref[tile], preferred_element_type=jnp.float32
            )
            out_ref[i, :, j * LANES : (j + 1) * LANES] = (fourth * keep_ref[:, columns]).astype(out_ref.dtype)


def call(kernel, operands, outs, scratch, flops, name, fetched=False, sent=()):
    source = pltpu.HBM if fetched else pltpu.VMEM
    spaces = [pltpu.HBM if i < len(sent) else pltpu.VMEM for i in range(len(outs))]
    scratch = [pltpu.VMEM(shape, dtype) for shape, dtype in scratch]
    if sent:
        scratch += [pltpu.VMEM(*outs[0])] + [pltpu.SemaphoreType.DMA((parts,)) for parts in sent]
    if fetched:
        scratch = [pltpu.VMEM(x.shape, x.dtype) for x in operands] + scratch
        scratch.append(pltpu.SemaphoreType.DMA((len(operands),)))
        operands = [pltpu.with_memory_space_constraint(x, pltpu.HBM) for x in operands]
    return pl.pallas_call(
        kernel,
        out_shape=[space(shape, dtype) for space, (shape, dtype) in zip(spaces, outs)],
        in_specs=[pl.BlockSpec(memory_space=source)] * len(operands),
        out_specs=[pl.BlockSpec(memory_space=space) for space in spaces],
        scratch_shapes=scratch,
        compiler_params=pltpu.CompilerParams(vmem_limit_bytes=VMEM_LIMIT),
        cost_estimate=pl.CostEstimate(flops=flops, bytes_accessed=1 << 20, transcendentals=0),
        name=name,
    )(*operands)


def freq_sum(z, send, own):
    total = own
    for shift in range(1, z.freq):
        pairs = [(source, (source + shift) % z.freq) for source in range(z.freq)]
        total = total + lax.ppermute(send[shift - 1], "freq", pairs).astype(jnp.float32)
    return total


def body(mesh, wave, filters, vel_bins, blend_levels, aperture):
    z = Sizes(mesh, wave.shape, filters.shape, aperture.shape)
    bf16, f32 = jnp.bfloat16, jnp.float32
    filters = jnp.transpose(filters, (0, 2, 3, 1, 4))
    vel_bins = jnp.transpose(vel_bins, (0, 2, 1, 3))
    blend_levels = jnp.transpose(blend_levels, (0, 2, 1, 3))
    width = 2 * z.rows
    chunks = ((z.wide, z.rows, width), bf16)
    split = z.pos // z.freq
    parts = [((z.freq - 1, z.rows, split), bf16), ((z.rows, split), f32)]
    small = [((8, LANES), f32), ((8, z.pos), f32)]
    dense = 2 * 2 * z.window * z.bins * z.pos * z.rows
    (first,) = call(
        functools.partial(first_kernel, z),
        (wave[:, 0], filters, vel_bins, blend_levels),
        [chunks],
        small
        + [
            ((2 * z.window, 2 * z.bins * LANES), bf16),
            ((z.tiles * z.rows, 2 * z.window), bf16),
            ((z.tiles * z.rows, 2 * LANES), f32),
            ((2 * z.bins, 16, LANES), f32),
        ],
        2 * dense,
        "first",
        fetched=True,
        sent=(z.tiles,),
    )
    moved = z.exchange(0, first)
    second_band, third_band, shallow_keep = call(
        functools.partial(prepare_middle_kernel, z),
        (filters, vel_bins, blend_levels, aperture),
        [
            ((z.tiles, LANES, 2 * z.window), bf16),
            ((z.tiles, LANES, 2 * z.window), bf16),
            ((z.blocks, width), f32),
        ],
        small + [((z.bins, z.pos, LANES), f32)],
        dense,
        "prepare_middle",
        fetched=True,
    )
    third, shallow = call(
        functools.partial(middle_kernel, z),
        (moved, second_band, third_band, shallow_keep),
        [chunks, ((z.pos, width), bf16)],
        [((z.tiles, LANES, width), bf16), ((z.pos, width), bf16), ((z.tiles, LANES, width), bf16)],
        dense,
        "middle",
        sent=(z.tiles, 1),
    )
    returned = z.exchange(1, third)
    fourth_band, deep_keep = call(
        functools.partial(prepare_last_kernel, z),
        (filters, vel_bins, blend_levels, aperture),
        [((z.tiles, 2 * z.window, LANES), bf16), ((z.rows, z.pos), f32)],
        small,
        dense,
        "prepare_last",
        fetched=True,
    )
    image_shallow = freq_sum(
        z,
        *call(
            functools.partial(turn_kernel, z),
            (shallow,),
            parts,
            [((z.rows, z.pos), bf16)],
            dense // 8,
            "turn",
            fetched=True,
        ),
    )
    returned, image_shallow, fourth_band, deep_keep = lax.optimization_barrier(
        (returned, image_shallow, fourth_band, deep_keep)
    )
    deep = []
    for shifts, part in ((range(1, z.freq), parts[0]), (range(1), ((1, z.rows, split), bf16))):
        deep += call(
            functools.partial(last_kernel, z, shifts),
            (returned, fourth_band, deep_keep),
            [part],
            [],
            dense // 8,
            "last_own" if len(deep) else "last_send",
        )
    image_deep = freq_sum(z, deep[0], deep[1][0].astype(f32))
    return image_shallow, image_deep


def solution(mesh):
    return jax.shard_map(
        functools.partial(body, mesh),
        mesh=mesh,
        in_specs=(P(None, "freq", "wide", None), P(None, None, "freq", None, None), P(), P(), P()),
        out_specs=(P("wide", "freq"), P("wide", "freq")),
        check_vma=False,
    )
```

```python
import functools
import math

import jax
import jax.numpy as jnp
from jax import lax
from jax.experimental import pallas as pl
from jax.experimental.pallas import tpu as pltpu
from jax.sharding import PartitionSpec as P

LANES = 128
VMEM_LIMIT = 24 * 1024 * 1024


class Sizes:
    def __init__(self, mesh, wave_shape, filters_shape, aperture_shape):
        self.wide = mesh.shape["wide"]
        self.freq = mesh.shape["freq"]
        self.pos = wave_shape[-1]
        self.rows = wave_shape[-2]
        self.side = math.isqrt(self.pos)
        self.bins = filters_shape[-2]
        self.tap_count = filters_shape[-1]
        self.taps = math.isqrt(self.tap_count)
        self.half = self.taps // 2
        self.tile_rows = LANES // self.side
        self.tiles = self.pos // LANES
        self.halo = -(-self.half // self.tile_rows)
        self.window = (1 + 2 * self.halo) * LANES
        self.blocks = aperture_shape[-1]
        self.blk = self.pos // self.blocks
        self.chunks = LANES // self.rows
        quarter = self.wide // 4
        blocks = [list(range(i * quarter, (i + 1) * quarter)) for i in range(4)]
        middle = quarter // 2
        self.start = blocks[2][middle]
        self.orders = (
            blocks[2][middle:] + blocks[2][:middle] + blocks[1][::-1] + blocks[0] + blocks[3],
            [(self.start + i) % self.wide for i in range(self.wide)],
        )

    def place(self, turn, index):
        return self.orders[turn].index(index)

    def exchange(self, turn, chunks):
        return lax.all_to_all(chunks, "wide", 0, 0, axis_index_groups=[self.orders[turn]], tiled=True)


def fill_taps(z, filt_ref, step, rows_ref):
    rows_ref[...] = jnp.zeros_like(rows_ref)
    for k in range(z.bins):
        pair = filt_ref[step, 0, k].astype(jnp.float32)
        for part in range(2):
            row = part * z.bins + k
            rows_ref[row : row + 1, : z.tap_count] = pair[part : part + 1]


def fill_table(z, bins_ref, levels_ref, step, side, table_ref):
    blend = bins_ref.shape[1]
    ids = [bins_ref[step, j, side : side + 1] for j in range(blend)]
    weights = [levels_ref[step, j, side : side + 1].astype(jnp.float32) for j in range(blend)]
    total = sum(weights[1:], weights[0])
    table_ref[...] = jnp.zeros_like(table_ref)
    for k in range(z.bins):
        hits = [jnp.where(i == k, w, 0.0) for i, w in zip(ids, weights)]
        table_ref[k : k + 1, :] = sum(hits[1:], hits[0]) / total


def tap_index(z, in_y, in_x, out_y, out_x):
    a = in_y - out_y + (z.half - z.halo * z.tile_rows)
    b = in_x - out_x + z.half
    valid = (a >= 0) & (a < z.taps) & (b >= 0) & (b < z.taps)
    return jnp.where(valid, a * z.taps + b, LANES - 1)


def spread(rows_ref, row, index):
    source = jnp.broadcast_to(rows_ref[row : row + 1, :], index.shape)
    return jnp.take_along_axis(source, index, axis=1, mode="promise_in_bounds")


def chunk_order(z, column):
    chunk, inside = column // (2 * z.rows), column % (2 * z.rows)
    return inside // z.rows, chunk * z.rows + inside % z.rows


def fetch(pairs, sems):
    copies = [pltpu.make_async_copy(source, target, sems.at[i]) for i, (source, target) in enumerate(pairs)]
    for copy in copies:
        copy.start()
    return copies


def sent(z, turn, out_ref, out_hbm, sems, tile):
    place = pl.ds(min(z.place(turn, tile * z.chunks + c) for c in range(z.chunks)), z.chunks)
    return pltpu.make_async_copy(out_ref.at[place], out_hbm.at[place], sems.at[tile])


def first_kernel(
    z,
    wave_hbm,
    filt_hbm,
    bins_hbm,
    levels_hbm,
    out_hbm,
    wave_ref,
    filt_ref,
    bins_ref,
    levels_ref,
    taps_ref,
    table_ref,
    band_ref,
    lhs_ref,
    acc_ref,
    source_ref,
    out_ref,
    out_sems,
    sems,
):
    copies = fetch(
        [(filt_hbm, filt_ref), (bins_hbm, bins_ref), (levels_hbm, levels_ref), (wave_hbm, wave_ref)], sems
    )
    group_rows = LANES // 2 // z.side
    window_rows = z.window // z.side
    lift = z.half - z.halo * z.tile_rows
    steps = window_rows - group_rows
    half_lanes = LANES // 2
    lane = lax.broadcasted_iota(jnp.int32, (z.side, LANES), 1)
    part, point = chunk_order(z, lane)
    b = lax.broadcasted_iota(jnp.int32, (z.side, LANES), 0) - point % z.side + z.half
    index = (group_rows - 1 - point // z.side) * z.taps + b + part * half_lanes
    index = jnp.where((b >= 0) & (b < z.taps), index, LANES - 1)
    lane = lax.broadcasted_iota(jnp.int32, (16, LANES), 1)
    row = lax.broadcasted_iota(jnp.int32, (16, LANES), 0)
    is_low = lane < half_lanes
    inside = jnp.where(is_low, lane, lane - half_lanes)
    tap = (row - (group_rows - 1) + lift) * z.taps + inside
    picked = jnp.where((inside < group_rows * z.taps) & (tap >= 0) & (tap < z.tap_count), tap, LANES - 1)
    empty = jnp.zeros((group_rows * z.side, LANES), jnp.bfloat16)
    for k in range(z.bins):
        for half in range(2):
            top, columns = half * z.window, 2 * k * LANES
            band_ref[top + z.window - group_rows * z.side : top + z.window, columns : columns + LANES] = empty
            band_ref[top : top + group_rows * z.side, columns + LANES : columns + 2 * LANES] = empty
    copies[0].wait()
    fill_taps(z, filt_ref, 0, taps_ref)
    for k in range(z.bins):
        columns = 2 * k * LANES
        real, imag = spread(taps_ref, k, picked), spread(taps_ref, z.bins + k, picked)
        source_ref[2 * k] = jnp.where(is_low, real, imag)
        source_ref[2 * k + 1] = jnp.where(is_low, -imag, real)
        for y in range(steps):
            for half in range(2):
                block = spread(source_ref.at[2 * k + half], y, index).astype(jnp.bfloat16)
                top = half * z.window + y * z.side
                band_ref[top : top + z.side, columns : columns + LANES] = block
                top += group_rows * z.side
                band_ref[top : top + z.side, columns + LANES : columns + 2 * LANES] = block
    copies[1].wait()
    copies[2].wait()
    copies[3].wait()
    spans = 1 + 2 * z.halo
    for part in range(2):
        for tile in range(z.tiles):
            for span in range(spans):
                source = tile + span - z.halo
                place = (part * spans + span) * LANES
                if 0 <= source < z.tiles:
                    piece = wave_ref[part, :, source * LANES : (source + 1) * LANES]
                else:
                    piece = jnp.zeros((z.rows, LANES), jnp.bfloat16)
                lhs_ref[tile * z.rows : (tile + 1) * z.rows, place : place + LANES] = piece
    lane = lax.broadcasted_iota(jnp.int32, (8, LANES), 1)
    points = [chunk_order(z, lane + v * LANES)[1] for v in range(2)]
    whole = jnp.dot(lhs_ref[...], band_ref[...], preferred_element_type=jnp.float32)
    for k in range(z.bins):
        product = whole[:, 2 * k * LANES : 2 * (k + 1) * LANES]
        if k == 0:
            fill_table(z, bins_ref, levels_ref, 0, 0, table_ref)
            columns = []
            for tile in range(z.tiles):
                weights = table_ref[:, tile * LANES : (tile + 1) * LANES]
                picked = [jnp.take_along_axis(weights, p, axis=1, mode="promise_in_bounds") for p in points]
                columns.append(jnp.concatenate(picked, axis=1))
        for tile in range(z.tiles):
            rows = slice(tile * z.rows, (tile + 1) * z.rows)
            part = product[rows] * columns[tile][k : k + 1]
            if k:
                part = part + acc_ref[rows, :]
            if k < z.bins - 1:
                acc_ref[rows, :] = part
            else:
                total = part.astype(jnp.bfloat16)
                for c in range(z.chunks):
                    out_ref[z.place(0, tile * z.chunks + c)] = total[:, 2 * z.rows * c : 2 * z.rows * (c + 1)]
                sent(z, 0, out_ref, out_hbm, out_sems, tile).start()
    for tile in range(z.tiles):
        sent(z, 0, out_ref, out_hbm, out_sems, tile).wait()


def prepare_middle_kernel(
    z,
    filt_hbm,
    bins_hbm,
    levels_hbm,
    aperture_hbm,
    second_ref,
    third_ref,
    keep_ref,
    filt_ref,
    bins_ref,
    levels_ref,
    aperture_ref,
    taps_ref,
    table_ref,
    columns_ref,
    sems,
):
    copies = fetch(
        [(filt_hbm, filt_ref), (bins_hbm, bins_ref), (levels_hbm, levels_ref), (aperture_hbm, aperture_ref)],
        sems,
    )
    for copy in copies:
        copy.wait()
    lane = lax.broadcasted_iota(jnp.int32, (LANES, LANES), 1)
    row = lax.broadcasted_iota(jnp.int32, (LANES, LANES), 0)
    for step, band_ref in ((0, second_ref), (1, third_ref)):
        fill_taps(z, filt_ref, step, taps_ref)
        fill_table(z, bins_ref, levels_ref, step, 1, table_ref)
        columns = jnp.transpose(table_ref[...])
        for k in range(z.bins):
            columns_ref[k] = jnp.broadcast_to(columns[:, k : k + 1], (z.pos, LANES))

        @pl.loop(0, 1 + 2 * z.halo)
        def _(span, band_ref=band_ref):
            inner = lane + span * LANES
            index = tap_index(z, inner // z.side, inner % z.side, row // z.side, row % z.side)
            for part in range(2):
                taps = [spread(taps_ref, part * z.bins + k, index) for k in range(z.bins)]
                place = pl.multiple_of(part * z.window + span * LANES, LANES)
                for tile in range(z.tiles):
                    total = 0.0
                    for k in range(z.bins):
                        total = total + taps[k] * columns_ref[k, tile * LANES : (tile + 1) * LANES, :]
                    band_ref[tile, :, pl.ds(place, LANES)] = total.astype(jnp.bfloat16)

    width = 2 * z.rows
    offset = lax.axis_index("wide") * z.rows
    receiver = lax.broadcasted_iota(jnp.int32, (z.blocks, width), 1) % z.rows + offset
    pick = (receiver // z.blk == lax.broadcasted_iota(jnp.int32, (z.blocks, width), 0)).astype(jnp.float32)
    keep_ref[...] = jnp.dot(aperture_ref[0].astype(jnp.float32), pick, preferred_element_type=jnp.float32)


def prepare_last_kernel(
    z,
    filt_hbm,
    bins_hbm,
    levels_hbm,
    aperture_hbm,
    fourth_ref,
    keep_ref,
    filt_ref,
    bins_ref,
    levels_ref,
    aperture_ref,
    taps_ref,
    table_ref,
    sems,
):
    copies = fetch(
        [(filt_hbm, filt_ref), (bins_hbm, bins_ref), (levels_hbm, levels_ref), (aperture_hbm, aperture_ref)],
        sems,
    )
    for copy in copies:
        copy.wait()
    fill_taps(z, filt_ref, 1, taps_ref)
    fill_table(z, bins_ref, levels_ref, 1, 0, table_ref)
    lane = lax.broadcasted_iota(jnp.int32, (z.rows, LANES), 1)
    row = lax.broadcasted_iota(jnp.int32, (z.rows, LANES), 0)

    @pl.loop(0, z.window // z.rows)
    def _(block):
        inner = row + block * z.rows
        index = tap_index(z, inner // z.side, inner % z.side, lane // z.side, lane % z.side)
        for part in range(2):
            taps = [spread(taps_ref, part * z.bins + k, index) for k in range(z.bins)]
            place = pl.multiple_of((2 * block + part) * z.rows, z.rows)
            for tile in range(z.tiles):
                total = 0.0
                for k in range(z.bins):
                    total = total + taps[k] * table_ref[k : k + 1, tile * LANES : (tile + 1) * LANES]
                total = total if part == 0 else -total
                if tile < z.halo:
                    total = jnp.where(block * z.rows >= (z.halo - tile) * LANES, total, 0.0)
                if tile >= z.tiles - z.halo:
                    total = jnp.where(block * z.rows < (z.tiles + z.halo - tile) * LANES, total, 0.0)
                fourth_ref[tile, pl.ds(place, z.rows), :] = total.astype(jnp.bfloat16)

    offset = lax.axis_index("wide") * z.rows
    source = lax.broadcasted_iota(jnp.int32, (z.rows, z.blocks), 0) + offset
    pick = (source // z.blk == lax.broadcasted_iota(jnp.int32, (z.rows, z.blocks), 1)).astype(jnp.float32)
    mine = jnp.dot(pick, aperture_ref[1].astype(jnp.float32), preferred_element_type=jnp.float32)
    receiver = lax.broadcasted_iota(jnp.int32, (z.blocks, z.pos), 1)
    stretch = (receiver // z.blk == lax.broadcasted_iota(jnp.int32, (z.blocks, z.pos), 0)).astype(jnp.float32)
    keep_ref[...] = jnp.dot(mine, stretch, preferred_element_type=jnp.float32)


def turned(z, block):
    return jnp.concatenate([-block[:, z.rows :], block[:, : z.rows]], axis=1)


def over_sources(z, band_ref, straight, turn, tile):
    low, high = max(tile - z.halo, 0), min(tile + z.halo, z.tiles - 1)
    reach = range(low, high + 1)
    rhs = jnp.concatenate([straight(j) for j in reach] + [turn(j) for j in reach], axis=0)
    width = len(reach) * LANES
    starts = [part * z.window + (low - tile + z.halo) * LANES for part in range(2)]
    band = jnp.concatenate([band_ref[tile, :, start : start + width] for start in starts], axis=1)
    return jnp.dot(band, rhs, preferred_element_type=jnp.float32)


def middle_kernel(
    z,
    moved_ref,
    second_ref,
    third_ref,
    keep_ref,
    out_hbm,
    shallow_hbm,
    turned_ref,
    straight2_ref,
    turned2_ref,
    out_ref,
    out_sems,
    shallow_sem,
):
    width = 2 * z.rows

    def field(tile):
        return jnp.concatenate([moved_ref[z.place(0, tile * z.chunks + c)] for c in range(z.chunks)], axis=0)

    for tile in range(z.tiles):
        turned_ref[tile] = turned(z, field(tile))
    per_tile = LANES // z.blk
    for tile in range(z.tiles):
        mask = keep_ref[tile * per_tile : (tile + 1) * per_tile, :]
        mask = jnp.broadcast_to(mask[:, None, :], (per_tile, z.blk, width)).reshape(LANES, width)
        shallow = over_sources(z, second_ref, field, lambda j: turned_ref[j], tile) * mask
        shallow = shallow.astype(jnp.bfloat16)
        straight2_ref[tile * LANES : (tile + 1) * LANES, :] = shallow
        turned2_ref[tile] = turned(z, shallow)
    shallow_copy = pltpu.make_async_copy(straight2_ref, shallow_hbm, shallow_sem.at[0])
    shallow_copy.start()
    for tile in range(z.tiles):
        chunk = z.place(1, tile * z.chunks)
        third = over_sources(
            z, third_ref, lambda j: straight2_ref[j * LANES : (j + 1) * LANES, :], lambda j: turned2_ref[j], tile
        ).astype(jnp.bfloat16)
        out_ref[chunk : chunk + z.chunks] = third.reshape(z.chunks, z.rows, width)
        sent(z, 1, out_ref, out_hbm, out_sems, tile).start()
    for tile in range(z.tiles):
        sent(z, 1, out_ref, out_hbm, out_sems, tile).wait()
    shallow_copy.wait()


def split_sum(z, real_ref, send_ref, own_ref):
    me = lax.axis_index("freq")
    width = z.pos // z.freq

    def part(shift):
        start = lax.rem(me + shift, z.freq) * width
        return real_ref[:, pl.ds(pl.multiple_of(start, width), width)]

    own_ref[...] = part(0).astype(jnp.float32)
    for shift in range(1, z.freq):
        send_ref[shift - 1] = part(shift)


def turn_kernel(z, shallow_hbm, send_ref, own_ref, shallow_ref, real_ref, sems):
    for copy in fetch([(shallow_hbm, shallow_ref)], sems):
        copy.wait()
    for tile in range(z.tiles):
        columns = slice(tile * LANES, (tile + 1) * LANES)
        flipped = jnp.transpose(shallow_ref[columns, :].astype(jnp.float32))
        real_ref[:, columns] = flipped[: z.rows].astype(jnp.bfloat16)
    split_sum(z, real_ref, send_ref, own_ref)


def last_kernel(z, shifts, field_ref, fourth_ref, keep_ref, out_ref):
    me = lax.axis_index("freq")
    tiles = z.tiles // z.freq
    for i, shift in enumerate(shifts):
        for j in range(tiles):
            tile = lax.rem(me + shift, z.freq) * tiles + j
            first = (tile - z.halo) * z.chunks - z.start + 2 * z.wide
            pieces = [field_ref[lax.rem(first + c, z.wide)] for c in range((1 + 2 * z.halo) * z.chunks)]
            columns = pl.ds(pl.multiple_of(tile * LANES, LANES), LANES)
            fourth = jnp.dot(
                jnp.concatenate(pieces, axis=1), fourth_ref[tile], preferred_element_type=jnp.float32
            )
            out_ref[i, :, j * LANES : (j + 1) * LANES] = (fourth * keep_ref[:, columns]).astype(out_ref.dtype)


def call(kernel, operands, outs, scratch, flops, name, fetched=False, sent=()):
    source = pltpu.HBM if fetched else pltpu.VMEM
    spaces = [pltpu.HBM if i < len(sent) else pltpu.VMEM for i in range(len(outs))]
    scratch = [pltpu.VMEM(shape, dtype) for shape, dtype in scratch]
    if sent:
        scratch += [pltpu.VMEM(*outs[0])] + [pltpu.SemaphoreType.DMA((parts,)) for parts in sent]
    if fetched:
        scratch = [pltpu.VMEM(x.shape, x.dtype) for x in operands] + scratch
        scratch.append(pltpu.SemaphoreType.DMA((len(operands),)))
        operands = [pltpu.with_memory_space_constraint(x, pltpu.HBM) for x in operands]
    return pl.pallas_call(
        kernel,
        out_shape=[space(shape, dtype) for space, (shape, dtype) in zip(spaces, outs)],
        in_specs=[pl.BlockSpec(memory_space=source)] * len(operands),
        out_specs=[pl.BlockSpec(memory_space=space) for space in spaces],
        scratch_shapes=scratch,
        compiler_params=pltpu.CompilerParams(vmem_limit_bytes=VMEM_LIMIT),
        cost_estimate=pl.CostEstimate(flops=flops, bytes_accessed=1 << 20, transcendentals=0),
        name=name,
    )(*operands)


def freq_sum(z, send, own):
    total = own
    for shift in range(1, z.freq):
        pairs = [(source, (source + shift) % z.freq) for source in range(z.freq)]
        total = total + lax.ppermute(send[shift - 1], "freq", pairs).astype(jnp.float32)
    return total


def body(mesh, wave, filters, vel_bins, blend_levels, aperture):
    z = Sizes(mesh, wave.shape, filters.shape, aperture.shape)
    bf16, f32 = jnp.bfloat16, jnp.float32
    filters = jnp.transpose(filters, (0, 2, 3, 1, 4))
    vel_bins = jnp.transpose(vel_bins, (0, 2, 1, 3))
    blend_levels = jnp.transpose(blend_levels, (0, 2, 1, 3))
    width = 2 * z.rows
    chunks = ((z.wide, z.rows, width), bf16)
    split = z.pos // z.freq
    parts = [((z.freq - 1, z.rows, split), bf16), ((z.rows, split), f32)]
    small = [((8, LANES), f32), ((8, z.pos), f32)]
    dense = 2 * 2 * z.window * z.bins * z.pos * z.rows
    (first,) = call(
        functools.partial(first_kernel, z),
        (wave[:, 0], filters, vel_bins, blend_levels),
        [chunks],
        small
        + [
            ((2 * z.window, 2 * z.bins * LANES), bf16),
            ((z.tiles * z.rows, 2 * z.window), bf16),
            ((z.tiles * z.rows, 2 * LANES), f32),
            ((2 * z.bins, 16, LANES), f32),
        ],
        2 * dense,
        "first",
        fetched=True,
        sent=(z.tiles,),
    )
    moved = z.exchange(0, first)
    second_band, third_band, shallow_keep = call(
        functools.partial(prepare_middle_kernel, z),
        (filters, vel_bins, blend_levels, aperture),
        [
            ((z.tiles, LANES, 2 * z.window), bf16),
            ((z.tiles, LANES, 2 * z.window), bf16),
            ((z.blocks, width), f32),
        ],
        small + [((z.bins, z.pos, LANES), f32)],
        dense,
        "prepare_middle",
        fetched=True,
    )
    third, shallow = call(
        functools.partial(middle_kernel, z),
        (moved, second_band, third_band, shallow_keep),
        [chunks, ((z.pos, width), bf16)],
        [((z.tiles, LANES, width), bf16), ((z.pos, width), bf16), ((z.tiles, LANES, width), bf16)],
        dense,
        "middle",
        sent=(z.tiles, 1),
    )
    returned = z.exchange(1, third)
    fourth_band, deep_keep = call(
        functools.partial(prepare_last_kernel, z),
        (filters, vel_bins, blend_levels, aperture),
        [((z.tiles, 2 * z.window, LANES), bf16), ((z.rows, z.pos), f32)],
        small,
        dense,
        "prepare_last",
        fetched=True,
    )
    image_shallow = freq_sum(
        z,
        *call(
            functools.partial(turn_kernel, z),
            (shallow,),
            parts,
            [((z.rows, z.pos), bf16)],
            dense // 8,
            "turn",
            fetched=True,
        ),
    )
    returned, image_shallow, fourth_band, deep_keep = lax.optimization_barrier(
        (returned, image_shallow, fourth_band, deep_keep)
    )
    deep = []
    for shifts, part in ((range(1, z.freq), parts[0]), (range(1), ((1, z.rows, split), bf16))):
        deep += call(
            functools.partial(last_kernel, z, shifts),
            (returned, fourth_band, deep_keep),
            [part],
            [],
            dense // 8,
            "last_own" if len(deep) else "last_send",
        )
    image_deep = freq_sum(z, deep[0], deep[1][0].astype(f32))
    return image_shallow, image_deep


def solution(mesh):
    return jax.shard_map(
        functools.partial(body, mesh),
        mesh=mesh,
        in_specs=(P(None, "freq", "wide", None), P(None, None, "freq", None, None), P(), P(), P()),
        out_specs=(P("wide", "freq"), P("wide", "freq")),
        check_vma=False,
    )
```

```python
import functools
import math

import jax
import jax.numpy as jnp
from jax import lax
from jax.experimental import pallas as pl
from jax.experimental.pallas import tpu as pltpu
from jax.sharding import PartitionSpec as P

LANES = 128
VMEM_LIMIT = 24 * 1024 * 1024


class Sizes:
    def __init__(self, mesh, wave_shape, filters_shape, aperture_shape):
        self.wide = mesh.shape["wide"]
        self.freq = mesh.shape["freq"]
        self.pos = wave_shape[-1]
        self.rows = wave_shape[-2]
        self.side = math.isqrt(self.pos)
        self.bins = filters_shape[-2]
        self.tap_count = filters_shape[-1]
        self.taps = math.isqrt(self.tap_count)
        self.half = self.taps // 2
        self.tile_rows = LANES // self.side
        self.tiles = self.pos // LANES
        self.halo = -(-self.half // self.tile_rows)
        self.window = (1 + 2 * self.halo) * LANES
        self.blocks = aperture_shape[-1]
        self.blk = self.pos // self.blocks
        self.chunks = LANES // self.rows
        quarter = self.wide // 4
        blocks = [list(range(i * quarter, (i + 1) * quarter)) for i in range(4)]
        middle = quarter // 2
        self.start = blocks[2][middle]
        self.orders = (
            blocks[2][middle:] + blocks[2][:middle] + blocks[1][::-1] + blocks[0] + blocks[3],
            [(self.start + i) % self.wide for i in range(self.wide)],
        )

    def place(self, turn, index):
        return self.orders[turn].index(index)

    def exchange(self, turn, chunks):
        return lax.all_to_all(chunks, "wide", 0, 0, axis_index_groups=[self.orders[turn]], tiled=True)


def fill_taps(z, filt_ref, step, rows_ref):
    rows_ref[...] = jnp.zeros_like(rows_ref)
    for k in range(z.bins):
        pair = filt_ref[step, 0, k].astype(jnp.float32)
        for part in range(2):
            row = part * z.bins + k
            rows_ref[row : row + 1, : z.tap_count] = pair[part : part + 1]


def fill_table(z, bins_ref, levels_ref, step, side, table_ref):
    blend = bins_ref.shape[1]
    ids = [bins_ref[step, j, side : side + 1] for j in range(blend)]
    weights = [levels_ref[step, j, side : side + 1].astype(jnp.float32) for j in range(blend)]
    total = sum(weights[1:], weights[0])
    table_ref[...] = jnp.zeros_like(table_ref)
    for k in range(z.bins):
        hits = [jnp.where(i == k, w, 0.0) for i, w in zip(ids, weights)]
        table_ref[k : k + 1, :] = sum(hits[1:], hits[0]) / total


def tap_index(z, in_y, in_x, out_y, out_x):
    a = in_y - out_y + (z.half - z.halo * z.tile_rows)
    b = in_x - out_x + z.half
    valid = (a >= 0) & (a < z.taps) & (b >= 0) & (b < z.taps)
    return jnp.where(valid, a * z.taps + b, LANES - 1)


def spread(rows_ref, row, index):
    source = jnp.broadcast_to(rows_ref[row : row + 1, :], index.shape)
    return jnp.take_along_axis(source, index, axis=1, mode="promise_in_bounds")


def chunk_order(z, column):
    chunk, inside = column // (2 * z.rows), column % (2 * z.rows)
    return inside // z.rows, chunk * z.rows + inside % z.rows


def fetch(pairs, sems):
    copies = [pltpu.make_async_copy(source, target, sems.at[i]) for i, (source, target) in enumerate(pairs)]
    for copy in copies:
        copy.start()
    return copies


def sent(z, turn, out_ref, out_hbm, sems, tile):
    place = pl.ds(min(z.place(turn, tile * z.chunks + c) for c in range(z.chunks)), z.chunks)
    return pltpu.make_async_copy(out_ref.at[place], out_hbm.at[place], sems.at[tile])


def first_kernel(
    z,
    wave_hbm,
    filt_hbm,
    bins_hbm,
    levels_hbm,
    out_hbm,
    wave_ref,
    filt_ref,
    bins_ref,
    levels_ref,
    taps_ref,
    table_ref,
    band_ref,
    lhs_ref,
    acc_ref,
    source_ref,
    out_ref,
    out_sems,
    sems,
):
    copies = fetch(
        [(filt_hbm, filt_ref), (bins_hbm, bins_ref), (levels_hbm, levels_ref), (wave_hbm, wave_ref)], sems
    )
    group_rows = LANES // 2 // z.side
    window_rows = z.window // z.side
    lift = z.half - z.halo * z.tile_rows
    steps = window_rows - group_rows
    half_lanes = LANES // 2
    lane = lax.broadcasted_iota(jnp.int32, (z.side, LANES), 1)
    part, point = chunk_order(z, lane)
    b = lax.broadcasted_iota(jnp.int32, (z.side, LANES), 0) - point % z.side + z.half
    index = (group_rows - 1 - point // z.side) * z.taps + b + part * half_lanes
    index = jnp.where((b >= 0) & (b < z.taps), index, LANES - 1)
    lane = lax.broadcasted_iota(jnp.int32, (16, LANES), 1)
    row = lax.broadcasted_iota(jnp.int32, (16, LANES), 0)
    is_low = lane < half_lanes
    inside = jnp.where(is_low, lane, lane - half_lanes)
    tap = (row - (group_rows - 1) + lift) * z.taps + inside
    picked = jnp.where((inside < group_rows * z.taps) & (tap >= 0) & (tap < z.tap_count), tap, LANES - 1)
    empty = jnp.zeros((group_rows * z.side, LANES), jnp.bfloat16)
    for k in range(z.bins):
        for half in range(2):
            top, columns = half * z.window, 2 * k * LANES
            band_ref[top + z.window - group_rows * z.side : top + z.window, columns : columns + LANES] = empty
            band_ref[top : top + group_rows * z.side, columns + LANES : columns + 2 * LANES] = empty
    copies[0].wait()
    fill_taps(z, filt_ref, 0, taps_ref)
    for k in range(z.bins):
        columns = 2 * k * LANES
        real, imag = spread(taps_ref, k, picked), spread(taps_ref, z.bins + k, picked)
        source_ref[2 * k] = jnp.where(is_low, real, imag)
        source_ref[2 * k + 1] = jnp.where(is_low, -imag, real)
        for y in range(steps):
            for half in range(2):
                block = spread(source_ref.at[2 * k + half], y, index).astype(jnp.bfloat16)
                top = half * z.window + y * z.side
                band_ref[top : top + z.side, columns : columns + LANES] = block
                top += group_rows * z.side
                band_ref[top : top + z.side, columns + LANES : columns + 2 * LANES] = block
    copies[1].wait()
    copies[2].wait()
    fill_table(z, bins_ref, levels_ref, 0, 0, table_ref)
    copies[3].wait()
    spans = 1 + 2 * z.halo
    for part in range(2):
        for tile in range(z.tiles):
            for span in range(spans):
                source = tile + span - z.halo
                place = (part * spans + span) * LANES
                if 0 <= source < z.tiles:
                    piece = wave_ref[part, :, source * LANES : (source + 1) * LANES]
                else:
                    piece = jnp.zeros((z.rows, LANES), jnp.bfloat16)
                lhs_ref[tile * z.rows : (tile + 1) * z.rows, place : place + LANES] = piece
    lane = lax.broadcasted_iota(jnp.int32, (8, LANES), 1)
    points = [chunk_order(z, lane + v * LANES)[1] for v in range(2)]
    columns = []
    for tile in range(z.tiles):
        weights = table_ref[:, tile * LANES : (tile + 1) * LANES]
        picked = [jnp.take_along_axis(weights, p, axis=1, mode="promise_in_bounds") for p in points]
        columns.append(jnp.concatenate(picked, axis=1))
    for k in range(z.bins):
        product = jnp.dot(
            lhs_ref[...],
            band_ref[:, 2 * k * LANES : 2 * (k + 1) * LANES],
            preferred_element_type=jnp.float32,
        )
        for tile in range(z.tiles):
            rows = slice(tile * z.rows, (tile + 1) * z.rows)
            part = product[rows] * columns[tile][k : k + 1]
            if k:
                part = part + acc_ref[rows, :]
            if k < z.bins - 1:
                acc_ref[rows, :] = part
            else:
                total = part.astype(jnp.bfloat16)
                for c in range(z.chunks):
                    out_ref[z.place(0, tile * z.chunks + c)] = total[:, 2 * z.rows * c : 2 * z.rows * (c + 1)]
                sent(z, 0, out_ref, out_hbm, out_sems, tile).start()
    for tile in range(z.tiles):
        sent(z, 0, out_ref, out_hbm, out_sems, tile).wait()


def prepare_middle_kernel(
    z,
    filt_hbm,
    bins_hbm,
    levels_hbm,
    aperture_hbm,
    second_ref,
    third_ref,
    keep_ref,
    filt_ref,
    bins_ref,
    levels_ref,
    aperture_ref,
    taps_ref,
    table_ref,
    columns_ref,
    sems,
):
    copies = fetch(
        [(filt_hbm, filt_ref), (bins_hbm, bins_ref), (levels_hbm, levels_ref), (aperture_hbm, aperture_ref)],
        sems,
    )
    for copy in copies:
        copy.wait()
    lane = lax.broadcasted_iota(jnp.int32, (LANES, LANES), 1)
    row = lax.broadcasted_iota(jnp.int32, (LANES, LANES), 0)
    for step, band_ref in ((0, second_ref), (1, third_ref)):
        fill_taps(z, filt_ref, step, taps_ref)
        fill_table(z, bins_ref, levels_ref, step, 1, table_ref)
        columns = jnp.transpose(table_ref[...])
        for k in range(z.bins):
            columns_ref[k] = jnp.broadcast_to(columns[:, k : k + 1], (z.pos, LANES))

        @pl.loop(0, 1 + 2 * z.halo)
        def _(span, band_ref=band_ref):
            inner = lane + span * LANES
            index = tap_index(z, inner // z.side, inner % z.side, row // z.side, row % z.side)
            for part in range(2):
                taps = [spread(taps_ref, part * z.bins + k, index) for k in range(z.bins)]
                place = pl.multiple_of(part * z.window + span * LANES, LANES)
                for tile in range(z.tiles):
                    total = 0.0
                    for k in range(z.bins):
                        total = total + taps[k] * columns_ref[k, tile * LANES : (tile + 1) * LANES, :]
                    band_ref[tile, :, pl.ds(place, LANES)] = total.astype(jnp.bfloat16)

    width = 2 * z.rows
    offset = lax.axis_index("wide") * z.rows
    receiver = lax.broadcasted_iota(jnp.int32, (z.blocks, width), 1) % z.rows + offset
    pick = (receiver // z.blk == lax.broadcasted_iota(jnp.int32, (z.blocks, width), 0)).astype(jnp.float32)
    keep_ref[...] = jnp.dot(aperture_ref[0].astype(jnp.float32), pick, preferred_element_type=jnp.float32)


def prepare_last_kernel(
    z,
    filt_hbm,
    bins_hbm,
    levels_hbm,
    aperture_hbm,
    fourth_ref,
    keep_ref,
    filt_ref,
    bins_ref,
    levels_ref,
    aperture_ref,
    taps_ref,
    table_ref,
    sems,
):
    copies = fetch(
        [(filt_hbm, filt_ref), (bins_hbm, bins_ref), (levels_hbm, levels_ref), (aperture_hbm, aperture_ref)],
        sems,
    )
    for copy in copies:
        copy.wait()
    fill_taps(z, filt_ref, 1, taps_ref)
    fill_table(z, bins_ref, levels_ref, 1, 0, table_ref)
    lane = lax.broadcasted_iota(jnp.int32, (z.rows, LANES), 1)
    row = lax.broadcasted_iota(jnp.int32, (z.rows, LANES), 0)

    @pl.loop(0, z.window // z.rows)
    def _(block):
        inner = row + block * z.rows
        index = tap_index(z, inner // z.side, inner % z.side, lane // z.side, lane % z.side)
        for part in range(2):
            taps = [spread(taps_ref, part * z.bins + k, index) for k in range(z.bins)]
            place = pl.multiple_of((2 * block + part) * z.rows, z.rows)
            for tile in range(z.tiles):
                total = 0.0
                for k in range(z.bins):
                    total = total + taps[k] * table_ref[k : k + 1, tile * LANES : (tile + 1) * LANES]
                total = total if part == 0 else -total
                if tile < z.halo:
                    total = jnp.where(block * z.rows >= (z.halo - tile) * LANES, total, 0.0)
                if tile >= z.tiles - z.halo:
                    total = jnp.where(block * z.rows < (z.tiles + z.halo - tile) * LANES, total, 0.0)
                fourth_ref[tile, pl.ds(place, z.rows), :] = total.astype(jnp.bfloat16)

    offset = lax.axis_index("wide") * z.rows
    source = lax.broadcasted_iota(jnp.int32, (z.rows, z.blocks), 0) + offset
    pick = (source // z.blk == lax.broadcasted_iota(jnp.int32, (z.rows, z.blocks), 1)).astype(jnp.float32)
    mine = jnp.dot(pick, aperture_ref[1].astype(jnp.float32), preferred_element_type=jnp.float32)
    receiver = lax.broadcasted_iota(jnp.int32, (z.blocks, z.pos), 1)
    stretch = (receiver // z.blk == lax.broadcasted_iota(jnp.int32, (z.blocks, z.pos), 0)).astype(jnp.float32)
    keep_ref[...] = jnp.dot(mine, stretch, preferred_element_type=jnp.float32)


def turned(z, block):
    return jnp.concatenate([-block[:, z.rows :], block[:, : z.rows]], axis=1)


def over_sources(z, band_ref, straight, turn, tile):
    low, high = max(tile - z.halo, 0), min(tile + z.halo, z.tiles - 1)
    reach = range(low, high + 1)
    rhs = jnp.concatenate([straight(j) for j in reach] + [turn(j) for j in reach], axis=0)
    width = len(reach) * LANES
    starts = [part * z.window + (low - tile + z.halo) * LANES for part in range(2)]
    band = jnp.concatenate([band_ref[tile, :, start : start + width] for start in starts], axis=1)
    return jnp.dot(band, rhs, preferred_element_type=jnp.float32)


def middle_kernel(
    z,
    moved_ref,
    second_ref,
    third_ref,
    keep_ref,
    out_hbm,
    shallow_hbm,
    turned_ref,
    straight2_ref,
    turned2_ref,
    out_ref,
    out_sems,
    shallow_sem,
):
    width = 2 * z.rows

    def field(tile):
        return jnp.concatenate([moved_ref[z.place(0, tile * z.chunks + c)] for c in range(z.chunks)], axis=0)

    for tile in range(z.halo):
        turned_ref[tile] = turned(z, field(tile))
    per_tile = LANES // z.blk
    for tile in range(z.tiles):
        if tile + z.halo < z.tiles:
            turned_ref[tile + z.halo] = turned(z, field(tile + z.halo))
        mask = keep_ref[tile * per_tile : (tile + 1) * per_tile, :]
        mask = jnp.broadcast_to(mask[:, None, :], (per_tile, z.blk, width)).reshape(LANES, width)
        shallow = over_sources(z, second_ref, field, lambda j: turned_ref[j], tile) * mask
        shallow = shallow.astype(jnp.bfloat16)
        straight2_ref[tile * LANES : (tile + 1) * LANES, :] = shallow
        turned2_ref[tile] = turned(z, shallow)
    shallow_copy = pltpu.make_async_copy(straight2_ref, shallow_hbm, shallow_sem.at[0])
    shallow_copy.start()
    for tile in range(z.tiles):
        chunk = z.place(1, tile * z.chunks)
        third = over_sources(
            z, third_ref, lambda j: straight2_ref[j * LANES : (j + 1) * LANES, :], lambda j: turned2_ref[j], tile
        ).astype(jnp.bfloat16)
        out_ref[chunk : chunk + z.chunks] = third.reshape(z.chunks, z.rows, width)
        sent(z, 1, out_ref, out_hbm, out_sems, tile).start()
    for tile in range(z.tiles):
        sent(z, 1, out_ref, out_hbm, out_sems, tile).wait()
    shallow_copy.wait()


def split_sum(z, real_ref, send_ref, own_ref):
    me = lax.axis_index("freq")
    width = z.pos // z.freq

    def part(shift):
        start = lax.rem(me + shift, z.freq) * width
        return real_ref[:, pl.ds(pl.multiple_of(start, width), width)]

    own_ref[...] = part(0).astype(jnp.float32)
    for shift in range(1, z.freq):
        send_ref[shift - 1] = part(shift)


def turn_kernel(z, shallow_hbm, send_ref, own_ref, shallow_ref, real_ref, sems):
    for copy in fetch([(shallow_hbm, shallow_ref)], sems):
        copy.wait()
    for tile in range(z.tiles):
        columns = slice(tile * LANES, (tile + 1) * LANES)
        flipped = jnp.transpose(shallow_ref[columns, :].astype(jnp.float32))
        real_ref[:, columns] = flipped[: z.rows].astype(jnp.bfloat16)
    split_sum(z, real_ref, send_ref, own_ref)


def last_kernel(z, shifts, field_ref, fourth_ref, keep_ref, out_ref):
    me = lax.axis_index("freq")
    tiles = z.tiles // z.freq
    for i, shift in enumerate(shifts):
        for j in range(tiles):
            tile = lax.rem(me + shift, z.freq) * tiles + j
            first = (tile - z.halo) * z.chunks - z.start + 2 * z.wide
            pieces = [field_ref[lax.rem(first + c, z.wide)] for c in range((1 + 2 * z.halo) * z.chunks)]
            columns = pl.ds(pl.multiple_of(tile * LANES, LANES), LANES)
            fourth = jnp.dot(
                jnp.concatenate(pieces, axis=1), fourth_ref[tile], preferred_element_type=jnp.float32
            )
            out_ref[i, :, j * LANES : (j + 1) * LANES] = (fourth * keep_ref[:, columns]).astype(out_ref.dtype)


def call(kernel, operands, outs, scratch, flops, name, fetched=False, sent=()):
    source = pltpu.HBM if fetched else pltpu.VMEM
    spaces = [pltpu.HBM if i < len(sent) else pltpu.VMEM for i in range(len(outs))]
    scratch = [pltpu.VMEM(shape, dtype) for shape, dtype in scratch]
    if sent:
        scratch += [pltpu.VMEM(*outs[0])] + [pltpu.SemaphoreType.DMA((parts,)) for parts in sent]
    if fetched:
        scratch = [pltpu.VMEM(x.shape, x.dtype) for x in operands] + scratch
        scratch.append(pltpu.SemaphoreType.DMA((len(operands),)))
        operands = [pltpu.with_memory_space_constraint(x, pltpu.HBM) for x in operands]
    return pl.pallas_call(
        kernel,
        out_shape=[space(shape, dtype) for space, (shape, dtype) in zip(spaces, outs)],
        in_specs=[pl.BlockSpec(memory_space=source)] * len(operands),
        out_specs=[pl.BlockSpec(memory_space=space) for space in spaces],
        scratch_shapes=scratch,
        compiler_params=pltpu.CompilerParams(vmem_limit_bytes=VMEM_LIMIT),
        cost_estimate=pl.CostEstimate(flops=flops, bytes_accessed=1 << 20, transcendentals=0),
        name=name,
    )(*operands)


def freq_sum(z, send, own):
    total = own
    for shift in range(1, z.freq):
        pairs = [(source, (source + shift) % z.freq) for source in range(z.freq)]
        total = total + lax.ppermute(send[shift - 1], "freq", pairs).astype(jnp.float32)
    return total


def body(mesh, wave, filters, vel_bins, blend_levels, aperture):
    z = Sizes(mesh, wave.shape, filters.shape, aperture.shape)
    bf16, f32 = jnp.bfloat16, jnp.float32
    filters = jnp.transpose(filters, (0, 2, 3, 1, 4))
    vel_bins = jnp.transpose(vel_bins, (0, 2, 1, 3))
    blend_levels = jnp.transpose(blend_levels, (0, 2, 1, 3))
    width = 2 * z.rows
    chunks = ((z.wide, z.rows, width), bf16)
    split = z.pos // z.freq
    parts = [((z.freq - 1, z.rows, split), bf16), ((z.rows, split), f32)]
    small = [((8, LANES), f32), ((8, z.pos), f32)]
    dense = 2 * 2 * z.window * z.bins * z.pos * z.rows
    (first,) = call(
        functools.partial(first_kernel, z),
        (wave[:, 0], filters, vel_bins, blend_levels),
        [chunks],
        small
        + [
            ((2 * z.window, 2 * z.bins * LANES), bf16),
            ((z.tiles * z.rows, 2 * z.window), bf16),
            ((z.tiles * z.rows, 2 * LANES), f32),
            ((2 * z.bins, 16, LANES), f32),
        ],
        2 * dense,
        "first",
        fetched=True,
        sent=(z.tiles,),
    )
    moved = z.exchange(0, first)
    second_band, third_band, shallow_keep = call(
        functools.partial(prepare_middle_kernel, z),
        (filters, vel_bins, blend_levels, aperture),
        [
            ((z.tiles, LANES, 2 * z.window), bf16),
            ((z.tiles, LANES, 2 * z.window), bf16),
            ((z.blocks, width), f32),
        ],
        small + [((z.bins, z.pos, LANES), f32)],
        dense,
        "prepare_middle",
        fetched=True,
    )
    third, shallow = call(
        functools.partial(middle_kernel, z),
        (moved, second_band, third_band, shallow_keep),
        [chunks, ((z.pos, width), bf16)],
        [((z.tiles, LANES, width), bf16), ((z.pos, width), bf16), ((z.tiles, LANES, width), bf16)],
        dense,
        "middle",
        sent=(z.tiles, 1),
    )
    returned = z.exchange(1, third)
    fourth_band, deep_keep = call(
        functools.partial(prepare_last_kernel, z),
        (filters, vel_bins, blend_levels, aperture),
        [((z.tiles, 2 * z.window, LANES), bf16), ((z.rows, z.pos), f32)],
        small,
        dense,
        "prepare_last",
        fetched=True,
    )
    image_shallow = freq_sum(
        z,
        *call(
            functools.partial(turn_kernel, z),
            (shallow,),
            parts,
            [((z.rows, z.pos), bf16)],
            dense // 8,
            "turn",
            fetched=True,
        ),
    )
    returned, image_shallow, fourth_band, deep_keep = lax.optimization_barrier(
        (returned, image_shallow, fourth_band, deep_keep)
    )
    deep = []
    for shifts, part in ((range(1, z.freq), parts[0]), (range(1), ((1, z.rows, split), bf16))):
        deep += call(
            functools.partial(last_kernel, z, shifts),
            (returned, fourth_band, deep_keep),
            [part],
            [],
            dense // 8,
            "last_own" if len(deep) else "last_send",
        )
    image_deep = freq_sum(z, deep[0], deep[1][0].astype(f32))
    return image_shallow, image_deep


def solution(mesh):
    return jax.shard_map(
        functools.partial(body, mesh),
        mesh=mesh,
        in_specs=(P(None, "freq", "wide", None), P(None, None, "freq", None, None), P(), P(), P()),
        out_specs=(P("wide", "freq"), P("wide", "freq")),
        check_vma=False,
    )
```
